128 devices in a mesh: dm: 2 (over core), bin: 64 (over x, y, z).
Axes of the slice: x: 4, y: 4, z: 4, core: 2. Of those that a mesh axis runs over, the one named last changes fastest.
Arguments:
- series: float32 [16777216], P(('dm', 'bin')), parts along dimension 0, may hold values from -6 to 6
- tap_coef: float32 [2, 16, 128], replicated, may hold values from -0.5 to 0.5
- tap_offset: int32 [16, 128], replicated, may hold values from 0 to 127, each once within a row
- harm_index: int32 [8, 524288], P(None, 'bin'), may hold values from 0 to 7, as said below
Outputs:
- summed: float32 [16, 1048576], P(None, ('dm', 'bin')), parts along dimension 1
The draws below stay inside these ranges and needn't reach their ends.
There are 2 independent parts, one for each index of `dm`. The reference program is written for one: setup_inputs(seed, part) draws one part's arguments, and reference() takes and returns one part's arrays. A program takes and returns all parts, laid end to end along the dimension named above; an argument that names none is the same for every part. Nothing has to cross between parts.
Inputs may be any that keep to these rules, and one draw needn't show every extreme that they name: `harm_index`: entry (h, f) is at most h. `tap_offset`: each row holds every number below 128 once.
All inputs are finite; a program needn't handle non-finite values.
Results may differ from the reference program's by a relative error of at most 0.0014.
Values may be sent and summed in bfloat16 or wider, within the bound.
A program may use at most 256 MiB of HBM per device.

```python
import math
import jax
import jax.numpy as jnp
from jax import lax

TMPL = 16
TAPS = 128
HARM = 8
LENGTH = 8388608
FUND = 524288


def draw_harm_index(key, part):
    key = jax.random.fold_in(key, 7)
    order_index = jnp.arange(HARM, dtype=jnp.int32)[:, None]
    fund_index = jnp.arange(FUND, dtype=jnp.int32)[None, :]
    jitter = jax.random.randint(key, (HARM, FUND), 0, 840, dtype=jnp.int32) % (order_index + 1)
    corner = (order_index == HARM - 1) & (fund_index == FUND - 1)
    return jnp.where(corner, HARM - 1, jitter)


def block_levels(rng, extent, cuts, smallest, top_value):
    factor_of, own = 1.0, jax.random.fold_in(rng, 6)
    for position, parts in cuts:
        draws = jnp.exp(jax.random.uniform(jax.random.fold_in(own, position), (parts,), jnp.float32, smallest / len(cuts), top_value / len(cuts)))
        factor_of = factor_of * jnp.repeat(draws, extent[position] // parts).reshape([-1 if axis == position else 1 for axis in range(len(extent))])
    return factor_of


def scatter_about(rng, dims, width, limit, shards=(), kind=jnp.bfloat16):
    values = width * jax.random.normal(rng, dims, jnp.float32)
    if shards:
        values = values * block_levels(rng, dims, shards, -0.22, 0.18)
    return jnp.clip(values, -limit, limit).astype(kind)


def setup_inputs(seed: int = 0, part: int = 0) -> dict:
    streams_of = jax.random.split(jax.random.key(seed), 5)
    own_keys = jax.random.split(jax.random.fold_in(streams_of[4], part), 5)
    series = scatter_about(own_keys[0], (LENGTH,), 1.0, 6.0, ((0, 64),), jnp.float32)
    tap_coef = scatter_about(streams_of[1], (2, TMPL, TAPS), TAPS ** -0.5, 0.5, (), jnp.float32)
    tap_offset = jax.vmap(lambda own: jax.random.permutation(own, TAPS))(jax.random.split(streams_of[2], TMPL)).reshape((TMPL, TAPS)).astype(jnp.int32)
    harm_index = draw_harm_index(jax.random.fold_in(streams_of[4], 71), part)
    return {"series": series, "tap_coef": tap_coef, "tap_offset": tap_offset, "harm_index": harm_index}


PRECISE = lax.Precision.HIGHEST

def toeplitz_blocks(tap_coef, tap_offset):
    tap_count = tap_offset.shape[1]
    lag_index = jnp.arange(tap_count, dtype=jnp.int32)
    onehot = (tap_offset[:, :, None] == lag_index[None, None, :]).astype(jnp.float32)
    dense_taps = jnp.einsum('ztj,tjd->ztd', tap_coef.astype(jnp.float32), onehot, precision=PRECISE)
    window = jnp.arange(2 * tap_count, dtype=jnp.int32)
    banded = (window[None, None, :] - lag_index[None, :, None] == lag_index[:, None, None]).astype(jnp.float32)
    band_matrix = jnp.einsum('ztd,dim->ztim', dense_taps, banded, precision=PRECISE)
    real_rows = jnp.stack([band_matrix[0], -band_matrix[1]], axis=2)
    imag_rows = jnp.stack([band_matrix[1], band_matrix[0]], axis=2)
    return jnp.stack([real_rows, imag_rows], axis=1)

def granule_power(matrix, windows):
    result = jnp.einsum('toizm,zqm->toqi', matrix, windows, precision=PRECISE)
    return (result[:, 0] * result[:, 0] + result[:, 1] * result[:, 1]).astype(jnp.bfloat16)

def reference(series, tap_coef, tap_offset, harm_index):
    length = series.shape[0]
    kept_bins = length // 2
    transformed = jnp.fft.fft(series) / math.sqrt(length)
    spectrum = jnp.stack([jnp.real(transformed[:kept_bins]), jnp.imag(transformed[:kept_bins])]).astype(jnp.float32)
    rim_width = TAPS // 2
    padded = jnp.pad(spectrum, ((0, 0), (rim_width, rim_width)))
    blocks = padded.reshape(2, kept_bins // TAPS + 1, TAPS)
    windows = jnp.concatenate([blocks[:, :-1], blocks[:, 1:]], axis=2)
    matrix = toeplitz_blocks(tap_coef, tap_offset)
    powers = lax.map(lambda single: granule_power(single[None], windows)[0], matrix)
    powers = powers.reshape(TMPL, kept_bins)
    fund_count = harm_index.shape[1]
    fund_index = jnp.arange(fund_count, dtype=jnp.int32)
    summed = jnp.zeros((TMPL, fund_count), jnp.float32)
    for harmonic in range(HARM):
        bins_read = ((harmonic + 1) * fund_index + harm_index[harmonic]).astype(jnp.int32)
        summed = summed + jnp.take(powers, bins_read, axis=1).astype(jnp.float32)
    return summed / HARM
```

```python
import functools
import math

import jax
import jax.numpy as jnp
import numpy as np
from jax import lax
from jax.experimental import pallas as pl
from jax.experimental.pallas import tpu as pltpu
from jax.sharding import PartitionSpec as P

D = 64
TMPL = 16
TAPS = 128
HARM = 8
LENGTH = 8388608
LOCAL = LENGTH // D
ALPHA = 512
BETA = 256
ORDER = (8, 7, 1, 6, 2, 5, 3, 4)
BLOCKS = tuple((h, r) for h in ORDER for r in range(h))
NB = len(BLOCKS)
FIRST = {h: BLOCKS.index((h, 0)) for h in ORDER}
ROWS = 80
HALO = 72
F32 = jnp.float32
BF16 = jnp.bfloat16


def np_split(x):
    x = np.asarray(x, np.float32)
    hi = x.astype(jnp.bfloat16)
    lo = (x - hi.astype(np.float32)).astype(jnp.bfloat16)
    return hi, lo


@functools.lru_cache(None)
def fft_tables():
    k1 = np.arange(D)[:, None]
    m = np.arange(LOCAL // D)[None, :]
    ang = -2 * np.pi * (k1 * m) / LENGTH
    tw1 = np.stack([np.cos(ang), np.sin(ang)]).astype(np.float32)
    k = np.arange(ALPHA)[:, None] * np.arange(ALPHA)[None, :] % ALPHA
    ang = -2 * np.pi * k / ALPHA
    c, s = np.cos(ang), np.sin(ang)
    wa = np.block([[c, -s], [s, c]])
    ang = -2 * np.pi * (np.arange(ALPHA)[:, None] * np.arange(BETA)[None, :]) / LOCAL
    tw2 = np.stack([np.cos(ang), np.sin(ang)]).astype(np.float32)
    half = BETA // 2
    ang = -2 * np.pi * (np.arange(BETA)[:, None] * np.arange(half)[None, :] % BETA) / BETA
    c, s = np.cos(ang), np.sin(ang)
    vb = np.block([[c, s], [-s, c]])
    return tw1, *np_split(wa), tw2, *np_split(vb)


@functools.lru_cache(None)
def perm_tables():
    out = []
    for h in range(1, HARM + 1):
        m = np.zeros((128 * h, 128 * h), np.float32)
        a = np.arange(128)
        for r in range(h):
            m[h * a + r, 128 * r + a] = 1
        out.append(m.astype(jnp.bfloat16))
    return tuple(out)


@functools.lru_cache(None)
def select_tables():
    i = np.arange(64)
    e = np.zeros((NB, 128, 128), np.float32)
    ex = np.zeros((NB, 64, 128), np.float32)
    jp = np.zeros((NB, 1, 128), np.float32)
    for n, (h, r) in enumerate(BLOCKS):
        b, j = np.divmod(64 * r + i, h)
        for t in range(2):
            e[n, 64 * t + i, 64 * t + b] = 1
            ex[n, b, 64 * t + i] = 1
            jp[n, 0, 64 * t + i] = j
    return e.astype(jnp.bfloat16), ex.astype(jnp.bfloat16), jp


def split(x):
    hi = x.astype(BF16)
    return hi, (x - hi.astype(F32)).astype(BF16)


def dot(a, b):
    return jnp.dot(a, b, preferred_element_type=F32)


def dot3(ah, al, bh, bl):
    return dot(ah, bh) + dot(ah, bl) + dot(al, bh)


def columns_kernel(xs, w1, tw, out):
    x = jnp.concatenate([xs[pl.ds(m, D, stride=16), :] for m in range(16)], axis=1)
    y = dot3(*split(w1[...]), *split(x))
    yr, yi = y[:D], y[D:]
    zr = yr * tw[0] - yi * tw[1]
    zi = yr * tw[1] + yi * tw[0]
    for c, z in enumerate((zr, zi)):
        for m in range(16):
            out[pl.ds(c * 16 + (m % 2) * 8 + m // 2, D, stride=32), :] = z[:, 128 * m : 128 * m + 128]


def local_fft_kernel(b, wah, wal, tw, vbh, vbl, *rest):
    perms, out, zn = rest[:HARM], rest[HARM], rest[HARM + 1]
    v = b[...].reshape(D, 4, 8, 128)
    parts = [v[:, n].reshape(ALPHA, 128) for n in range(4)]
    rhs = jnp.concatenate(
        [jnp.concatenate(parts[0:2], axis=1), jnp.concatenate(parts[2:4], axis=1)], axis=0
    )
    y = dot3(wah[...], wal[...], *split(rhs))
    yr, yi = y[:ALPHA], y[ALPHA:]
    t = jnp.concatenate([yr * tw[0] - yi * tw[1], yr * tw[1] + yi * tw[0]], axis=1)
    th, tl = split(t)
    z = dot3(th, tl, vbh[...], vbl[...])
    zero = jnp.zeros((8, 128), F32)
    for c in range(2):
        zt = z[:, 128 * c : 128 * c + 128].T
        zn[c, 0:8, :] = zero
        zn[c, 520:528, :] = zero
        for n in range(4):
            zn[c, pl.ds(8 + n, 128, stride=4), :] = zt[:, 128 * n : 128 * n + 128]
    lane = lax.broadcasted_iota(jnp.int32, (D, 128), 1)
    halo = jnp.zeros((D, 128), F32)
    for h in range(1, HARM + 1):
        src = jnp.concatenate(
            [
                jnp.concatenate([zn[c, pl.ds(8 + n, D, stride=h), :] for n in range(h)], axis=1)
                for c in range(2)
            ],
            axis=0,
        )
        hi, lo = split(src)
        moved = dot(jnp.concatenate([hi, lo], axis=0), perms[h - 1][...])
        moved = moved[:128] + moved[128:]
        for r in range(h):
            for c in range(2):
                out[pl.ds(2 * (FIRST[h] + r) + c, D, stride=ROWS), :] = moved[
                    64 * c : 64 * c + 64, 128 * r : 128 * r + 128
                ]
        for c in range(2):
            left = zn[c, pl.ds(7, D, stride=h), :][:, 127:128]
            right = zn[c, pl.ds(8 + h, D, stride=h), :][:, 0:1]
            halo = jnp.where(lane == c * 8 + h - 1, left, halo)
            halo = jnp.where(lane == 16 + c * 8 + h - 1, right, halo)
    out[pl.ds(HALO, D, stride=ROWS), :] = halo
    for n in range(HALO + 1, ROWS):
        out[pl.ds(n, D, stride=ROWS), :] = jnp.zeros((D, 128), F32)


def search_kernel(land, jit, taps, e, ex, jp, out, xt, xl, pm, msk, sm):
    lane8 = lax.broadcasted_iota(jnp.int32, (8, 128), 1)
    for n in range(NB):
        re = land[pl.ds(2 * n, D, stride=ROWS), :]
        im = land[pl.ds(2 * n + 1, D, stride=ROWS), :]
        xt[n, 8:136, :] = jnp.concatenate([re, im], axis=0).T
    edge = land[pl.ds(HALO, D, stride=ROWS), :]
    et = jnp.concatenate([edge, jnp.zeros((D, 128), F32)], axis=0).T
    left = jnp.where(lane8 < 64, et[0:8], pltpu.roll(et[8:16], 64, 1))
    right = jnp.where(lane8 < 64, et[16:24], pltpu.roll(et[24:32], 64, 1))
    for h in range(1, HARM + 1):
        xt[FIRST[h] + h - 1, 7:8, :] = left[h - 1 : h]
        xt[FIRST[h], 136:137, :] = right[h - 1 : h]

    def put(n, slot, hi, lo):
        xl[pl.ds(128 * n, 128), pl.ds(128 * slot, 128)] = hi
        xl[pl.ds(128 * n, 128), pl.ds(384 + 128 * slot, 128)] = lo

    for n, (h, r) in enumerate(BLOCKS):
        hi, lo = split(xt[n, 8:136, :])
        put(n, 1, hi, lo)
        if r > 0:
            put(n - 1, 2, hi, lo)
        if r < h - 1:
            put(n + 1, 0, hi, lo)
        if r == 0:
            put(n, 0, *split(xt[n + h - 1, 7:135, :]))
        if r == h - 1:
            put(n, 2, *split(xt[n - h + 1, 9:137, :]))
        msk[pl.ds(128 * n, 128), :] = jnp.where(dot(jit[h - 1], ex[n]) == jp[n], 1.0, 0.0)

    def template_pair(tp, carry):
        for g in range(NB // 4):
            rows = pl.ds(512 * g, 512)
            lhs = jnp.concatenate([xl[rows, :], xl[rows, 0:384]], axis=1)
            acc = dot(lhs, taps[tp])
            re, im = acc[:, :128], acc[:, 128:]
            kept = jnp.where(msk[rows, :] > 0.5, re * re + im * im, 0.0).astype(BF16)
            for q in range(4):
                pm[4 * g + q, pl.ds(pl.multiple_of(128 * tp, 128), 128), :] = kept[128 * q : 128 * q + 128]
        return carry

    lax.fori_loop(0, TMPL // 2, template_pair, 0)
    lane = lax.broadcasted_iota(jnp.int32, (64, 128), 1)

    def finish(tp, carry):
        rows = pl.ds(pl.multiple_of(256 * tp, 256), 256)
        total = jnp.zeros((256, 128), F32)
        for n in range(0, NB, 2):
            total += dot(
                jnp.concatenate([pm[n, rows, :], pm[n + 1, rows, :]], axis=1),
                jnp.concatenate([e[n], e[n + 1]], axis=0),
            )
        sm[...] = total * (1.0 / HARM)
        for q in range(2):
            even = sm[pl.ds(128 * q, 64, stride=2), :]
            odd = sm[pl.ds(128 * q + 1, 64, stride=2), :]
            out[4 * tp + 2 * q] = jnp.where(lane < 64, even, pltpu.roll(odd, 64, 1))
            out[4 * tp + 2 * q + 1] = jnp.where(lane < 64, pltpu.roll(even, 64, 1), odd)
        return carry

    lax.fori_loop(0, TMPL // 4, finish, 0)


def vmem(count):
    return [pl.BlockSpec(memory_space=pltpu.VMEM)] * count


def call(kernel, count, shape, scratch=(), flops=0, moved=0, limit=56):
    return pl.pallas_call(
        kernel,
        out_shape=jax.ShapeDtypeStruct(shape, F32),
        in_specs=vmem(count),
        out_specs=pl.BlockSpec(memory_space=pltpu.VMEM),
        scratch_shapes=list(scratch),
        compiler_params=pltpu.CompilerParams(vmem_limit_bytes=limit * 1024 * 1024),
        cost_estimate=pl.CostEstimate(flops=flops, bytes_accessed=moved, transcendentals=0),
    )


def columns(xs, w1, tw1):
    return call(columns_kernel, 3, (2048, 128), flops=10**8, moved=3 * 10**6)(xs, w1, tw1)


def local_fft(b, wah, wal, tw2, vbh, vbl, perms):
    return call(
        local_fft_kernel,
        6 + HARM,
        (D * ROWS, 128),
        [pltpu.VMEM((2, 528, 128), F32)],
        flops=4 * 10**9,
        moved=2 * 10**7,
    )(b, wah, wal, tw2, vbh, vbl, *perms)


def search(land, jit, taps, e, ex, jp):
    return call(
        search_kernel,
        6,
        (TMPL, 64, 128),
        [
            pltpu.VMEM((NB, 144, 128), F32),
            pltpu.VMEM((NB * 128, 768), BF16),
            pltpu.VMEM((NB, 1024, 128), BF16),
            pltpu.VMEM((NB * 128, 128), F32),
            pltpu.VMEM((256, 128), F32),
        ],
        flops=25 * 10**9,
        moved=2 * 10**7,
    )(land, jit, taps, e, ex, jp)


def device_matrix(e):
    k1 = jnp.arange(D, dtype=jnp.int32)[:, None]
    n1 = jnp.arange(D, dtype=jnp.int32)[None, :]
    ang = (k1 * (D * n1 + e) % (D * D)).astype(F32) * (2 * math.pi / (D * D))
    scale = 1.0 / math.sqrt(LENGTH)
    return jnp.concatenate([jnp.cos(ang), -jnp.sin(ang)], axis=0) * scale


def tap_matrix(tap_coef, tap_offset):
    lag = jnp.arange(TAPS, dtype=jnp.int32)
    onehot = (tap_offset[:, :, None] == lag[None, None, :]).astype(F32)
    dense = jnp.einsum("ztj,tjd->ztd", tap_coef, onehot, precision=lax.Precision.HIGHEST)
    parts = jnp.stack([jnp.stack([dense[0], dense[1]]), jnp.stack([-dense[1], dense[0]])])
    w = jnp.arange(192, dtype=jnp.int32)
    i = jnp.arange(64, dtype=jnp.int32)
    band = (w[None, :, None] - i[None, None, :] == lag[:, None, None]).astype(BF16)
    hi = lax.reduce_precision(parts, 8, 7)
    both = jnp.stack([hi, parts - hi]).astype(BF16)
    full = jnp.einsum("scotd,dwi->scotwi", both, band, preferred_element_type=F32).astype(BF16)
    full = full.reshape(2, 2, 2, TMPL // 2, 2, 3, 64, 64)
    full = full.transpose(3, 0, 5, 1, 6, 2, 4, 7).reshape(TMPL // 2, 2, 384, 256)
    return jnp.concatenate([full[:, 0], full[:, 0], full[:, 1]], axis=1)


def shards(series, tap_coef, tap_offset, harm_index):
    e = lax.axis_index("bin")
    tw1, wah, wal, tw2, vbh, vbl = fft_tables()
    xs = lax.all_to_all(series.reshape(D, 16, 128), "bin", split_axis=0, concat_axis=0, tiled=True)
    part = columns(xs.reshape(1024, 128), device_matrix(e), tw1)
    got = lax.all_to_all(part.reshape(D, 32, 128), "bin", split_axis=0, concat_axis=0, tiled=True)
    send = local_fft(got.reshape(2048, 128), wah, wal, tw2, vbh, vbl, perm_tables())
    land = lax.all_to_all(send.reshape(D, ROWS, 128), "bin", split_axis=0, concat_axis=0, tiled=True)
    jit = harm_index.reshape(HARM, 128, 64).astype(BF16)
    out = search(land.reshape(D * ROWS, 128), jit, tap_matrix(tap_coef, tap_offset), *select_tables())
    return out.reshape(TMPL, 8192)


def solution(mesh):
    return jax.shard_map(
        shards,
        mesh=mesh,
        in_specs=(P(("dm", "bin")), P(), P(), P(None, "bin")),
        out_specs=P(None, ("dm", "bin")),
        check_vma=False,
    )
```

```python
import functools
import math

import jax
import jax.numpy as jnp
import numpy as np
from jax import lax
from jax.experimental import pallas as pl
from jax.experimental.pallas import tpu as pltpu
from jax.sharding import PartitionSpec as P

D = 64
TMPL = 16
TAPS = 128
HARM = 8
LENGTH = 8388608
LOCAL = LENGTH // D
ALPHA = 512
BETA = 256
ORDER = (8, 7, 1, 6, 2, 5, 3, 4)
BLOCKS = tuple((h, r) for h in ORDER for r in range(h))
NB = len(BLOCKS)
FIRST = {h: BLOCKS.index((h, 0)) for h in ORDER}
ROWS = 80
CHUNKS = ((0, 24, 0, 8), (24, 32, 8, 24), (56, 24, 24, 36))
F32 = jnp.float32
BF16 = jnp.bfloat16


def np_split(x):
    x = np.asarray(x, np.float32)
    hi = x.astype(jnp.bfloat16)
    lo = (x - hi.astype(np.float32)).astype(jnp.bfloat16)
    return hi, lo


@functools.lru_cache(None)
def fft_tables():
    k1 = np.arange(D)[:, None]
    m = np.arange(LOCAL // D)[None, :]
    ang = -2 * np.pi * (k1 * m) / LENGTH
    tw1 = np.stack([np.cos(ang), np.sin(ang)]).astype(np.float32)
    k = np.arange(ALPHA)[:, None] * np.arange(ALPHA)[None, :] % ALPHA
    ang = -2 * np.pi * k / ALPHA
    c, s = np.cos(ang), np.sin(ang)
    wa = np.block([[c, -s], [s, c]])
    ang = -2 * np.pi * (np.arange(ALPHA)[:, None] * np.arange(BETA)[None, :]) / LOCAL
    tw2 = np.stack([np.cos(ang), np.sin(ang)]).astype(np.float32)
    half = BETA // 2
    ang = -2 * np.pi * (np.arange(BETA)[:, None] * np.arange(half)[None, :] % BETA) / BETA
    c, s = np.cos(ang), np.sin(ang)
    vb = np.block([[c, s], [-s, c]])
    return tw1, *np_split(wa), tw2, *np_split(vb)


@functools.lru_cache(None)
def perm_tables():
    out = []
    for h in range(1, HARM + 1):
        m = np.zeros((128 * h, 128 * h), np.float32)
        a = np.arange(128)
        for r in range(h):
            m[h * a + r, 128 * r + a] = 1
        out.append(m.astype(jnp.bfloat16))
    return tuple(out)


@functools.lru_cache(None)
def select_tables():
    i = np.arange(64)
    e = np.zeros((NB, 128, 128), np.float32)
    ex = np.zeros((NB, 64, 128), np.float32)
    jp = np.zeros((NB, 1, 128), np.float32)
    for n, (h, r) in enumerate(BLOCKS):
        b, j = np.divmod(64 * r + i, h)
        for t in range(2):
            e[n, 64 * t + i, 64 * t + b] = 1
            ex[n, b, 64 * t + i] = 1
            jp[n, 0, 64 * t + i] = j
    return e.astype(jnp.bfloat16), ex.astype(jnp.bfloat16), jp.reshape(NB, 128)


def split(x):
    hi = x.astype(BF16)
    return hi, (x - hi.astype(F32)).astype(BF16)


def dot(a, b):
    return jnp.dot(a, b, preferred_element_type=F32)


def dot3(ah, al, bh, bl):
    return dot(ah, bh) + dot(ah, bl) + dot(al, bh)


def partner(me, step):
    x = (me // 16 + step // 16) % 4
    y = (me // 4 + step // 4) % 4
    return x * 16 + y * 4 + (me + step) % 4


def exchange(me, dm, src, dst, first, rows, pitch, sems):
    def start(step, carry):
        to = partner(me, step)
        pltpu.make_async_remote_copy(
            src_ref=src.at[pl.ds(pl.multiple_of(to * pitch + first, 8), rows)],
            dst_ref=dst.at[pl.ds(pl.multiple_of(me * pitch + first, 8), rows)],
            send_sem=sems[0],
            recv_sem=sems[1],
            device_id=(dm, to),
            device_id_type=pl.DeviceIdType.MESH,
        ).start()
        return carry

    lax.fori_loop(1, D, start, 0)
    own = pl.ds(pl.multiple_of(me * pitch + first, 8), rows)
    dst[own, :] = src[own, :]


def wait_for(ref, rows, sem):
    part = ref.at[pl.ds(0, (D - 1) * rows)]
    pltpu.make_async_copy(part, part, sem).wait()


def make_taps(vx, taps):
    lane = lax.broadcasted_iota(jnp.int32, (64, 128), 1)

    def pair(tp, carry):
        for x in range(3):
            both = []
            for z in range(2):
                rolled = []
                for t in range(2):
                    row = vx[2 * tp + t, 3 * z + x : 3 * z + x + 1, :]
                    rolled.append(
                        pltpu.roll(jnp.broadcast_to(row, (64, 128)), 64 * t, 1, stride=1, stride_axis=0)
                    )
                both.append(split(jnp.where(lane < 64, rolled[0], rolled[1])))
            for part, n in ((0, 0), (1, 0), (2, 1)):
                tr, ti = both[0][n], both[1][n]
                row = 384 * part + 128 * x
                taps[tp, row : row + 64, 0:128] = tr
                taps[tp, row : row + 64, 128:256] = ti
                taps[tp, row + 64 : row + 128, 0:128] = -ti
                taps[tp, row + 64 : row + 128, 128:256] = tr
        return carry

    lax.fori_loop(0, TMPL // 2, pair, 0)


def columns(xs, w1, tw, out):
    x = jnp.concatenate([xs[pl.ds(m, D, stride=16), :] for m in range(16)], axis=1)
    y = dot3(*split(w1[...]), *split(x))
    yr, yi = y[:D], y[D:]
    zr = yr * tw[0] - yi * tw[1]
    zi = yr * tw[1] + yi * tw[0]
    for c, z in enumerate((zr, zi)):
        for m in range(16):
            out[pl.ds(c * 16 + (m % 2) * 8 + m // 2, D, stride=32), :] = z[:, 128 * m : 128 * m + 128]


def local_fft(b, wah, wal, tw, vbh, vbl, zn):
    v = b[...].reshape(D, 4, 8, 128)
    parts = [v[:, n].reshape(ALPHA, 128) for n in range(4)]
    rhs = jnp.concatenate(
        [jnp.concatenate(parts[0:2], axis=1), jnp.concatenate(parts[2:4], axis=1)], axis=0
    )
    y = dot3(wah[...], wal[...], *split(rhs))
    yr, yi = y[:ALPHA], y[ALPHA:]
    t = jnp.concatenate([yr * tw[0] - yi * tw[1], yr * tw[1] + yi * tw[0]], axis=1)
    th, tl = split(t)
    z = dot3(th, tl, vbh[...], vbl[...])
    zero = jnp.zeros((8, 128), F32)
    for c in range(2):
        zt = z[:, 128 * c : 128 * c + 128].T
        zn[c, 0:8, :] = zero
        zn[c, 520:528, :] = zero
        for n in range(4):
            zn[c, pl.ds(8 + n, 128, stride=4), :] = zt[:, 128 * n : 128 * n + 128]


def pack_ends(zn, out):
    lane = lax.broadcasted_iota(jnp.int32, (D, 128), 1)
    halo = jnp.zeros((D, 128), F32)
    for h in range(1, HARM + 1):
        for c in range(2):
            left = zn[c, pl.ds(7, D, stride=h), :][:, 127:128]
            right = zn[c, pl.ds(8 + h, D, stride=h), :][:, 0:1]
            halo = jnp.where(lane == c * 8 + h - 1, left, halo)
            halo = jnp.where(lane == 16 + c * 8 + h - 1, right, halo)
    out[pl.ds(0, D, stride=ROWS), :] = halo
    for n in range(1, 8):
        out[pl.ds(n, D, stride=ROWS), :] = jnp.zeros((D, 128), F32)


def pack_harmonic(h, zn, perm, out):
    src = jnp.concatenate(
        [
            jnp.concatenate([zn[c, pl.ds(8 + n, D, stride=h), :] for n in range(h)], axis=1)
            for c in range(2)
        ],
        axis=0,
    )
    hi, lo = split(src)
    moved = dot(jnp.concatenate([hi, lo], axis=0), perm[...])
    moved = moved[:128] + moved[128:]
    for r in range(h):
        for c in range(2):
            out[pl.ds(8 + 2 * (FIRST[h] + r) + c, D, stride=ROWS), :] = moved[
                64 * c : 64 * c + 64, 128 * r : 128 * r + 128
            ]


def unpack_ends(land, ends):
    lane = lax.broadcasted_iota(jnp.int32, (8, 128), 1)
    edge = land[pl.ds(0, D, stride=ROWS), :]
    et = jnp.concatenate([edge, jnp.zeros((D, 128), F32)], axis=0).T
    ends[0:8, :] = jnp.where(lane < 64, et[0:8], pltpu.roll(et[8:16], 64, 1))
    ends[8:16, :] = jnp.where(lane < 64, et[16:24], pltpu.roll(et[24:32], 64, 1))


def unpack(land, ends, first, last, xt, xl):
    for n in range(first, last):
        re = land[pl.ds(8 + 2 * n, D, stride=ROWS), :]
        im = land[pl.ds(9 + 2 * n, D, stride=ROWS), :]
        xt[n, 8:136, :] = jnp.concatenate([re, im], axis=0).T
        h, r = BLOCKS[n]
        if r == h - 1:
            xt[n, 7:8, :] = ends[h - 1 : h, :]
        if r == 0:
            xt[n, 136:137, :] = ends[h + 7 : h + 8, :]

    def put(n, slot, hi, lo):
        xl[pl.ds(128 * n, 128), pl.ds(128 * slot, 128)] = hi
        xl[pl.ds(128 * n, 128), pl.ds(384 + 128 * slot, 128)] = lo

    for n in range(first, last):
        h, r = BLOCKS[n]
        hi, lo = split(xt[n, 8:136, :])
        put(n, 1, hi, lo)
        if r > 0:
            put(n - 1, 2, hi, lo)
        if r < h - 1:
            put(n + 1, 0, hi, lo)
        if r == 0:
            put(n, 0, *split(xt[n + h - 1, 7:135, :]))
        if r == h - 1:
            put(n, 2, *split(xt[n - h + 1, 9:137, :]))


def make_masks(jit, ex, jp, msk):
    for n, (h, _) in enumerate(BLOCKS):
        msk[pl.ds(128 * n, 128), :] = jnp.where(dot(jit[h - 1], ex[n]) == jp[n : n + 1, :], 1.0, 0.0)


def correlate(first, last, xl, taps, msk, pm):
    def template_pair(tp, carry):
        for g in range(first // 4, last // 4):
            rows = pl.ds(512 * g, 512)
            lhs = jnp.concatenate([xl[rows, :], xl[rows, 0:384]], axis=1)
            acc = dot(lhs, taps[tp])
            re, im = acc[:, :128], acc[:, 128:]
            kept = jnp.where(msk[rows, :] > 0.5, re * re + im * im, 0.0).astype(BF16)
            for q in range(4):
                pm[4 * g + q, pl.ds(pl.multiple_of(128 * tp, 128), 128), :] = kept[128 * q : 128 * q + 128]
        return carry

    lax.fori_loop(0, TMPL // 2, template_pair, 0)


def add_harmonics(pm, e, sm, out):
    lane = lax.broadcasted_iota(jnp.int32, (64, 128), 1)

    def finish(tp, carry):
        rows = pl.ds(pl.multiple_of(256 * tp, 256), 256)
        total = jnp.zeros((256, 128), F32)
        for n in range(0, NB, 2):
            total += dot(
                jnp.concatenate([pm[n, rows, :], pm[n + 1, rows, :]], axis=1),
                jnp.concatenate([e[n], e[n + 1]], axis=0),
            )
        sm[...] = total * (1.0 / HARM)
        for q in range(2):
            even = sm[pl.ds(128 * q, 64, stride=2), :]
            odd = sm[pl.ds(128 * q + 1, 64, stride=2), :]
            out[4 * tp + 2 * q] = jnp.where(lane < 64, even, pltpu.roll(odd, 64, 1))
            out[4 * tp + 2 * q + 1] = jnp.where(lane < 64, pltpu.roll(even, 64, 1), odd)
        return carry

    lax.fori_loop(0, TMPL // 4, finish, 0)


def search_kernel(*refs):
    series, w1, vx, jit, jp = refs[:5]
    count = len(CONSTANTS)
    held = refs[5 : 5 + count]
    out = refs[5 + count]
    rest = refs[6 + count :]
    local, rest = rest[:count], rest[count:]
    land1, send2, land2, zn, send3, land3, ends, xt, xl, pm, msk, taps, sm = rest[:13]
    const_sem, sems = rest[13:]
    copies = {
        name: pltpu.make_async_copy(held[n], local[n], const_sem.at[n])
        for n, name in enumerate(CONSTANTS)
    }
    ref = dict(zip(CONSTANTS, local))
    for copy in copies.values():
        copy.start()
    me, dm = lax.axis_index("bin"), lax.axis_index("dm")

    barrier = pltpu.get_barrier_semaphore()

    def greet(step, carry):
        pl.semaphore_signal(
            barrier, inc=1, device_id=(dm, partner(me, step)), device_id_type=pl.DeviceIdType.MESH
        )
        return carry

    lax.fori_loop(1, D, greet, 0)
    pl.semaphore_wait(barrier, D - 1)

    exchange(me, dm, series, land1, 0, 16, 16, (sems.at[0], sems.at[1]))
    make_taps(vx, taps)
    copies["ex"].wait()
    make_masks(jit, ref["ex"], jp, msk)
    copies["tw1"].wait()
    wait_for(land1, 16, sems.at[1])
    columns(land1, w1, ref["tw1"], send2)
    exchange(me, dm, send2, land2, 0, 32, 32, (sems.at[2], sems.at[3]))
    for name in ("wah", "wal", "tw2", "vbh", "vbl", "e"):
        copies[name].wait()
    for h in range(1, HARM + 1):
        copies["p%d" % h].wait()
    wait_for(land2, 32, sems.at[3])
    local_fft(land2, ref["wah"], ref["wal"], ref["tw2"], ref["vbh"], ref["vbl"], zn)
    pack_ends(zn, send3)
    for n, (row, rows, first, last) in enumerate(CHUNKS):
        for h in ORDER:
            if first <= FIRST[h] < last:
                pack_harmonic(h, zn, ref["p%d" % h], send3)
        exchange(me, dm, send3, land3, row, rows, ROWS, (sems.at[4 + 2 * n], sems.at[5 + 2 * n]))
    for n, (row, rows, first, last) in enumerate(CHUNKS):
        wait_for(land3, rows, sems.at[5 + 2 * n])
        if n == 0:
            unpack_ends(land3, ends)
        unpack(land3, ends, first, last, xt, xl)
        correlate(first, last, xl, taps, msk, pm)
    add_harmonics(pm, ref["e"], sm, out)
    wait_for(land1, 16, sems.at[0])
    wait_for(land2, 32, sems.at[2])
    for n, (_, rows, _, _) in enumerate(CHUNKS):
        wait_for(land3, rows, sems.at[4 + 2 * n])


CONSTANTS = ("ex", "tw1", "wah", "wal", "tw2", "vbh", "vbl") + tuple(
    "p%d" % h for h in range(1, HARM + 1)
) + ("e",)


def constants():
    tw1, wah, wal, tw2, vbh, vbl = fft_tables()
    e, ex, jp = select_tables()
    return [ex, tw1, wah, wal, tw2, vbh, vbl, *perm_tables(), e], jp


def search(series, w1, vx, jit):
    held, jp = constants()
    whole = pl.BlockSpec(memory_space=pltpu.VMEM)
    return pl.pallas_call(
        search_kernel,
        out_shape=jax.ShapeDtypeStruct((TMPL, 64, 128), F32),
        in_specs=[whole] * 5 + [pl.BlockSpec(memory_space=pl.ANY)] * len(held),
        out_specs=whole,
        scratch_shapes=[pltpu.VMEM(c.shape, c.dtype) for c in held]
        + [
            pltpu.VMEM((1024, 128), F32),
            pltpu.VMEM((2048, 128), F32),
            pltpu.VMEM((2048, 128), F32),
            pltpu.VMEM((2, 528, 128), F32),
            pltpu.VMEM((D * ROWS, 128), F32),
            pltpu.VMEM((D * ROWS, 128), F32),
            pltpu.VMEM((16, 128), F32),
            pltpu.VMEM((NB, 144, 128), F32),
            pltpu.VMEM((NB * 128, 768), BF16),
            pltpu.VMEM((NB, 1024, 128), BF16),
            pltpu.VMEM((NB * 128, 128), F32),
            pltpu.VMEM((TMPL // 2, 1152, 256), BF16),
            pltpu.VMEM((256, 128), F32),
            pltpu.SemaphoreType.DMA((len(held),)),
            pltpu.SemaphoreType.DMA((4 + 2 * len(CHUNKS),)),
        ],
        compiler_params=pltpu.CompilerParams(
            collective_id=0, has_side_effects=True, vmem_limit_bytes=62 * 1024 * 1024
        ),
        cost_estimate=pl.CostEstimate(flops=3 * 10**10, bytes_accessed=3 * 10**7, transcendentals=0),
    )(series, w1, vx, jit, jp, *held)


def device_matrix(e):
    k1 = jnp.arange(D, dtype=jnp.int32)[:, None]
    n1 = jnp.arange(D, dtype=jnp.int32)[None, :]
    ang = (k1 * (D * n1 + e) % (D * D)).astype(F32) * (2 * math.pi / (D * D))
    scale = 1.0 / math.sqrt(LENGTH)
    return jnp.concatenate([jnp.cos(ang), -jnp.sin(ang)], axis=0) * scale


def tap_rows(tap_coef, tap_offset):
    m = np.arange(128)
    m = np.where(m < 64, m, m - 128)
    lag = np.concatenate([64 * x - m for x in range(3)])
    lag = np.where(np.tile(m == -64, 3) | (lag < 0) | (lag >= TAPS), -1, lag).astype(np.int32)
    onehot = (tap_offset[:, :, None] == lag[None, None, :]).astype(F32)
    rows = jnp.einsum("ztj,tjy->tzy", tap_coef, onehot, precision=lax.Precision.HIGHEST)
    return rows.reshape(TMPL, 6, 128)


def shards(series, tap_coef, tap_offset, harm_index):
    e = lax.axis_index("bin")
    jit = harm_index.reshape(HARM, 128, 64).astype(BF16)
    out = search(series.reshape(1024, 128), device_matrix(e), tap_rows(tap_coef, tap_offset), jit)
    return out.reshape(TMPL, 8192)


def solution(mesh):
    return jax.shard_map(
        shards,
        mesh=mesh,
        in_specs=(P(("dm", "bin")), P(), P(), P(None, "bin")),
        out_specs=P(None, ("dm", "bin")),
        check_vma=False,
    )
```

```python
import functools
import math

import jax
import jax.numpy as jnp
import numpy as np
from jax import lax
from jax.experimental import pallas as pl
from jax.experimental.pallas import tpu as pltpu
from jax.sharding import PartitionSpec as P

D = 64
TMPL = 16
TAPS = 128
HARM = 8
LENGTH = 8388608
LOCAL = LENGTH // D
ALPHA = 512
BETA = 256
ORDER = (4, 8, 7, 1, 6, 2, 5, 3)
BLOCKS = tuple((h, r) for h in ORDER for r in range(h))
NB = len(BLOCKS)
FIRST = {h: BLOCKS.index((h, 0)) for h in ORDER}
ROWS = 40
CHUNKS = ((0, 8, 0, 4), (8, 16, 4, 20), (24, 16, 20, 36))
FULL = 32767.0
SAMPLE_BOUND = 6.0
PART_BOUND = SAMPLE_BOUND * D / math.sqrt(LENGTH)
F32 = jnp.float32
BF16 = jnp.bfloat16


def np_split(x):
    x = np.asarray(x, np.float32)
    hi = x.astype(jnp.bfloat16)
    lo = (x - hi.astype(np.float32)).astype(jnp.bfloat16)
    return hi, lo


@functools.lru_cache(None)
def fft_tables():
    k1 = np.arange(D)[:, None]
    m = np.arange(LOCAL // D)[None, :]
    ang = -2 * np.pi * (k1 * m) / LENGTH
    tw1 = np.stack([np.cos(ang), np.sin(ang)]).astype(np.float32)
    k = np.arange(ALPHA)[:, None] * np.arange(ALPHA)[None, :] % ALPHA
    ang = -2 * np.pi * k / ALPHA
    c, s = np.cos(ang), np.sin(ang)
    wa = np.block([[c, -s], [s, c]])
    ang = -2 * np.pi * (np.arange(ALPHA)[:, None] * np.arange(BETA)[None, :]) / LOCAL
    tw2 = np.stack([np.cos(ang), np.sin(ang)]).astype(np.float32)
    half = BETA // 2
    ang = -2 * np.pi * (np.arange(BETA)[:, None] * np.arange(half)[None, :] % BETA) / BETA
    c, s = np.cos(ang), np.sin(ang)
    vb = np.block([[c, s], [-s, c]])
    k = k1 * (D * np.arange(D)[None, None, :] + np.arange(D)[:, None, None]) % (D * D)
    ang = -2 * np.pi * k / (D * D)
    w1 = np.concatenate([np.cos(ang), np.sin(ang)], axis=1) / math.sqrt(LENGTH)
    return w1.astype(np.float32), tw1, *np_split(wa), tw2, *np_split(vb)


@functools.lru_cache(None)
def perm_tables():
    out = []
    for h in range(1, HARM + 1):
        m = np.zeros((128 * h, 128 * h), np.float32)
        a = np.arange(128)
        for r in range(h):
            m[h * a + r, 128 * r + 64 * (a % 2) + a // 2] = 1
        out.append(m.astype(jnp.bfloat16))
    return tuple(out)


@functools.lru_cache(None)
def select_tables():
    i = np.arange(64)
    e = np.zeros((NB, 128, 128), np.float32)
    ex = np.zeros((NB, 128, 128), np.float32)
    jp = np.zeros((NB, 1, 128), np.float32)
    for n, (h, r) in enumerate(BLOCKS):
        b, j = np.divmod(64 * r + i, h)
        for t in range(2):
            e[n, 64 * t + i, 64 * t + b] = 1
            ex[n, b, 64 * t + i] = 1
            jp[n, 0, 64 * t + i] = j
    return e.astype(jnp.bfloat16), ex.astype(jnp.bfloat16), jp.reshape(NB, 128)


def split(x):
    hi = x.astype(BF16)
    return hi, (x - hi.astype(F32)).astype(BF16)


def dot(a, b):
    return jnp.dot(a, b, preferred_element_type=F32)


def dot3(ah, al, bh, bl):
    return dot(ah, bh) + dot(ah, bl) + dot(al, bh)


def encode(x, bound):
    size = jnp.sqrt(jnp.sqrt(jnp.abs(x) * (1.0 / bound)))
    code = jnp.minimum(size * FULL + 0.5, FULL).astype(jnp.int32)
    return jnp.where(x < 0, -code, code)


def decode(code, bound):
    x = code.astype(F32)
    return x * jnp.abs(x) * (x * x * (bound / FULL**4))


def join(high, low):
    return (high << 16) | (low & 0xFFFF)


def parted(word):
    return word >> 16, (word << 16) >> 16


def partner(me, step):
    x = (me // 16 + step // 16) % 4
    y = (me // 4 + step // 4) % 4
    return x * 16 + y * 4 + (me + step) % 4


def exchange(me, dm, src, dst, first, rows, pitch, sems):
    def start(step, carry):
        to = partner(me, step)
        pltpu.make_async_remote_copy(
            src_ref=src.at[pl.ds(pl.multiple_of(to * pitch + first, 8), rows)],
            dst_ref=dst.at[pl.ds(pl.multiple_of(me * pitch + first, 8), rows)],
            send_sem=sems[0],
            recv_sem=sems[1],
            device_id=(dm, to),
            device_id_type=pl.DeviceIdType.MESH,
        ).start()
        return carry

    lax.fori_loop(1, D, start, 0)
    own = pl.ds(pl.multiple_of(me * pitch + first, 8), rows)
    dst[own, :] = src[own, :]


def wait_for(ref, rows, sem):
    part = ref.at[pl.ds(0, (D - 1) * rows)]
    pltpu.make_async_copy(part, part, sem).wait()


def make_taps(vx, taps):
    lane = lax.broadcasted_iota(jnp.int32, (64, 128), 1)

    def pair(tp, carry):
        for x in range(3):
            both = []
            for z in range(2):
                rolled = []
                for t in range(2):
                    row = vx[2 * tp + t, 3 * z + x : 3 * z + x + 1, :]
                    rolled.append(
                        pltpu.roll(jnp.broadcast_to(row, (64, 128)), 64 * t, 1, stride=1, stride_axis=0)
                    )
                both.append(split(jnp.where(lane < 64, rolled[0], rolled[1])))
            for part, n in ((0, 0), (1, 0), (2, 1)):
                tr, ti = both[0][n], both[1][n]
                row = 384 * part + 128 * x
                taps[tp, row : row + 64, 0:128] = tr
                taps[tp, row : row + 64, 128:256] = ti
                taps[tp, row + 64 : row + 128, 0:128] = -ti
                taps[tp, row + 64 : row + 128, 128:256] = tr
        return carry

    lax.fori_loop(0, TMPL // 2, pair, 0)


def make_tap_rows(coef, offset, vx):
    lane = lax.broadcasted_iota(jnp.int32, (128, 384), 1)
    m = lane % 128
    lag = lane // 128 * 64 - jnp.where(m < 64, m, m - 128)
    lag = jnp.where(m == 64, -1, lag).astype(F32)
    where = jnp.concatenate([offset[...].astype(F32), jnp.zeros((112, 128), F32)], axis=0).T
    first = coef[...].astype(BF16)
    rest = coef[...] - first.astype(F32)
    second = rest.astype(BF16)
    third = (rest - second.astype(F32)).astype(BF16)
    lhs = jnp.concatenate([first, second, third], axis=0)
    for t in range(TMPL):
        onehot = jnp.where(where[:, t : t + 1] == lag, 1.0, 0.0).astype(BF16)
        rows = dot(lhs, onehot)
        rows = rows[0:32] + rows[32:64] + rows[64:96]
        for z in range(2):
            for x in range(3):
                vx[t, 3 * z + x : 3 * z + x + 1, :] = rows[16 * z + t : 16 * z + t + 1, 128 * x : 128 * x + 128]


def code_samples(series, out):
    v = series[...].reshape(D, 16, 128)
    word = join(encode(v[:, :8], SAMPLE_BOUND), encode(v[:, 8:], SAMPLE_BOUND))
    out[...] = word.reshape(512, 128)


def columns(xs, w1, tw, out):
    pairs = [parted(xs[pl.ds(m, D, stride=8), :]) for m in range(8)]
    x = jnp.concatenate([p[0] for p in pairs] + [p[1] for p in pairs], axis=1)
    y = dot3(*split(w1[...]), *split(decode(x, SAMPLE_BOUND)))
    yr, yi = y[:D], y[D:]
    zr = yr * tw[0] - yi * tw[1]
    zi = yr * tw[1] + yi * tw[0]
    word = join(encode(zr, PART_BOUND), encode(zi, PART_BOUND))
    for m in range(16):
        out[pl.ds((m % 2) * 8 + m // 2, D, stride=16), :] = word[:, 128 * m : 128 * m + 128]


def local_fft(b, wah, wal, tw, vbh, vbl, zn):
    v = b[...].reshape(D, 2, 8, 128)
    word = jnp.concatenate([v[:, n].reshape(ALPHA, 128) for n in range(2)], axis=1)
    rhs = jnp.concatenate([decode(x, PART_BOUND) for x in parted(word)], axis=0)
    y = dot3(wah[...], wal[...], *split(rhs))
    yr, yi = y[:ALPHA], y[ALPHA:]
    t = jnp.concatenate([yr * tw[0] - yi * tw[1], yr * tw[1] + yi * tw[0]], axis=1)
    th, tl = split(t)
    z = dot3(th, tl, vbh[...], vbl[...])
    zero = jnp.zeros((8, 128), F32)
    for c in range(2):
        zt = z[:, 128 * c : 128 * c + 128].T
        zn[c, 0:8, :] = zero
        zn[c, 520:528, :] = zero
        for n in range(4):
            zn[c, pl.ds(8 + n, 128, stride=4), :] = zt[:, 128 * n : 128 * n + 128]


def quantized(x, factor):
    return jnp.clip(jnp.round(x * factor), -FULL, FULL)


def pack_ends(zn, factors, out):
    lane = lax.broadcasted_iota(jnp.int32, (D, 128), 1)
    ends = jnp.zeros((D, 128), jnp.int32)
    for h in range(1, HARM + 1):
        left = [zn[c, pl.ds(7, D, stride=h), :][:, 127:128] for c in range(2)]
        right = [zn[c, pl.ds(8 + h, D, stride=h), :][:, 0:1] for c in range(2)]
        top = jnp.abs(zn[0, pl.ds(8, D, stride=h), :])
        for c in range(2):
            for n in range(h):
                top = jnp.maximum(top, jnp.abs(zn[c, pl.ds(8 + n, D, stride=h), :]))
        top = jnp.max(top, axis=1, keepdims=True)
        for v in left + right:
            top = jnp.maximum(top, jnp.abs(v))
        level = jnp.ceil(jnp.log2(jnp.maximum(top, 1e-30)))
        factor = jnp.exp2(-level) * FULL
        factors[h - 1] = jnp.broadcast_to(factor, (D, 128))
        for n, v in enumerate((left, right)):
            word = join(*[quantized(part, factor).astype(jnp.int32) for part in v])
            ends = jnp.where(lane == 8 * n + h - 1, word, ends)
        ends = jnp.where(lane == 16 + h - 1, level.astype(jnp.int32), ends)
    out[pl.ds(0, D, stride=ROWS), :] = ends
    for n in range(1, 4):
        out[pl.ds(n, D, stride=ROWS), :] = jnp.zeros((D, 128), jnp.int32)


def pack_harmonic(h, zn, factors, perm, out):
    factor = factors[h - 1]
    src = jnp.concatenate(
        [
            jnp.concatenate(
                [quantized(zn[c, pl.ds(8 + n, D, stride=h), :], factor) for n in range(h)], axis=1
            )
            for c in range(2)
        ],
        axis=0,
    )
    hi, lo = split(src)
    moved = dot(jnp.concatenate([hi, lo], axis=0), perm[...])
    moved = (moved[:128] + moved[128:]).astype(jnp.int32)
    word = join(moved[:64], moved[64:])
    for r in range(h):
        out[pl.ds(4 + FIRST[h] + r, D, stride=ROWS), :] = word[:, 128 * r : 128 * r + 128]


def unpack_ends(land, ends):
    lane = lax.broadcasted_iota(jnp.int32, (8, 128), 1)
    word = land[pl.ds(0, D, stride=ROWS), :]
    re, im = parted(word)
    zero = jnp.zeros((D, 128), F32)
    re, im, word = [jnp.concatenate([v.astype(F32), zero], axis=0).T for v in (re, im, word)]
    level = jnp.exp2(word[16:24]) * (1.0 / FULL)
    scale = jnp.where(lane < 64, level, pltpu.roll(level, 64, 1))
    for n in range(2):
        part = slice(8 * n, 8 * n + 8)
        ends[part, :] = jnp.where(lane < 64, re[part], pltpu.roll(im[part], 64, 1)) * scale
    ends[16:24, :] = scale


def unpack(land, ends, first, last, side, xl):
    def put(n, slot, hi, lo):
        xl[pl.ds(128 * n, 128), pl.ds(128 * slot, 128)] = hi
        xl[pl.ds(128 * n, 128), pl.ds(384 + 128 * slot, 128)] = lo

    for n in range(first, last):
        h, r = BLOCKS[n]
        re, im = parted(land[pl.ds(4 + n, D, stride=ROWS), :])
        block = jnp.concatenate([re.astype(F32), im.astype(F32)], axis=0).T * ends[15 + h : 16 + h, :]
        hi, lo = split(block)
        put(n, 1, hi, lo)
        if r > 0:
            put(n - 1, 2, hi, lo)
        if r < h - 1:
            put(n + 1, 0, hi, lo)
        if r == h - 1:
            side[n, 7:8, :] = ends[h - 1 : h, :]
            side[n, 8:72, :] = block[64:]
            before = jnp.concatenate([side[n, 7:71, :], block[:64]], axis=0)
            put(n - h + 1, 0, *split(before))
        if r == 0:
            side[n, 80:144, :] = block[:64]
            side[n, 144:145, :] = ends[h + 7 : h + 8, :]
            after = jnp.concatenate([block[64:], side[n, 81:145, :]], axis=0)
            put(n + h - 1, 2, *split(after))


def make_masks(jit, ex, jp, js, msk):
    for g in range(64):
        js[8 * g : 8 * g + 8, :] = jit[:, 128 * g : 128 * g + 128].astype(F32)
    for h in range(1, HARM + 1):
        even = js[pl.ds(h - 1, 64, stride=8), :]
        lhs = jnp.concatenate([even, pltpu.roll(even, 64, 1)], axis=0).astype(BF16)
        for n in range(FIRST[h], FIRST[h] + h):
            msk[pl.ds(128 * n, 128), :] = jnp.where(dot(lhs, ex[n]) == jp[n : n + 1, :], 1.0, 0.0)


def correlate(first, last, xl, taps, msk, pm):
    def template_pair(tp, carry):
        for g in range(first // 4, last // 4):
            rows = pl.ds(512 * g, 512)
            lhs = jnp.concatenate([xl[rows, :], xl[rows, 0:384]], axis=1)
            acc = dot(lhs, taps[tp])
            re, im = acc[:, :128], acc[:, 128:]
            kept = jnp.where(msk[rows, :] > 0.5, re * re + im * im, 0.0).astype(BF16)
            for q in range(4):
                pm[4 * g + q, pl.ds(pl.multiple_of(128 * tp, 128), 128), :] = kept[128 * q : 128 * q + 128]
        return carry

    lax.fori_loop(0, TMPL // 2, template_pair, 0)


def add_harmonics(pm, e, out):
    lane = lax.broadcasted_iota(jnp.int32, (64, 128), 1)
    for tp in range(TMPL // 4):
        rows = pl.ds(256 * tp, 256)
        total = jnp.zeros((256, 128), F32)
        for n in range(0, NB, 2):
            total += dot(
                jnp.concatenate([pm[n, rows, :], pm[n + 1, rows, :]], axis=1),
                jnp.concatenate([e[n], e[n + 1]], axis=0),
            )
        total = total * (1.0 / HARM)
        for q in range(2):
            even = total[128 * q : 128 * q + 64]
            odd = total[128 * q + 64 : 128 * q + 128]
            t = 4 * tp + 2 * q
            row = t // 8 * 512 + t % 8
            out[pl.ds(row, 64, stride=8), :] = jnp.where(lane < 64, even, pltpu.roll(odd, 64, 1))
            out[pl.ds(row + 1, 64, stride=8), :] = jnp.where(lane < 64, pltpu.roll(even, 64, 1), odd)


def search_kernel(*refs):
    series, coef, offset, jit, jp, w1_all = refs[:6]
    count = len(CONSTANTS)
    held = refs[6 : 6 + count]
    out = refs[6 + count]
    rest = refs[7 + count :]
    local, rest = rest[:count], rest[count:]
    xs, w1, send1, land1, send2, land2, zn, factors, send3, land3, ends, side, xl, pm, js, msk, vx, taps = rest[:18]
    const_sem, sems = rest[18:]
    me, dm = lax.axis_index("bin"), lax.axis_index("dm")
    own = [
        pltpu.make_async_copy(series, xs, const_sem.at[count]),
        pltpu.make_async_copy(w1_all.at[me], w1, const_sem.at[count + 1]),
    ]
    copies = {
        name: pltpu.make_async_copy(held[n], local[n], const_sem.at[n])
        for n, name in enumerate(CONSTANTS)
    }
    ref = dict(zip(CONSTANTS, local))
    for copy in own + list(copies.values()):
        copy.start()

    barrier = pltpu.get_barrier_semaphore()

    def greet(step, carry):
        pl.semaphore_signal(
            barrier, inc=1, device_id=(dm, partner(me, step)), device_id_type=pl.DeviceIdType.MESH
        )
        return carry

    lax.fori_loop(1, D, greet, 0)
    for copy in own:
        copy.wait()
    code_samples(xs, send1)
    pl.semaphore_wait(barrier, D - 1)

    exchange(me, dm, send1, land1, 0, 8, 8, (sems.at[0], sems.at[1]))
    make_tap_rows(coef, offset, vx)
    make_taps(vx, taps)
    copies["ex"].wait()
    make_masks(jit, ref["ex"], jp, js, msk)
    copies["tw1"].wait()
    wait_for(land1, 8, sems.at[1])
    columns(land1, w1, ref["tw1"], send2)
    exchange(me, dm, send2, land2, 0, 16, 16, (sems.at[2], sems.at[3]))
    for name in ("wah", "wal", "tw2", "vbh", "vbl", "e"):
        copies[name].wait()
    for h in range(1, HARM + 1):
        copies["p%d" % h].wait()
    wait_for(land2, 16, sems.at[3])
    local_fft(land2, ref["wah"], ref["wal"], ref["tw2"], ref["vbh"], ref["vbl"], zn)
    pack_ends(zn, factors, send3)
    for n, (row, rows, first, last) in enumerate(CHUNKS):
        for h in ORDER:
            if first <= FIRST[h] < last:
                pack_harmonic(h, zn, factors, ref["p%d" % h], send3)
        exchange(me, dm, send3, land3, row, rows, ROWS, (sems.at[4 + 2 * n], sems.at[5 + 2 * n]))
    for n, (row, rows, first, last) in enumerate(CHUNKS):
        wait_for(land3, rows, sems.at[5 + 2 * n])
        if n == 0:
            unpack_ends(land3, ends)
        unpack(land3, ends, first, last, side, xl)
        correlate(first, last, xl, taps, msk, pm)
    add_harmonics(pm, ref["e"], out)
    wait_for(land1, 8, sems.at[0])
    wait_for(land2, 16, sems.at[2])
    for n, (_, rows, _, _) in enumerate(CHUNKS):
        wait_for(land3, rows, sems.at[4 + 2 * n])


CONSTANTS = ("ex", "tw1", "wah", "wal", "tw2", "vbh", "vbl") + tuple(
    "p%d" % h for h in range(1, HARM + 1)
) + ("e",)


def constants():
    w1, tw1, wah, wal, tw2, vbh, vbl = fft_tables()
    e, ex, jp = select_tables()
    return [ex, tw1, wah, wal, tw2, vbh, vbl, *perm_tables(), e], jp, w1


def search(series, coef, offset, jit):
    held, jp, w1 = constants()
    whole = pl.BlockSpec(memory_space=pltpu.VMEM)
    far = pl.BlockSpec(memory_space=pl.ANY)
    return pl.pallas_call(
        search_kernel,
        out_shape=jax.ShapeDtypeStruct((TMPL * 64, 128), F32),
        in_specs=[far] + [whole] * 4 + [far] * (1 + len(held)),
        out_specs=whole,
        scratch_shapes=[pltpu.VMEM(c.shape, c.dtype) for c in held]
        + [
            pltpu.VMEM((1024, 128), F32),
            pltpu.VMEM((128, D), F32),
            pltpu.VMEM((512, 128), jnp.int32),
            pltpu.VMEM((512, 128), jnp.int32),
            pltpu.VMEM((1024, 128), jnp.int32),
            pltpu.VMEM((1024, 128), jnp.int32),
            pltpu.VMEM((2, 528, 128), F32),
            pltpu.VMEM((HARM, D, 128), F32),
            pltpu.VMEM((D * ROWS, 128), jnp.int32),
            pltpu.VMEM((D * ROWS, 128), jnp.int32),
            pltpu.VMEM((24, 128), F32),
            pltpu.VMEM((NB, 152, 128), F32),
            pltpu.VMEM((NB * 128, 768), BF16),
            pltpu.VMEM((NB, 1024, 128), BF16),
            pltpu.VMEM((512, 128), F32),
            pltpu.VMEM((NB * 128, 128), F32),
            pltpu.VMEM((TMPL, 8, 128), F32),
            pltpu.VMEM((TMPL // 2, 1152, 256), BF16),
            pltpu.SemaphoreType.DMA((len(held) + 2,)),
            pltpu.SemaphoreType.DMA((4 + 2 * len(CHUNKS),)),
        ],
        compiler_params=pltpu.CompilerParams(
            collective_id=0, has_side_effects=True, vmem_limit_bytes=62 * 1024 * 1024
        ),
        cost_estimate=pl.CostEstimate(flops=3 * 10**10, bytes_accessed=3 * 10**7, transcendentals=0),
    )(series, coef, offset, jit, jp, w1, *held)


def shards(series, tap_coef, tap_offset, harm_index):
    out = search(series.reshape(1024, 128), tap_coef.reshape(32, 128), tap_offset, harm_index)
    return out.reshape(2, 64, 8, 128).transpose(0, 2, 1, 3).reshape(TMPL, 8192)


def solution(mesh):
    return jax.shard_map(
        shards,
        mesh=mesh,
        in_specs=(P(("dm", "bin")), P(), P(), P(None, "bin")),
        out_specs=P(None, ("dm", "bin")),
        check_vma=False,
    )
```

```python
import functools
import math

import jax
import jax.numpy as jnp
import numpy as np
from jax import lax
from jax.experimental import pallas as pl
from jax.experimental.pallas import tpu as pltpu
from jax.sharding import PartitionSpec as P

D = 64
TMPL = 16
TAPS = 128
HARM = 8
LENGTH = 8388608
LOCAL = LENGTH // D
ALPHA = 512
BETA = 256
ORDER = (4, 8, 7, 1, 6, 2, 5, 3)
BLOCKS = tuple((h, r) for h in ORDER for r in range(h))
NB = len(BLOCKS)
FIRST = {h: BLOCKS.index((h, 0)) for h in ORDER}
ROWS = 40
CHUNKS = ((0, 8, 0, 4), (8, 8, 4, 12), (16, 8, 12, 20), (24, 8, 20, 28), (32, 8, 28, 36))
FULL = 32767.0
SAMPLE_BOUND = 6.0
PART_BOUND = SAMPLE_BOUND * D / math.sqrt(LENGTH)
F32 = jnp.float32
BF16 = jnp.bfloat16
F8 = jnp.float8_e4m3fn
LOW = 512.0


def np_split(x):
    x = np.asarray(x, np.float32)
    hi = x.astype(jnp.bfloat16)
    lo = (x - hi.astype(np.float32)).astype(jnp.bfloat16)
    return hi, lo


@functools.lru_cache(None)
def fft_tables():
    k1 = np.arange(D)[:, None]
    m = np.arange(LOCAL // D)[None, :]
    ang = -2 * np.pi * (k1 * m) / LENGTH
    tw1 = np.stack([np.cos(ang), np.sin(ang)]).astype(np.float32)
    k = np.arange(ALPHA)[:, None] * np.arange(ALPHA)[None, :] % ALPHA
    ang = -2 * np.pi * k / ALPHA
    c, s = np.cos(ang), np.sin(ang)
    wa = np.block([[c, -s], [s, c]])
    ang = -2 * np.pi * (np.arange(ALPHA)[:, None] * np.arange(BETA)[None, :]) / LOCAL
    tw2 = np.stack([np.cos(ang), np.sin(ang)]).astype(np.float32)
    half = BETA // 2
    ang = -2 * np.pi * (np.arange(BETA)[:, None] * np.arange(half)[None, :] % BETA) / BETA
    c, s = np.cos(ang), np.sin(ang)
    vb = np.block([[c, s], [-s, c]])
    k = k1 * (D * np.arange(D)[None, None, :] + np.arange(D)[:, None, None]) % (D * D)
    ang = -2 * np.pi * k / (D * D)
    w1 = np.concatenate([np.cos(ang), np.sin(ang)], axis=1) / math.sqrt(LENGTH)
    return w1.astype(np.float32), tw1, *np_split(wa), tw2, *np_split(vb)


@functools.lru_cache(None)
def perm_tables():
    out = []
    for h in range(1, HARM + 1):
        m = np.zeros((128 * h, 128 * h), np.float32)
        a = np.arange(128)
        for r in range(h):
            m[h * a + r, 128 * r + 64 * (a % 2) + a // 2] = 1
        out.append(m.astype(jnp.bfloat16))
    return tuple(out)


@functools.lru_cache(None)
def select_tables():
    i = np.arange(64)
    e = np.zeros((NB, 128, 128), np.float32)
    ex = np.zeros((NB, 128, 128), np.float32)
    jp = np.zeros((NB, 1, 128), np.float32)
    for n, (h, r) in enumerate(BLOCKS):
        b, j = np.divmod(64 * r + i, h)
        for t in range(2):
            e[n, 64 * t + i, 64 * t + b] = 1
            ex[n, b, 64 * t + i] = 1
            jp[n, 0, 64 * t + i] = j
    return e.astype(jnp.bfloat16), ex.astype(jnp.bfloat16), jp.reshape(NB, 128)


def split(x):
    hi = x.astype(BF16)
    return hi, (x - hi.astype(F32)).astype(BF16)


def dot(a, b):
    return jnp.dot(a, b, preferred_element_type=F32)


def dot3(ah, al, bh, bl):
    return dot(ah, bh) + dot(ah, bl) + dot(al, bh)


def encode(x, bound):
    size = jnp.sqrt(jnp.sqrt(jnp.abs(x) * (1.0 / bound)))
    code = jnp.minimum(size * FULL + 0.5, FULL).astype(jnp.int32)
    return jnp.where(x < 0, -code, code)


def decode(code, bound):
    x = code.astype(F32)
    return x * jnp.abs(x) * (x * x * (bound / FULL**4))


def join(high, low):
    return (high << 16) | (low & 0xFFFF)


def parted(word):
    return word >> 16, (word << 16) >> 16


def partner(me, step):
    def way(digit):
        return jnp.where(digit == 0, 2, jnp.where(digit == 2, 3, jnp.where(digit == 3, 0, 1)))

    x = (me // 16 + way(step // 16)) % 4
    y = (me // 4 + way(step // 4 % 4)) % 4
    return x * 16 + y * 4 + (me + way(step % 4)) % 4


def exchange(me, dm, src, dst, first, rows, pitch, sems):
    def start(step, carry):
        to = partner(me, step)
        pltpu.make_async_remote_copy(
            src_ref=src.at[pl.ds(pl.multiple_of(to * pitch + first, 8), rows)],
            dst_ref=dst.at[pl.ds(pl.multiple_of(me * pitch + first, 8), rows)],
            send_sem=sems[0],
            recv_sem=sems[1],
            device_id=(dm, to),
            device_id_type=pl.DeviceIdType.MESH,
        ).start()
        return carry

    lax.fori_loop(0, D - 1, start, 0)
    own = pl.ds(pl.multiple_of(me * pitch + first, 8), rows)
    dst[own, :] = src[own, :]


def wait_for(ref, rows, sem):
    part = ref.at[pl.ds(0, (D - 1) * rows)]
    pltpu.make_async_copy(part, part, sem).wait()


def make_taps(vx, taps, taps8):
    lane = lax.broadcasted_iota(jnp.int32, (64, 128), 1)

    def pair(tp, carry):
        for x in range(3):
            both = []
            for z in range(2):
                rolled = []
                for t in range(2):
                    row = vx[2 * tp + t, 3 * z + x : 3 * z + x + 1, :]
                    rolled.append(
                        pltpu.roll(jnp.broadcast_to(row, (64, 128)), 64 * t, 1, stride=1, stride_axis=0)
                    )
                v = jnp.where(lane < 64, rolled[0], rolled[1])
                high = v.astype(BF16).astype(F32)
                both.append((high, (v - high) * LOW))

            def put(ref, row, kind, tr, ti):
                ref[tp, row : row + 64, 0:128] = tr.astype(kind)
                ref[tp, row : row + 64, 128:256] = ti.astype(kind)
                ref[tp, row + 64 : row + 128, 0:128] = (-ti).astype(kind)
                ref[tp, row + 64 : row + 128, 128:256] = tr.astype(kind)

            (rh, rl), (ih, il) = both
            put(taps, 128 * x, BF16, rh * LOW, ih * LOW)
            put(taps8, 128 * x, F8, rl, il)
            put(taps8, 384 + 128 * x, F8, rh, ih)
        return carry

    lax.fori_loop(0, TMPL // 2, pair, 0)


def level_of(x):
    return jnp.ceil(jnp.log2(jnp.maximum(jnp.max(jnp.abs(x), keepdims=True), 1e-30)))


def make_tap_rows(coef, offset, vx, levels):
    lane = lax.broadcasted_iota(jnp.int32, (128, 384), 1)
    m = lane % 128
    lag = lane // 128 * 64 - jnp.where(m < 64, m, m - 128)
    lag = jnp.where(m == 64, -1, lag).astype(F32)
    where = jnp.concatenate([offset[...].astype(F32), jnp.zeros((112, 128), F32)], axis=0).T
    level = level_of(coef[...])
    factor = jnp.exp2(8.0 - level)
    levels[0:8, :] = jnp.broadcast_to(level, (8, 128))
    first = coef[...].astype(BF16)
    rest = coef[...] - first.astype(F32)
    second = rest.astype(BF16)
    third = (rest - second.astype(F32)).astype(BF16)
    lhs = jnp.concatenate([first, second, third], axis=0)
    for t in range(TMPL):
        onehot = jnp.where(where[:, t : t + 1] == lag, 1.0, 0.0).astype(BF16)
        rows = dot(lhs, onehot)
        rows = (rows[0:32] + rows[32:64] + rows[64:96]) * factor
        for z in range(2):
            for x in range(3):
                vx[t, 3 * z + x : 3 * z + x + 1, :] = rows[16 * z + t : 16 * z + t + 1, 128 * x : 128 * x + 128]


def code_samples(series, out):
    v = series[...].reshape(D, 16, 128)
    word = join(encode(v[:, :8], SAMPLE_BOUND), encode(v[:, 8:], SAMPLE_BOUND))
    out[...] = word.reshape(512, 128)


def columns(xs, w1, tw, out):
    pairs = [parted(xs[pl.ds(m, D, stride=8), :]) for m in range(8)]
    x = jnp.concatenate([p[0] for p in pairs] + [p[1] for p in pairs], axis=1)
    y = dot3(*split(w1[...]), *split(decode(x, SAMPLE_BOUND)))
    yr, yi = y[:D], y[D:]
    zr = yr * tw[0] - yi * tw[1]
    zi = yr * tw[1] + yi * tw[0]
    word = join(encode(zr, PART_BOUND), encode(zi, PART_BOUND))
    for m in range(16):
        out[pl.ds((m % 2) * 8 + m // 2, D, stride=16), :] = word[:, 128 * m : 128 * m + 128]


def local_fft(b, wah, wal, tw, vbh, vbl, zn, levels):
    v = b[...].reshape(D, 2, 8, 128)
    word = jnp.concatenate([v[:, n].reshape(ALPHA, 128) for n in range(2)], axis=1)
    rhs = jnp.concatenate([decode(x, PART_BOUND) for x in parted(word)], axis=0)
    y = dot3(wah[...], wal[...], *split(rhs))
    yr, yi = y[:ALPHA], y[ALPHA:]
    t = jnp.concatenate([yr * tw[0] - yi * tw[1], yr * tw[1] + yi * tw[0]], axis=1)
    th, tl = split(t)
    z = dot3(th, tl, vbh[...], vbl[...])
    level = level_of(z)
    levels[16:24, :] = jnp.broadcast_to(level, (8, 128))
    z = jnp.clip(jnp.round(z * (jnp.exp2(-level) * FULL)), -FULL, FULL)
    zero = jnp.zeros((8, 128), F32)
    for c in range(2):
        zt = z[:, 128 * c : 128 * c + 128].T
        zn[c, 0:8, :] = zero
        zn[c, 520:528, :] = zero
        for n in range(4):
            zn[c, pl.ds(8 + n, 128, stride=4), :] = zt[:, 128 * n : 128 * n + 128]


def pack_ends(zn, levels, out):
    lane = lax.broadcasted_iota(jnp.int32, (D, 128), 1)
    ends = jnp.broadcast_to(levels[16:17, :], (D, 128)).astype(jnp.int32)
    for h in range(1, HARM + 1):
        left = [zn[c, pl.ds(7, D, stride=h), :].astype(jnp.int32) for c in range(2)]
        right = [zn[c, pl.ds(8 + h, D, stride=h), :].astype(jnp.int32) for c in range(2)]
        ends = jnp.where(lane == h - 1, join(*left)[:, 127:128], ends)
        ends = jnp.where(lane == 8 + h - 1, join(*right)[:, 0:1], ends)
    out[pl.ds(0, D, stride=ROWS), :] = ends
    for n in range(1, 4):
        out[pl.ds(n, D, stride=ROWS), :] = jnp.zeros((D, 128), jnp.int32)


def pack_harmonic(h, zn, perm, out):
    src = jnp.concatenate(
        [
            jnp.concatenate([zn[c, pl.ds(8 + n, D, stride=h), :] for n in range(h)], axis=1)
            for c in range(2)
        ],
        axis=0,
    )
    hi, lo = split(src)
    moved = dot(jnp.concatenate([hi, lo], axis=0), perm[...])
    moved = (moved[:128] + moved[128:]).astype(jnp.int32)
    word = join(moved[:64], moved[64:])
    for r in range(h):
        out[pl.ds(4 + FIRST[h] + r, D, stride=ROWS), :] = word[:, 128 * r : 128 * r + 128]


def unpack_ends(land, ends, levels):
    lane = lax.broadcasted_iota(jnp.int32, (8, 128), 1)
    word = land[pl.ds(0, D, stride=ROWS), :]
    re, im = parted(word)
    zero = jnp.zeros((D, 128), F32)
    re, im, word = [jnp.concatenate([v.astype(F32), zero], axis=0).T for v in (re, im, word)]
    level = jnp.where(lane < 64, word[16:24], -1000.0)
    top = jnp.max(level[0:1], axis=1, keepdims=True)
    levels[8:16, :] = jnp.broadcast_to(top, (8, 128))
    scale = jnp.exp2(level - top + 8.0) * (1.0 / FULL)
    scale = jnp.where(lane < 64, scale, pltpu.roll(scale, 64, 1))
    scale = jnp.broadcast_to(scale[0:1], (8, 128))
    for n in range(2):
        part = slice(8 * n, 8 * n + 8)
        ends[part, :] = jnp.where(lane < 64, re[part], pltpu.roll(im[part], 64, 1)) * scale
    ends[16:24, :] = scale


def unpack(land, ends, first, last, side, xl, xl8):
    def put(n, slot, x):
        high = x.astype(BF16)
        wide = high.astype(F32)
        parts = (high, wide.astype(F8), ((x - wide) * LOW).astype(F8))
        return put_parts(n, slot, parts)

    def put_parts(n, slot, parts):
        xl[pl.ds(128 * n, 128), pl.ds(128 * slot, 128)] = parts[0]
        xl8[pl.ds(128 * n, 128), pl.ds(128 * slot, 128)] = parts[1]
        xl8[pl.ds(128 * n, 128), pl.ds(384 + 128 * slot, 128)] = parts[2]
        return parts

    for n in range(first, last):
        h, r = BLOCKS[n]
        re, im = parted(land[pl.ds(4 + n, D, stride=ROWS), :])
        block = jnp.concatenate([re.astype(F32), im.astype(F32)], axis=0).T * ends[16:17, :]
        parts = put(n, 1, block)
        if r > 0:
            put_parts(n - 1, 2, parts)
        if r < h - 1:
            put_parts(n + 1, 0, parts)
        if r == h - 1:
            side[7:8, :] = ends[h - 1 : h, :]
            side[8:72, :] = block[64:]
            put(n - h + 1, 0, jnp.concatenate([side[7:71, :], block[:64]], axis=0))
        if r == 0:
            side[80:144, :] = block[:64]
            side[144:145, :] = ends[h + 7 : h + 8, :]
            put(n + h - 1, 2, jnp.concatenate([block[64:], side[81:145, :]], axis=0))


def make_masks(jit, ex, jp, js, msk):
    for g in range(64):
        js[8 * g : 8 * g + 8, :] = jit[:, 128 * g : 128 * g + 128].astype(F32)
    for h in range(1, HARM + 1):
        even = js[pl.ds(h - 1, 64, stride=8), :]
        lhs = jnp.concatenate([even, pltpu.roll(even, 64, 1)], axis=0).astype(BF16)
        for n in range(FIRST[h], FIRST[h] + h):
            msk[pl.ds(128 * n, 128), :] = jnp.where(dot(lhs, ex[n]) == jp[n : n + 1, :], 1.0, 0.0)


def correlate(first, last, xl, xl8, taps, taps8, msk, pm):
    def template_pair(tp, carry):
        for g in range(first // 4, last // 4):
            rows = pl.ds(512 * g, 512)
            acc = dot(xl[rows, :], taps[tp]) + dot(xl8[rows, :], taps8[tp])
            re, im = acc[:, :128], acc[:, 128:]
            kept = jnp.where(msk[rows, :] > 0.5, re * re + im * im, 0.0).astype(BF16)
            for q in range(4):
                pm[4 * g + q, pl.ds(pl.multiple_of(128 * tp, 128), 128), :] = kept[128 * q : 128 * q + 128]
        return carry

    lax.fori_loop(0, TMPL // 2, template_pair, 0)


def add_harmonics(pm, e, levels, out):
    factor = jnp.exp2(2.0 * (levels[0:1, :] + levels[8:9, :] - 25.0)) * (1.0 / HARM)
    lane = lax.broadcasted_iota(jnp.int32, (64, 128), 1)
    for tp in range(TMPL // 4):
        rows = pl.ds(256 * tp, 256)
        total = jnp.zeros((256, 128), F32)
        for n in range(0, NB, 2):
            total += dot(
                jnp.concatenate([pm[n, rows, :], pm[n + 1, rows, :]], axis=1),
                jnp.concatenate([e[n], e[n + 1]], axis=0),
            )
        total = total * factor
        for q in range(2):
            even = total[128 * q : 128 * q + 64]
            odd = total[128 * q + 64 : 128 * q + 128]
            t = 4 * tp + 2 * q
            row = t // 8 * 512 + t % 8
            out[pl.ds(row, 64, stride=8), :] = jnp.where(lane < 64, even, pltpu.roll(odd, 64, 1))
            out[pl.ds(row + 1, 64, stride=8), :] = jnp.where(lane < 64, pltpu.roll(even, 64, 1), odd)


def search_kernel(*refs):
    series, coef, offset, jit, jp, w1_all = refs[:6]
    count = len(CONSTANTS)
    held = refs[6 : 6 + count]
    out = refs[6 + count]
    rest = refs[7 + count :]
    local, rest = rest[:count], rest[count:]
    xs, w1, send1, land1, send2, land2, zn, levels, send3, land3, ends, side = rest[:12]
    xl, xl8, pm, js, msk, vx, taps, taps8, const_sem, sems = rest[12:]
    me, dm = lax.axis_index("bin"), lax.axis_index("dm")
    own = [
        pltpu.make_async_copy(series, xs, const_sem.at[count]),
        pltpu.make_async_copy(w1_all.at[me], w1, const_sem.at[count + 1]),
    ]
    copies = {
        name: pltpu.make_async_copy(held[n], local[n], const_sem.at[n])
        for n, name in enumerate(CONSTANTS)
    }
    ref = dict(zip(CONSTANTS, local))
    for copy in own:
        copy.start()

    barrier = pltpu.get_barrier_semaphore()

    def greet(step, carry):
        pl.semaphore_signal(
            barrier, inc=1, device_id=(dm, partner(me, step)), device_id_type=pl.DeviceIdType.MESH
        )
        return carry

    lax.fori_loop(0, D - 1, greet, 0)
    for copy in copies.values():
        copy.start()
    for copy in own:
        copy.wait()
    code_samples(xs, send1)
    pl.semaphore_wait(barrier, D - 1)

    exchange(me, dm, send1, land1, 0, 8, 8, (sems.at[0], sems.at[1]))
    make_tap_rows(coef, offset, vx, levels)
    make_taps(vx, taps, taps8)
    copies["ex"].wait()
    make_masks(jit, ref["ex"], jp, js, msk)
    copies["tw1"].wait()
    wait_for(land1, 8, sems.at[1])
    columns(land1, w1, ref["tw1"], send2)
    exchange(me, dm, send2, land2, 0, 16, 16, (sems.at[2], sems.at[3]))
    for name in ("wah", "wal", "tw2", "vbh", "vbl", "e"):
        copies[name].wait()
    for h in range(1, HARM + 1):
        copies["p%d" % h].wait()
    wait_for(land2, 16, sems.at[3])
    local_fft(land2, ref["wah"], ref["wal"], ref["tw2"], ref["vbh"], ref["vbl"], zn, levels)
    pack_ends(zn, levels, send3)

    def give(n):
        row, rows, first, last = CHUNKS[n]
        for h in ORDER:
            if first <= FIRST[h] < last:
                pack_harmonic(h, zn, ref["p%d" % h], send3)
        exchange(me, dm, send3, land3, row, rows, ROWS, (sems.at[4 + 2 * n], sems.at[5 + 2 * n]))

    def take(n):
        _, rows, first, last = CHUNKS[n]
        wait_for(land3, rows, sems.at[5 + 2 * n])
        if n == 0:
            unpack_ends(land3, ends, levels)
        unpack(land3, ends, first, last, side, xl, xl8)
        correlate(first, last, xl, xl8, taps, taps8, msk, pm)

    for act, n in SCHEDULE:
        (give if act else take)(n)
    add_harmonics(pm, ref["e"], levels, out)
    wait_for(land1, 8, sems.at[0])
    wait_for(land2, 16, sems.at[2])
    for n, (_, rows, _, _) in enumerate(CHUNKS):
        wait_for(land3, rows, sems.at[4 + 2 * n])


SCHEDULE = ((1, 0), (1, 1), (1, 2), (0, 0), (1, 3), (0, 1), (1, 4), (0, 2), (0, 3), (0, 4))
CONSTANTS = ("ex", "tw1", "wah", "wal", "tw2", "vbh", "vbl") + tuple(
    "p%d" % h for h in range(1, HARM + 1)
) + ("e",)


def constants():
    w1, tw1, wah, wal, tw2, vbh, vbl = fft_tables()
    e, ex, jp = select_tables()
    return [ex, tw1, wah, wal, tw2, vbh, vbl, *perm_tables(), e], jp, w1


def search(series, coef, offset, jit):
    held, jp, w1 = constants()
    whole = pl.BlockSpec(memory_space=pltpu.VMEM)
    far = pl.BlockSpec(memory_space=pl.ANY)
    return pl.pallas_call(
        search_kernel,
        out_shape=jax.ShapeDtypeStruct((TMPL * 64, 128), F32),
        in_specs=[far] + [whole] * 4 + [far] * (1 + len(held)),
        out_specs=whole,
        scratch_shapes=[pltpu.VMEM(c.shape, c.dtype) for c in held]
        + [
            pltpu.VMEM((1024, 128), F32),
            pltpu.VMEM((128, D), F32),
            pltpu.VMEM((512, 128), jnp.int32),
            pltpu.VMEM((512, 128), jnp.int32),
            pltpu.VMEM((1024, 128), jnp.int32),
            pltpu.VMEM((1024, 128), jnp.int32),
            pltpu.VMEM((2, 528, 128), F32),
            pltpu.VMEM((24, 128), F32),
            pltpu.VMEM((D * ROWS, 128), jnp.int32),
            pltpu.VMEM((D * ROWS, 128), jnp.int32),
            pltpu.VMEM((24, 128), F32),
            pltpu.VMEM((152, 128), F32),
            pltpu.VMEM((NB * 128, 384), BF16),
            pltpu.VMEM((NB * 128, 768), F8),
            pltpu.VMEM((NB, 1024, 128), BF16),
            pltpu.VMEM((512, 128), F32),
            pltpu.VMEM((NB * 128, 128), F32),
            pltpu.VMEM((TMPL, 8, 128), F32),
            pltpu.VMEM((TMPL // 2, 384, 256), BF16),
            pltpu.VMEM((TMPL // 2, 768, 256), F8),
            pltpu.SemaphoreType.DMA((len(held) + 2,)),
            pltpu.SemaphoreType.DMA((4 + 2 * len(CHUNKS),)),
        ],
        compiler_params=pltpu.CompilerParams(
            collective_id=0, has_side_effects=True, vmem_limit_bytes=62 * 1024 * 1024
        ),
        cost_estimate=pl.CostEstimate(flops=3 * 10**10, bytes_accessed=3 * 10**7, transcendentals=0),
    )(series, coef, offset, jit, jp, w1, *held)


def shards(series, tap_coef, tap_offset, harm_index):
    out = search(series.reshape(1024, 128), tap_coef.reshape(32, 128), tap_offset, harm_index)
    return out.reshape(2, 64, 8, 128).transpose(0, 2, 1, 3).reshape(TMPL, 8192)


def solution(mesh):
    return jax.shard_map(
        shards,
        mesh=mesh,
        in_specs=(P(("dm", "bin")), P(), P(), P(None, "bin")),
        out_specs=P(None, ("dm", "bin")),
        check_vma=False,
    )
```

```python
import functools
import math

import jax
import jax.numpy as jnp
import numpy as np
from jax import lax
from jax.experimental import pallas as pl
from jax.experimental.pallas import tpu as pltpu
from jax.sharding import PartitionSpec as P

D = 64
TMPL = 16
TAPS = 128
HARM = 8
LENGTH = 8388608
LOCAL = LENGTH // D
ALPHA = 512
BETA = 256
ORDER = (4, 8, 7, 1, 6, 2, 5, 3)
BLOCKS = tuple((h, r) for h in ORDER for r in range(h))
NB = len(BLOCKS)
FIRST = {h: BLOCKS.index((h, 0)) for h in ORDER}
ROWS = 40
CHUNKS = ((0, 8, 0, 4), (8, 16, 4, 20), (24, 16, 20, 36))
FULL = 32767.0
SAMPLE_BOUND = 6.0
PART_BOUND = SAMPLE_BOUND * D / math.sqrt(LENGTH)
F32 = jnp.float32
BF16 = jnp.bfloat16
F8 = jnp.float8_e4m3fn
LOW = 512.0


def np_split(x):
    x = np.asarray(x, np.float32)
    hi = x.astype(jnp.bfloat16)
    lo = (x - hi.astype(np.float32)).astype(jnp.bfloat16)
    return hi, lo


@functools.lru_cache(None)
def fft_tables():
    k1 = np.arange(D)[:, None]
    m = np.arange(LOCAL // D)[None, :]
    ang = -2 * np.pi * (k1 * m) / LENGTH
    tw1 = np.stack([np.cos(ang), np.sin(ang)]).astype(np.float32)
    k = np.arange(ALPHA)[:, None] * np.arange(ALPHA)[None, :] % ALPHA
    ang = -2 * np.pi * k / ALPHA
    c, s = np.cos(ang), np.sin(ang)
    wa = np.block([[c, -s], [s, c]])
    ang = -2 * np.pi * (np.arange(ALPHA)[:, None] * np.arange(BETA)[None, :]) / LOCAL
    tw2 = np.stack([np.cos(ang), np.sin(ang)]).astype(np.float32)
    half = BETA // 2
    ang = -2 * np.pi * (np.arange(BETA)[:, None] * np.arange(half)[None, :] % BETA) / BETA
    c, s = np.cos(ang), np.sin(ang)
    vb = np.block([[c, s], [-s, c]])
    k = k1 * (D * np.arange(D)[None, None, :] + np.arange(D)[:, None, None]) % (D * D)
    ang = -2 * np.pi * k / (D * D)
    w1 = np.concatenate([np.cos(ang), np.sin(ang)], axis=1) / math.sqrt(LENGTH)
    return w1.astype(np.float32), tw1, *np_split(wa), tw2, *np_split(vb)


@functools.lru_cache(None)
def perm_tables():
    out = []
    for h in range(1, HARM + 1):
        m = np.zeros((128 * h, 128 * h), np.float32)
        a = np.arange(128)
        for r in range(h):
            m[h * a + r, 128 * r + 64 * (a % 2) + a // 2] = 1
        out.append(m.astype(jnp.bfloat16))
    return tuple(out)


@functools.lru_cache(None)
def select_tables():
    i = np.arange(64)
    e = np.zeros((NB, 128, 128), np.float32)
    ex = np.zeros((NB, 128, 128), np.float32)
    jp = np.zeros((NB, 1, 128), np.float32)
    for n, (h, r) in enumerate(BLOCKS):
        b, j = np.divmod(64 * r + i, h)
        for t in range(2):
            e[n, 64 * t + i, 64 * t + b] = 1
            ex[n, b, 64 * t + i] = 1
            jp[n, 0, 64 * t + i] = j
    return e.astype(jnp.bfloat16), ex.astype(jnp.bfloat16), jp.reshape(NB, 128)


def split(x):
    hi = x.astype(BF16)
    return hi, (x - hi.astype(F32)).astype(BF16)


def dot(a, b):
    return jnp.dot(a, b, preferred_element_type=F32)


def dot3(ah, al, bh, bl):
    return dot(ah, bh) + dot(ah, bl) + dot(al, bh)


def encode(x, bound):
    size = jnp.sqrt(jnp.sqrt(jnp.abs(x) * (1.0 / bound)))
    code = jnp.minimum(size * FULL + 0.5, FULL).astype(jnp.int32)
    return jnp.where(x < 0, -code, code)


def decode(code, bound):
    x = code.astype(F32)
    return x * jnp.abs(x) * (x * x * (bound / FULL**4))


def join(high, low):
    return (high << 16) | (low & 0xFFFF)


def parted(word):
    return word >> 16, (word << 16) >> 16


def for_partners(me, act):
    far = (2, 1, 3, 0)
    x = [(me // 16 + k) % 4 * 16 for k in far]
    y = [(me // 4 + k) % 4 * 4 for k in far]
    z = [(me + k) % 4 for k in far]
    plane = [b + c for b in y for c in z][:-1]

    def row(i, carry):
        first = (me // 16 + 2 + i) % 4 * 16
        for v in plane:
            act(first + v)
        return carry

    lax.fori_loop(0, 4, row, 0)
    for v in x[:-1]:
        act(v + y[-1] + z[-1])


def exchange(me, dm, src, dst, first, rows, pitch, sems):
    target = dst.at[pl.ds(pl.multiple_of(me * pitch + first, 8), rows)]

    def start(to):
        pltpu.make_async_remote_copy(
            src_ref=src.at[pl.ds(pl.multiple_of(to * pitch + first, 8), rows)],
            dst_ref=target,
            send_sem=sems[0],
            recv_sem=sems[1],
            device_id=(dm, to),
            device_id_type=pl.DeviceIdType.MESH,
        ).start()

    for_partners(me, start)
    own = pl.ds(pl.multiple_of(me * pitch + first, 8), rows)
    dst[own, :] = src[own, :]


def wait_for(ref, rows, sem):
    part = ref.at[pl.ds(0, (D - 1) * rows)]
    pltpu.make_async_copy(part, part, sem).wait()


def make_taps(vx, taps, taps8):
    lane = lax.broadcasted_iota(jnp.int32, (64, 128), 1)

    def pair(tp, carry):
        for x in range(3):
            both = []
            for z in range(2):
                rolled = []
                for t in range(2):
                    row = vx[2 * tp + t, 3 * z + x : 3 * z + x + 1, :]
                    rolled.append(
                        pltpu.roll(jnp.broadcast_to(row, (64, 128)), 64 * t, 1, stride=1, stride_axis=0)
                    )
                v = jnp.where(lane < 64, rolled[0], rolled[1])
                high = v.astype(BF16).astype(F32)
                both.append((high, (v - high) * LOW))

            def put(ref, row, kind, tr, ti):
                ref[tp, row : row + 64, 0:128] = tr.astype(kind)
                ref[tp, row : row + 64, 128:256] = ti.astype(kind)
                ref[tp, row + 64 : row + 128, 0:128] = (-ti).astype(kind)
                ref[tp, row + 64 : row + 128, 128:256] = tr.astype(kind)

            (rh, rl), (ih, il) = both
            put(taps, 128 * x, BF16, rh * LOW, ih * LOW)
            put(taps8, 128 * x, F8, rl, il)
            put(taps8, 384 + 128 * x, F8, rh, ih)
        return carry

    lax.fori_loop(0, TMPL // 2, pair, 0)


def level_of(x):
    return jnp.ceil(jnp.log2(jnp.maximum(jnp.max(jnp.abs(x), keepdims=True), 1e-30)))


def make_tap_rows(coef, offset, vx, levels):
    lane = lax.broadcasted_iota(jnp.int32, (128, 384), 1)
    m = lane % 128
    lag = lane // 128 * 64 - jnp.where(m < 64, m, m - 128)
    lag = jnp.where(m == 64, -1, lag).astype(F32)
    where = jnp.concatenate([offset[...].astype(F32), jnp.zeros((112, 128), F32)], axis=0).T
    level = level_of(coef[...])
    factor = jnp.exp2(8.0 - level)
    levels[0:8, :] = jnp.broadcast_to(level, (8, 128))
    first = coef[...].astype(BF16)
    rest = coef[...] - first.astype(F32)
    second = rest.astype(BF16)
    third = (rest - second.astype(F32)).astype(BF16)
    lhs = jnp.concatenate([first, second, third], axis=0)
    for t in range(TMPL):
        onehot = jnp.where(where[:, t : t + 1] == lag, 1.0, 0.0).astype(BF16)
        rows = dot(lhs, onehot)
        rows = (rows[0:32] + rows[32:64] + rows[64:96]) * factor
        for z in range(2):
            for x in range(3):
                vx[t, 3 * z + x : 3 * z + x + 1, :] = rows[16 * z + t : 16 * z + t + 1, 128 * x : 128 * x + 128]


def code_samples(series, out):
    v = series[...].reshape(D, 16, 128)
    word = join(encode(v[:, :8], SAMPLE_BOUND), encode(v[:, 8:], SAMPLE_BOUND))
    out[...] = word.reshape(512, 128)


def columns(xs, w1, tw, out):
    pairs = [parted(xs[pl.ds(m, D, stride=8), :]) for m in range(8)]
    x = jnp.concatenate([p[0] for p in pairs] + [p[1] for p in pairs], axis=1)
    y = dot3(*split(w1[...]), *split(decode(x, SAMPLE_BOUND)))
    yr, yi = y[:D], y[D:]
    zr = yr * tw[0] - yi * tw[1]
    zi = yr * tw[1] + yi * tw[0]
    word = join(encode(zr, PART_BOUND), encode(zi, PART_BOUND))
    for m in range(16):
        out[pl.ds((m % 2) * 8 + m // 2, D, stride=16), :] = word[:, 128 * m : 128 * m + 128]


def local_fft(b, wah, wal, tw, vbh, vbl, zn, levels):
    v = b[...].reshape(D, 2, 8, 128)
    word = jnp.concatenate([v[:, n].reshape(ALPHA, 128) for n in range(2)], axis=1)
    rhs = jnp.concatenate([decode(x, PART_BOUND) for x in parted(word)], axis=0)
    y = dot3(wah[...], wal[...], *split(rhs))
    yr, yi = y[:ALPHA], y[ALPHA:]
    t = jnp.concatenate([yr * tw[0] - yi * tw[1], yr * tw[1] + yi * tw[0]], axis=1)
    th, tl = split(t)
    z = dot3(th, tl, vbh[...], vbl[...])
    level = level_of(z)
    levels[16:24, :] = jnp.broadcast_to(level, (8, 128))
    z = jnp.clip(jnp.round(z * (jnp.exp2(-level) * FULL)), -FULL, FULL)
    zero = jnp.zeros((8, 128), F32)
    for c in range(2):
        zt = z[:, 128 * c : 128 * c + 128].T
        zn[c, 0:8, :] = zero
        zn[c, 520:528, :] = zero
        for n in range(4):
            zn[c, pl.ds(8 + n, 128, stride=4), :] = zt[:, 128 * n : 128 * n + 128]


def pack_ends(zn, levels, out):
    lane = lax.broadcasted_iota(jnp.int32, (D, 128), 1)
    ends = jnp.broadcast_to(levels[16:17, :], (D, 128)).astype(jnp.int32)
    for h in range(1, HARM + 1):
        left = [zn[c, pl.ds(7, D, stride=h), :].astype(jnp.int32) for c in range(2)]
        right = [zn[c, pl.ds(8 + h, D, stride=h), :].astype(jnp.int32) for c in range(2)]
        ends = jnp.where(lane == h - 1, join(*left)[:, 127:128], ends)
        ends = jnp.where(lane == 8 + h - 1, join(*right)[:, 0:1], ends)
    out[pl.ds(0, D, stride=ROWS), :] = ends
    for n in range(1, 4):
        out[pl.ds(n, D, stride=ROWS), :] = jnp.zeros((D, 128), jnp.int32)


def pack_harmonic(h, zn, perm, out):
    src = jnp.concatenate(
        [
            jnp.concatenate([zn[c, pl.ds(8 + n, D, stride=h), :] for n in range(h)], axis=1)
            for c in range(2)
        ],
        axis=0,
    )
    hi, lo = split(src)
    moved = dot(jnp.concatenate([hi, lo], axis=0), perm[...])
    moved = (moved[:128] + moved[128:]).astype(jnp.int32)
    word = join(moved[:64], moved[64:])
    for r in range(h):
        out[pl.ds(4 + FIRST[h] + r, D, stride=ROWS), :] = word[:, 128 * r : 128 * r + 128]


def unpack_ends(land, ends, levels):
    lane = lax.broadcasted_iota(jnp.int32, (8, 128), 1)
    word = land[pl.ds(0, D, stride=ROWS), :]
    re, im = parted(word)
    zero = jnp.zeros((D, 128), F32)
    re, im, word = [jnp.concatenate([v.astype(F32), zero], axis=0).T for v in (re, im, word)]
    level = jnp.where(lane < 64, word[16:24], -1000.0)
    top = jnp.max(level[0:1], axis=1, keepdims=True)
    levels[8:16, :] = jnp.broadcast_to(top, (8, 128))
    scale = jnp.exp2(level - top + 8.0) * (1.0 / FULL)
    scale = jnp.where(lane < 64, scale, pltpu.roll(scale, 64, 1))
    scale = jnp.broadcast_to(scale[0:1], (8, 128))
    for n in range(2):
        part = slice(8 * n, 8 * n + 8)
        ends[part, :] = jnp.where(lane < 64, re[part], pltpu.roll(im[part], 64, 1)) * scale
    ends[16:24, :] = scale


def unpack(land, ends, first, last, side, xl, xl8):
    def put(n, slot, x):
        high = x.astype(BF16)
        wide = high.astype(F32)
        parts = (high, wide.astype(F8), ((x - wide) * LOW).astype(F8))
        return put_parts(n, slot, parts)

    def put_parts(n, slot, parts):
        xl[pl.ds(128 * n, 128), pl.ds(128 * slot, 128)] = parts[0]
        xl8[pl.ds(128 * n, 128), pl.ds(128 * slot, 128)] = parts[1]
        xl8[pl.ds(128 * n, 128), pl.ds(384 + 128 * slot, 128)] = parts[2]
        return parts

    for n in range(first, last):
        h, r = BLOCKS[n]
        re, im = parted(land[pl.ds(4 + n, D, stride=ROWS), :])
        block = jnp.concatenate([re.astype(F32), im.astype(F32)], axis=0).T * ends[16:17, :]
        parts = put(n, 1, block)
        if r > 0:
            put_parts(n - 1, 2, parts)
        if r < h - 1:
            put_parts(n + 1, 0, parts)
        if r == h - 1:
            side[7:8, :] = ends[h - 1 : h, :]
            side[8:72, :] = block[64:]
            put(n - h + 1, 0, jnp.concatenate([side[7:71, :], block[:64]], axis=0))
        if r == 0:
            side[80:144, :] = block[:64]
            side[144:145, :] = ends[h + 7 : h + 8, :]
            put(n + h - 1, 2, jnp.concatenate([block[64:], side[81:145, :]], axis=0))


def make_masks(jit, ex, jp, js, msk):
    for g in range(64):
        js[8 * g : 8 * g + 8, :] = jit[:, 128 * g : 128 * g + 128].astype(F32)
    for h in range(1, HARM + 1):
        even = js[pl.ds(h - 1, 64, stride=8), :]
        lhs = jnp.concatenate([even, pltpu.roll(even, 64, 1)], axis=0).astype(BF16)
        for n in range(FIRST[h], FIRST[h] + h):
            msk[pl.ds(128 * n, 128), :] = jnp.where(dot(lhs, ex[n]) == jp[n : n + 1, :], 1.0, 0.0)


def correlate(first, last, xl, xl8, taps, taps8, msk, pm):
    groups = range(first // 4, last // 4)
    pairs = max(1, 8 // len(groups))

    def one(tp):
        for g in groups:
            rows = pl.ds(512 * g, 512)
            acc = dot(xl[rows, :], taps[tp]) + dot(xl8[rows, :], taps8[tp])
            re, im = acc[:, :128], acc[:, 128:]
            kept = jnp.where(msk[rows, :] > 0.5, re * re + im * im, 0.0).astype(BF16)
            for q in range(4):
                pm[4 * g + q, pl.ds(pl.multiple_of(128 * tp, 128), 128), :] = kept[128 * q : 128 * q + 128]

    def several(step, carry):
        for k in range(pairs):
            one(pairs * step + k)
        return carry

    lax.fori_loop(0, TMPL // 2 // pairs, several, 0)


def add_harmonics(pm, e, levels, out):
    factor = jnp.exp2(2.0 * (levels[0:1, :] + levels[8:9, :] - 25.0)) * (1.0 / HARM)
    lane = lax.broadcasted_iota(jnp.int32, (64, 128), 1)
    for tp in range(TMPL // 4):
        rows = pl.ds(256 * tp, 256)
        total = jnp.zeros((256, 128), F32)
        for n in range(0, NB, 2):
            total += dot(
                jnp.concatenate([pm[n, rows, :], pm[n + 1, rows, :]], axis=1),
                jnp.concatenate([e[n], e[n + 1]], axis=0),
            )
        total = total * factor
        for q in range(2):
            even = total[128 * q : 128 * q + 64]
            odd = total[128 * q + 64 : 128 * q + 128]
            t = 4 * tp + 2 * q
            row = t // 8 * 512 + t % 8
            out[pl.ds(row, 64, stride=8), :] = jnp.where(lane < 64, even, pltpu.roll(odd, 64, 1))
            out[pl.ds(row + 1, 64, stride=8), :] = jnp.where(lane < 64, pltpu.roll(even, 64, 1), odd)


def search_kernel(*refs):
    series, coef, offset, jit, jp, w1_all = refs[:6]
    count = len(CONSTANTS)
    held = refs[6 : 6 + count]
    out = refs[6 + count]
    rest = refs[7 + count :]
    local, rest = rest[:count], rest[count:]
    xs, w1, send1, land1, send2, land2, zn, levels, send3, land3, ends, side = rest[:12]
    xl, xl8, pm, js, msk, vx, taps, taps8, const_sem, sems = rest[12:]
    me, dm = lax.axis_index("bin"), lax.axis_index("dm")
    own = [
        pltpu.make_async_copy(series, xs, const_sem.at[count]),
        pltpu.make_async_copy(w1_all.at[me], w1, const_sem.at[count + 1]),
    ]
    copies = {
        name: pltpu.make_async_copy(held[n], local[n], const_sem.at[n])
        for n, name in enumerate(CONSTANTS)
    }
    ref = dict(zip(CONSTANTS, local))
    for copy in own:
        copy.start()

    barrier = pltpu.get_barrier_semaphore()

    def greet(to):
        pl.semaphore_signal(barrier, inc=1, device_id=(dm, to), device_id_type=pl.DeviceIdType.MESH)

    for_partners(me, greet)
    for copy in copies.values():
        copy.start()
    for copy in own:
        copy.wait()
    code_samples(xs, send1)
    pl.semaphore_wait(barrier, D - 1)

    exchange(me, dm, send1, land1, 0, 8, 8, (sems.at[0], sems.at[1]))
    make_tap_rows(coef, offset, vx, levels)
    make_taps(vx, taps, taps8)
    copies["ex"].wait()
    make_masks(jit, ref["ex"], jp, js, msk)
    copies["tw1"].wait()
    wait_for(land1, 8, sems.at[1])
    columns(land1, w1, ref["tw1"], send2)
    exchange(me, dm, send2, land2, 0, 16, 16, (sems.at[2], sems.at[3]))
    for name in ("wah", "wal", "tw2", "vbh", "vbl", "e"):
        copies[name].wait()
    for h in range(1, HARM + 1):
        copies["p%d" % h].wait()
    wait_for(land2, 16, sems.at[3])
    local_fft(land2, ref["wah"], ref["wal"], ref["tw2"], ref["vbh"], ref["vbl"], zn, levels)
    pack_ends(zn, levels, send3)

    def give(n):
        row, rows, first, last = CHUNKS[n]
        for h in ORDER:
            if first <= FIRST[h] < last:
                pack_harmonic(h, zn, ref["p%d" % h], send3)
        exchange(me, dm, send3, land3, row, rows, ROWS, (sems.at[4 + 2 * n], sems.at[5 + 2 * n]))

    def take(n):
        _, rows, first, last = CHUNKS[n]
        wait_for(land3, rows, sems.at[5 + 2 * n])
        if n == 0:
            unpack_ends(land3, ends, levels)
        unpack(land3, ends, first, last, side, xl, xl8)
        correlate(first, last, xl, xl8, taps, taps8, msk, pm)

    for act, n in SCHEDULE:
        (give if act else take)(n)
    add_harmonics(pm, ref["e"], levels, out)
    wait_for(land1, 8, sems.at[0])
    wait_for(land2, 16, sems.at[2])
    for n, (_, rows, _, _) in enumerate(CHUNKS):
        wait_for(land3, rows, sems.at[4 + 2 * n])


SCHEDULE = ((1, 0), (1, 1), (0, 0), (1, 2), (0, 1), (0, 2))
CONSTANTS = ("ex", "tw1", "wah", "wal", "tw2", "vbh", "vbl") + tuple(
    "p%d" % h for h in range(1, HARM + 1)
) + ("e",)


def constants():
    w1, tw1, wah, wal, tw2, vbh, vbl = fft_tables()
    e, ex, jp = select_tables()
    return [ex, tw1, wah, wal, tw2, vbh, vbl, *perm_tables(), e], jp, w1


def search(series, coef, offset, jit):
    held, jp, w1 = constants()
    whole = pl.BlockSpec(memory_space=pltpu.VMEM)
    far = pl.BlockSpec(memory_space=pl.ANY)
    return pl.pallas_call(
        search_kernel,
        out_shape=jax.ShapeDtypeStruct((TMPL * 64, 128), F32),
        in_specs=[far] + [whole] * 4 + [far] * (1 + len(held)),
        out_specs=whole,
        scratch_shapes=[pltpu.VMEM(c.shape, c.dtype) for c in held]
        + [
            pltpu.VMEM((1024, 128), F32),
            pltpu.VMEM((128, D), F32),
            pltpu.VMEM((512, 128), jnp.int32),
            pltpu.VMEM((512, 128), jnp.int32),
            pltpu.VMEM((1024, 128), jnp.int32),
            pltpu.VMEM((1024, 128), jnp.int32),
            pltpu.VMEM((2, 528, 128), F32),
            pltpu.VMEM((24, 128), F32),
            pltpu.VMEM((D * ROWS, 128), jnp.int32),
            pltpu.VMEM((D * ROWS, 128), jnp.int32),
            pltpu.VMEM((24, 128), F32),
            pltpu.VMEM((152, 128), F32),
            pltpu.VMEM((NB * 128, 384), BF16),
            pltpu.VMEM((NB * 128, 768), F8),
            pltpu.VMEM((NB, 1024, 128), BF16),
            pltpu.VMEM((512, 128), F32),
            pltpu.VMEM((NB * 128, 128), F32),
            pltpu.VMEM((TMPL, 8, 128), F32),
            pltpu.VMEM((TMPL // 2, 384, 256), BF16),
            pltpu.VMEM((TMPL // 2, 768, 256), F8),
            pltpu.SemaphoreType.DMA((len(held) + 2,)),
            pltpu.SemaphoreType.DMA((4 + 2 * len(CHUNKS),)),
        ],
        compiler_params=pltpu.CompilerParams(
            collective_id=0, has_side_effects=True, vmem_limit_bytes=62 * 1024 * 1024
        ),
        cost_estimate=pl.CostEstimate(flops=3 * 10**10, bytes_accessed=3 * 10**7, transcendentals=0),
    )(series, coef, offset, jit, jp, w1, *held)


def shards(series, tap_coef, tap_offset, harm_index):
    out = search(series.reshape(1024, 128), tap_coef.reshape(32, 128), tap_offset, harm_index)
    return out.reshape(2, 64, 8, 128).transpose(0, 2, 1, 3).reshape(TMPL, 8192)


def solution(mesh):
    return jax.shard_map(
        shards,
        mesh=mesh,
        in_specs=(P(("dm", "bin")), P(), P(), P(None, "bin")),
        out_specs=P(None, ("dm", "bin")),
        check_vma=False,
    )
```

```python
import functools
import math

import jax
import jax.numpy as jnp
import numpy as np
from jax import lax
from jax.experimental import pallas as pl
from jax.experimental.pallas import tpu as pltpu
from jax.sharding import PartitionSpec as P

D = 64
TMPL = 16
TAPS = 128
HARM = 8
LENGTH = 8388608
LOCAL = LENGTH // D
ALPHA = 512
BETA = 256
ORDER = (4, 8, 7, 1, 6, 2, 5, 3)
BLOCKS = tuple((h, r) for h in ORDER for r in range(h))
NB = len(BLOCKS)
FIRST = {h: BLOCKS.index((h, 0)) for h in ORDER}
ROWS = 40
CHUNKS = ((0, 8, 0, 4), (8, 8, 4, 12), (16, 8, 12, 20), (24, 16, 20, 36))
FULL = 32767.0
SAMPLE_BOUND = 6.0
PART_BOUND = SAMPLE_BOUND * D / math.sqrt(LENGTH)
F32 = jnp.float32
BF16 = jnp.bfloat16
F8 = jnp.float8_e4m3fn
LOW = 512.0


def np_split(x):
    x = np.asarray(x, np.float32)
    hi = x.astype(jnp.bfloat16)
    lo = (x - hi.astype(np.float32)).astype(jnp.bfloat16)
    return hi, lo


@functools.lru_cache(None)
def fft_tables():
    k1 = np.arange(D)[:, None]
    m = np.arange(LOCAL // D)[None, :]
    ang = -2 * np.pi * (k1 * m) / LENGTH
    tw1 = np.stack([np.cos(ang), np.sin(ang)]).astype(np.float32)
    k = np.arange(ALPHA)[:, None] * np.arange(ALPHA)[None, :] % ALPHA
    ang = -2 * np.pi * k / ALPHA
    c, s = np.cos(ang), np.sin(ang)
    wa = np.block([[c, -s], [s, c]])
    ang = -2 * np.pi * (np.arange(ALPHA)[:, None] * np.arange(BETA)[None, :]) / LOCAL
    tw2 = np.stack([np.cos(ang), np.sin(ang)]).astype(np.float32)
    half = BETA // 2
    ang = -2 * np.pi * (np.arange(BETA)[:, None] * np.arange(half)[None, :] % BETA) / BETA
    c, s = np.cos(ang), np.sin(ang)
    vb = np.block([[c, s], [-s, c]])
    k = k1 * (D * np.arange(D)[None, None, :] + np.arange(D)[:, None, None]) % (D * D)
    ang = -2 * np.pi * k / (D * D)
    w1 = np.concatenate([np.cos(ang), np.sin(ang)], axis=1) / math.sqrt(LENGTH)
    return w1.astype(np.float32), tw1, *np_split(wa), tw2, *np_split(vb)


@functools.lru_cache(None)
def perm_tables():
    out = []
    for h in range(1, HARM + 1):
        m = np.zeros((128 * h, 128 * h), np.float32)
        a = np.arange(128)
        for r in range(h):
            m[h * a + r, 128 * r + 64 * (a % 2) + a // 2] = 1
        out.append(m.astype(jnp.bfloat16))
    return tuple(out)


@functools.lru_cache(None)
def select_tables():
    i = np.arange(64)
    e = np.zeros((NB, 128, 128), np.float32)
    ex = np.zeros((NB, 128, 128), np.float32)
    jp = np.zeros((NB, 1, 128), np.float32)
    for n, (h, r) in enumerate(BLOCKS):
        b, j = np.divmod(64 * r + i, h)
        for t in range(2):
            e[n, 64 * t + i, 64 * t + b] = 1
            ex[n, b, 64 * t + i] = 1
            jp[n, 0, 64 * t + i] = j
    return e.astype(jnp.bfloat16), ex.astype(jnp.bfloat16), jp.reshape(NB, 128)


def split(x):
    hi = x.astype(BF16)
    return hi, (x - hi.astype(F32)).astype(BF16)


def dot(a, b):
    return jnp.dot(a, b, preferred_element_type=F32)


def dot3(ah, al, bh, bl):
    return dot(ah, bh) + dot(ah, bl) + dot(al, bh)


def encode(x, bound):
    size = jnp.sqrt(jnp.sqrt(jnp.abs(x) * (1.0 / bound)))
    code = jnp.minimum(size * FULL + 0.5, FULL).astype(jnp.int32)
    return jnp.where(x < 0, -code, code)


def decode(code, bound):
    x = code.astype(F32)
    return x * jnp.abs(x) * (x * x * (bound / FULL**4))


def join(high, low):
    return (high << 16) | (low & 0xFFFF)


def parted(word):
    return word >> 16, (word << 16) >> 16


def for_partners(me, act):
    far = (2, 1, 3, 0)
    x = [(me // 16 + k) % 4 * 16 for k in far]
    y = [(me // 4 + k) % 4 * 4 for k in far]
    z = [(me + k) % 4 for k in far]
    plane = [b + c for b in y for c in z][:-1]

    def row(i, carry):
        first = (me // 16 + 2 + i) % 4 * 16
        for v in plane:
            act(first + v)
        return carry

    lax.fori_loop(0, 4, row, 0)
    for v in x[:-1]:
        act(v + y[-1] + z[-1])


def exchange(me, dm, src, dst, first, rows, pitch, sems):
    target = dst.at[pl.ds(pl.multiple_of(me * pitch + first, 8), rows)]

    def start(to):
        pltpu.make_async_remote_copy(
            src_ref=src.at[pl.ds(pl.multiple_of(to * pitch + first, 8), rows)],
            dst_ref=target,
            send_sem=sems[0],
            recv_sem=sems[1],
            device_id=(dm, to),
            device_id_type=pl.DeviceIdType.MESH,
        ).start()

    for_partners(me, start)
    own = pl.ds(pl.multiple_of(me * pitch + first, 8), rows)
    dst[own, :] = src[own, :]


def wait_for(ref, rows, sem):
    part = ref.at[pl.ds(0, (D - 1) * rows)]
    pltpu.make_async_copy(part, part, sem).wait()


def make_taps(vx, taps, taps8):
    lane = lax.broadcasted_iota(jnp.int32, (64, 128), 1)

    def pair(tp, carry):
        for x in range(3):
            both = []
            for z in range(2):
                rolled = []
                for t in range(2):
                    row = vx[2 * tp + t, 3 * z + x : 3 * z + x + 1, :]
                    rolled.append(
                        pltpu.roll(jnp.broadcast_to(row, (64, 128)), 64 * t, 1, stride=1, stride_axis=0)
                    )
                v = jnp.where(lane < 64, rolled[0], rolled[1])
                high = v.astype(BF16).astype(F32)
                both.append((high, (v - high) * LOW))

            def put(ref, row, kind, tr, ti):
                ref[tp, row : row + 64, 0:128] = tr.astype(kind)
                ref[tp, row : row + 64, 128:256] = ti.astype(kind)
                ref[tp, row + 64 : row + 128, 0:128] = (-ti).astype(kind)
                ref[tp, row + 64 : row + 128, 128:256] = tr.astype(kind)

            (rh, rl), (ih, il) = both
            put(taps, 128 * x, BF16, rh * LOW, ih * LOW)
            put(taps8, 128 * x, F8, rl, il)
            put(taps8, 384 + 128 * x, F8, rh, ih)
        return carry

    lax.fori_loop(0, TMPL // 2, pair, 0)


def level_of(x):
    return jnp.ceil(jnp.log2(jnp.maximum(jnp.max(jnp.abs(x), keepdims=True), 1e-30)))


def make_tap_rows(coef, offset, vx, levels):
    lane = lax.broadcasted_iota(jnp.int32, (128, 384), 1)
    m = lane % 128
    lag = lane // 128 * 64 - jnp.where(m < 64, m, m - 128)
    lag = jnp.where(m == 64, -1, lag).astype(F32)
    where = jnp.concatenate([offset[...].astype(F32), jnp.zeros((112, 128), F32)], axis=0).T
    level = level_of(coef[...])
    factor = jnp.exp2(8.0 - level)
    levels[0:8, :] = jnp.broadcast_to(level, (8, 128))
    first = coef[...].astype(BF16)
    rest = coef[...] - first.astype(F32)
    second = rest.astype(BF16)
    third = (rest - second.astype(F32)).astype(BF16)
    lhs = jnp.concatenate([first, second, third], axis=0)
    for t in range(TMPL):
        onehot = jnp.where(where[:, t : t + 1] == lag, 1.0, 0.0).astype(BF16)
        rows = dot(lhs, onehot)
        rows = (rows[0:32] + rows[32:64] + rows[64:96]) * factor
        for z in range(2):
            for x in range(3):
                vx[t, 3 * z + x : 3 * z + x + 1, :] = rows[16 * z + t : 16 * z + t + 1, 128 * x : 128 * x + 128]


def code_samples(series, out):
    v = series[...].reshape(D, 16, 128)
    word = join(encode(v[:, :8], SAMPLE_BOUND), encode(v[:, 8:], SAMPLE_BOUND))
    out[...] = word.reshape(512, 128)


def columns(xs, w1, tw, out):
    pairs = [parted(xs[pl.ds(m, D, stride=8), :]) for m in range(8)]
    x = jnp.concatenate([p[0] for p in pairs] + [p[1] for p in pairs], axis=1)
    y = dot3(*split(w1[...]), *split(decode(x, SAMPLE_BOUND)))
    yr, yi = y[:D], y[D:]
    zr = yr * tw[0] - yi * tw[1]
    zi = yr * tw[1] + yi * tw[0]
    word = join(encode(zr, PART_BOUND), encode(zi, PART_BOUND))
    for m in range(16):
        out[pl.ds((m % 2) * 8 + m // 2, D, stride=16), :] = word[:, 128 * m : 128 * m + 128]


def local_fft(b, wah, wal, tw, vbh, vbl, zn, levels):
    v = b[...].reshape(D, 2, 8, 128)
    word = jnp.concatenate([v[:, n].reshape(ALPHA, 128) for n in range(2)], axis=1)
    rhs = jnp.concatenate([decode(x, PART_BOUND) for x in parted(word)], axis=0)
    y = dot3(wah[...], wal[...], *split(rhs))
    yr, yi = y[:ALPHA], y[ALPHA:]
    t = jnp.concatenate([yr * tw[0] - yi * tw[1], yr * tw[1] + yi * tw[0]], axis=1)
    th, tl = split(t)
    z = dot3(th, tl, vbh[...], vbl[...])
    level = level_of(z)
    levels[16:24, :] = jnp.broadcast_to(level, (8, 128))
    z = jnp.clip(jnp.round(z * (jnp.exp2(-level) * FULL)), -FULL, FULL)
    zero = jnp.zeros((8, 128), F32)
    for c in range(2):
        zt = z[:, 128 * c : 128 * c + 128].T
        zn[c, 0:8, :] = zero
        zn[c, 520:528, :] = zero
        for n in range(4):
            zn[c, pl.ds(8 + n, 128, stride=4), :] = zt[:, 128 * n : 128 * n + 128]


def pack_ends(zn, levels, out):
    lane = lax.broadcasted_iota(jnp.int32, (D, 128), 1)
    ends = jnp.broadcast_to(levels[16:17, :], (D, 128)).astype(jnp.int32)
    for h in range(1, HARM + 1):
        left = [zn[c, pl.ds(7, D, stride=h), :].astype(jnp.int32) for c in range(2)]
        right = [zn[c, pl.ds(8 + h, D, stride=h), :].astype(jnp.int32) for c in range(2)]
        ends = jnp.where(lane == h - 1, join(*left)[:, 127:128], ends)
        ends = jnp.where(lane == 8 + h - 1, join(*right)[:, 0:1], ends)
    out[pl.ds(0, D, stride=ROWS), :] = ends
    for n in range(1, 4):
        out[pl.ds(n, D, stride=ROWS), :] = jnp.zeros((D, 128), jnp.int32)


def pack_harmonic(h, zn, perm, out):
    src = jnp.concatenate(
        [
            jnp.concatenate([zn[c, pl.ds(8 + n, D, stride=h), :] for n in range(h)], axis=1)
            for c in range(2)
        ],
        axis=0,
    )
    hi, lo = split(src)
    moved = dot(jnp.concatenate([hi, lo], axis=0), perm[...])
    moved = (moved[:128] + moved[128:]).astype(jnp.int32)
    word = join(moved[:64], moved[64:])
    for r in range(h):
        out[pl.ds(4 + FIRST[h] + r, D, stride=ROWS), :] = word[:, 128 * r : 128 * r + 128]


def unpack_ends(land, ends, levels):
    lane = lax.broadcasted_iota(jnp.int32, (8, 128), 1)
    word = land[pl.ds(0, D, stride=ROWS), :]
    re, im = parted(word)
    zero = jnp.zeros((D, 128), F32)
    re, im, word = [jnp.concatenate([v.astype(F32), zero], axis=0).T for v in (re, im, word)]
    level = jnp.where(lane < 64, word[16:24], -1000.0)
    top = jnp.max(level[0:1], axis=1, keepdims=True)
    levels[8:16, :] = jnp.broadcast_to(top, (8, 128))
    scale = jnp.exp2(level - top + 8.0) * (1.0 / FULL)
    scale = jnp.where(lane < 64, scale, pltpu.roll(scale, 64, 1))
    scale = jnp.broadcast_to(scale[0:1], (8, 128))
    for n in range(2):
        part = slice(8 * n, 8 * n + 8)
        ends[part, :] = jnp.where(lane < 64, re[part], pltpu.roll(im[part], 64, 1)) * scale
    ends[16:24, :] = scale


def unpack(land, ends, first, last, side, xl, xl8):
    def put(n, slot, x):
        high = x.astype(BF16)
        wide = high.astype(F32)
        parts = (high, wide.astype(F8), ((x - wide) * LOW).astype(F8))
        return put_parts(n, slot, parts)

    def put_parts(n, slot, parts):
        xl[pl.ds(128 * n, 128), pl.ds(128 * slot, 128)] = parts[0]
        xl8[pl.ds(128 * n, 128), pl.ds(128 * slot, 128)] = parts[1]
        xl8[pl.ds(128 * n, 128), pl.ds(384 + 128 * slot, 128)] = parts[2]
        return parts

    for n in range(first, last):
        h, r = BLOCKS[n]
        re, im = parted(land[pl.ds(4 + n, D, stride=ROWS), :])
        block = jnp.concatenate([re.astype(F32), im.astype(F32)], axis=0).T * ends[16:17, :]
        parts = put(n, 1, block)
        if r > 0:
            put_parts(n - 1, 2, parts)
        if r < h - 1:
            put_parts(n + 1, 0, parts)
        if r == h - 1:
            side[7:8, :] = ends[h - 1 : h, :]
            side[8:72, :] = block[64:]
            put(n - h + 1, 0, jnp.concatenate([side[7:71, :], block[:64]], axis=0))
        if r == 0:
            side[80:144, :] = block[:64]
            side[144:145, :] = ends[h + 7 : h + 8, :]
            put(n + h - 1, 2, jnp.concatenate([block[64:], side[81:145, :]], axis=0))


def make_masks(jit, ex, jp, js, msk):
    for g in range(64):
        js[8 * g : 8 * g + 8, :] = jit[:, 128 * g : 128 * g + 128].astype(F32)
    for h in range(1, HARM + 1):
        even = js[pl.ds(h - 1, 64, stride=8), :]
        lhs = jnp.concatenate([even, pltpu.roll(even, 64, 1)], axis=0).astype(BF16)
        for n in range(FIRST[h], FIRST[h] + h):
            msk[pl.ds(128 * n, 128), :] = jnp.where(dot(lhs, ex[n]) == jp[n : n + 1, :], 1.0, 0.0)


def correlate(first, last, xl, xl8, taps, taps8, msk, pm):
    groups = range(first // 4, last // 4)
    pairs = max(1, 8 // len(groups))

    def one(tp):
        for g in groups:
            rows = pl.ds(512 * g, 512)
            acc = dot(xl[rows, :], taps[tp]) + dot(xl8[rows, :], taps8[tp])
            re, im = acc[:, :128], acc[:, 128:]
            kept = jnp.where(msk[rows, :] > 0.5, re * re + im * im, 0.0).astype(BF16)
            for q in range(4):
                pm[4 * g + q, pl.ds(pl.multiple_of(128 * tp, 128), 128), :] = kept[128 * q : 128 * q + 128]

    def several(step, carry):
        for k in range(pairs):
            one(pairs * step + k)
        return carry

    lax.fori_loop(0, TMPL // 2 // pairs, several, 0)


def add_harmonics(pm, e, levels, out):
    factor = jnp.exp2(2.0 * (levels[0:1, :] + levels[8:9, :] - 25.0)) * (1.0 / HARM)
    lane = lax.broadcasted_iota(jnp.int32, (64, 128), 1)
    for tp in range(TMPL // 4):
        rows = pl.ds(256 * tp, 256)
        total = jnp.zeros((256, 128), F32)
        for n in range(0, NB, 2):
            total += dot(
                jnp.concatenate([pm[n, rows, :], pm[n + 1, rows, :]], axis=1),
                jnp.concatenate([e[n], e[n + 1]], axis=0),
            )
        total = total * factor
        for q in range(2):
            even = total[128 * q : 128 * q + 64]
            odd = total[128 * q + 64 : 128 * q + 128]
            t = 4 * tp + 2 * q
            row = t // 8 * 512 + t % 8
            out[pl.ds(row, 64, stride=8), :] = jnp.where(lane < 64, even, pltpu.roll(odd, 64, 1))
            out[pl.ds(row + 1, 64, stride=8), :] = jnp.where(lane < 64, pltpu.roll(even, 64, 1), odd)


def search_kernel(*refs):
    series, coef, offset, jit, jp, w1_all = refs[:6]
    count = len(CONSTANTS)
    held = refs[6 : 6 + count]
    out = refs[6 + count]
    rest = refs[7 + count :]
    local, rest = rest[:count], rest[count:]
    xs, w1, send1, land1, send2, land2, zn, levels, send3, land3, ends, side = rest[:12]
    xl, xl8, pm, js, msk, vx, taps, taps8, const_sem, sems = rest[12:]
    me, dm = lax.axis_index("bin"), lax.axis_index("dm")
    own = [
        pltpu.make_async_copy(series, xs, const_sem.at[count]),
        pltpu.make_async_copy(w1_all.at[me], w1, const_sem.at[count + 1]),
    ]
    copies = {
        name: pltpu.make_async_copy(held[n], local[n], const_sem.at[n])
        for n, name in enumerate(CONSTANTS)
    }
    ref = dict(zip(CONSTANTS, local))
    for copy in own:
        copy.start()

    barrier = pltpu.get_barrier_semaphore()

    def greet(to):
        pl.semaphore_signal(barrier, inc=1, device_id=(dm, to), device_id_type=pl.DeviceIdType.MESH)

    for_partners(me, greet)
    for copy in copies.values():
        copy.start()
    for copy in own:
        copy.wait()
    code_samples(xs, send1)
    pl.semaphore_wait(barrier, D - 1)

    exchange(me, dm, send1, land1, 0, 8, 8, (sems.at[0], sems.at[1]))
    make_tap_rows(coef, offset, vx, levels)
    make_taps(vx, taps, taps8)
    copies["ex"].wait()
    make_masks(jit, ref["ex"], jp, js, msk)
    copies["tw1"].wait()
    wait_for(land1, 8, sems.at[1])
    columns(land1, w1, ref["tw1"], send2)
    exchange(me, dm, send2, land2, 0, 16, 16, (sems.at[2], sems.at[3]))
    for name in ("wah", "wal", "tw2", "vbh", "vbl", "e"):
        copies[name].wait()
    for h in range(1, HARM + 1):
        copies["p%d" % h].wait()
    wait_for(land2, 16, sems.at[3])
    local_fft(land2, ref["wah"], ref["wal"], ref["tw2"], ref["vbh"], ref["vbl"], zn, levels)
    pack_ends(zn, levels, send3)

    def give(n):
        row, rows, first, last = CHUNKS[n]
        for h in ORDER:
            if first <= FIRST[h] < last:
                pack_harmonic(h, zn, ref["p%d" % h], send3)
        exchange(me, dm, send3, land3, row, rows, ROWS, (sems.at[4 + 2 * n], sems.at[5 + 2 * n]))

    def take(n):
        _, rows, first, last = CHUNKS[n]
        wait_for(land3, rows, sems.at[5 + 2 * n])
        if n == 0:
            unpack_ends(land3, ends, levels)
        unpack(land3, ends, first, last, side, xl, xl8)
        correlate(first, last, xl, xl8, taps, taps8, msk, pm)

    for act, n in SCHEDULE:
        (give if act else take)(n)
    add_harmonics(pm, ref["e"], levels, out)
    wait_for(land1, 8, sems.at[0])
    wait_for(land2, 16, sems.at[2])
    for n, (_, rows, _, _) in enumerate(CHUNKS):
        wait_for(land3, rows, sems.at[4 + 2 * n])


SCHEDULE = ((1, 0), (1, 1), (1, 2), (0, 0), (1, 3), (0, 1), (0, 2), (0, 3))
CONSTANTS = ("ex", "tw1", "wah", "wal", "tw2", "vbh", "vbl") + tuple(
    "p%d" % h for h in range(1, HARM + 1)
) + ("e",)


def constants():
    w1, tw1, wah, wal, tw2, vbh, vbl = fft_tables()
    e, ex, jp = select_tables()
    return [ex, tw1, wah, wal, tw2, vbh, vbl, *perm_tables(), e], jp, w1


def search(series, coef, offset, jit):
    held, jp, w1 = constants()
    whole = pl.BlockSpec(memory_space=pltpu.VMEM)
    far = pl.BlockSpec(memory_space=pl.ANY)
    return pl.pallas_call(
        search_kernel,
        out_shape=pltpu.VMEM((TMPL * 64, 128), F32),
        in_specs=[far] + [whole] * 4 + [far] * (1 + len(held)),
        out_specs=whole,
        scratch_shapes=[pltpu.VMEM(c.shape, c.dtype) for c in held]
        + [
            pltpu.VMEM((1024, 128), F32),
            pltpu.VMEM((128, D), F32),
            pltpu.VMEM((512, 128), jnp.int32),
            pltpu.VMEM((512, 128), jnp.int32),
            pltpu.VMEM((1024, 128), jnp.int32),
            pltpu.VMEM((1024, 128), jnp.int32),
            pltpu.VMEM((2, 528, 128), F32),
            pltpu.VMEM((24, 128), F32),
            pltpu.VMEM((D * ROWS, 128), jnp.int32),
            pltpu.VMEM((D * ROWS, 128), jnp.int32),
            pltpu.VMEM((24, 128), F32),
            pltpu.VMEM((152, 128), F32),
            pltpu.VMEM((NB * 128, 384), BF16),
            pltpu.VMEM((NB * 128, 768), F8),
            pltpu.VMEM((NB, 1024, 128), BF16),
            pltpu.VMEM((512, 128), F32),
            pltpu.VMEM((NB * 128, 128), F32),
            pltpu.VMEM((TMPL, 8, 128), F32),
            pltpu.VMEM((TMPL // 2, 384, 256), BF16),
            pltpu.VMEM((TMPL // 2, 768, 256), F8),
            pltpu.SemaphoreType.DMA((len(held) + 2,)),
            pltpu.SemaphoreType.DMA((4 + 2 * len(CHUNKS),)),
        ],
        compiler_params=pltpu.CompilerParams(
            collective_id=0, has_side_effects=True, vmem_limit_bytes=62 * 1024 * 1024
        ),
        cost_estimate=pl.CostEstimate(flops=3 * 10**10, bytes_accessed=3 * 10**7, transcendentals=0),
    )(series, coef, offset, jit, jp, w1, *held)


def shards(series, tap_coef, tap_offset, harm_index):
    out = search(series.reshape(1024, 128), tap_coef.reshape(32, 128), tap_offset, harm_index)
    return out.reshape(2, 64, 8, 128).transpose(0, 2, 1, 3).reshape(TMPL, 8192)


def solution(mesh):
    return jax.shard_map(
        shards,
        mesh=mesh,
        in_specs=(P(("dm", "bin")), P(), P(), P(None, "bin")),
        out_specs=P(None, ("dm", "bin")),
        check_vma=False,
    )
```

```python
import functools
import math

import jax
import jax.numpy as jnp
import numpy as np
from jax import lax
from jax.experimental import pallas as pl
from jax.experimental.pallas import tpu as pltpu
from jax.sharding import PartitionSpec as P

D = 64
TMPL = 16
TAPS = 128
HARM = 8
LENGTH = 8388608
LOCAL = LENGTH // D
ALPHA = 512
BETA = 256
ORDER = (4, 8, 7, 1, 6, 2, 5, 3)
BLOCKS = tuple((h, r) for h in ORDER for r in range(h))
NB = len(BLOCKS)
FIRST = {h: BLOCKS.index((h, 0)) for h in ORDER}
ROWS = 40
CHUNKS = ((0, 8, 0, 4), (8, 8, 4, 12), (16, 8, 12, 20), (24, 16, 20, 36))
FULL = 32767.0
FAR = (2, 1, 3, 0)
SAMPLE_BOUND = 6.0
PART_BOUND = SAMPLE_BOUND * D / math.sqrt(LENGTH)
F32 = jnp.float32
BF16 = jnp.bfloat16
F8 = jnp.float8_e4m3fn
LOW = 512.0


def np_split(x):
    x = np.asarray(x, np.float32)
    hi = x.astype(jnp.bfloat16)
    lo = (x - hi.astype(np.float32)).astype(jnp.bfloat16)
    return hi, lo


@functools.lru_cache(None)
def fft_tables():
    k1 = np.arange(D)[:, None]
    m = np.arange(LOCAL // D)[None, :]
    ang = -2 * np.pi * (k1 * m) / LENGTH
    tw1 = np.stack([np.cos(ang), np.sin(ang)]).astype(np.float32)
    k = np.arange(ALPHA)[:, None] * np.arange(ALPHA)[None, :] % ALPHA
    ang = -2 * np.pi * k / ALPHA
    c, s = np.cos(ang), np.sin(ang)
    wa = np.block([[c, -s], [s, c]])
    ang = -2 * np.pi * (np.arange(ALPHA)[:, None] * np.arange(BETA)[None, :]) / LOCAL
    tw2 = np.stack([np.cos(ang), np.sin(ang)]).astype(np.float32)
    half = BETA // 2
    ang = -2 * np.pi * (np.arange(BETA)[:, None] * np.arange(half)[None, :] % BETA) / BETA
    c, s = np.cos(ang), np.sin(ang)
    vb = np.block([[c, s], [-s, c]])
    k = k1 * (D * np.arange(D)[None, None, :] + np.arange(D)[:, None, None]) % (D * D)
    ang = -2 * np.pi * k / (D * D)
    w1 = np.stack([np.cos(ang), np.sin(ang)], axis=1) / math.sqrt(LENGTH)
    w1 = w1.reshape(D, 2, 4, 16, D)
    w1 = np.stack([w1[e][:, [(e // 16 + f) % 4 for f in FAR]] for e in range(D)]).reshape(D, 2 * D, D)
    wa = wa.reshape(2 * ALPHA, 2, 4, 128).transpose(2, 0, 1, 3).reshape(4, 2 * ALPHA, 256)
    return w1.astype(np.float32), tw1, *np_split(wa), tw2, *np_split(vb)


@functools.lru_cache(None)
def perm_tables():
    out = []
    for h in range(1, HARM + 1):
        m = np.zeros((128 * h, 128 * h), np.float32)
        a = np.arange(128)
        for r in range(h):
            m[h * a + r, 128 * r + 64 * (a % 2) + a // 2] = 1
        out.append(m.astype(jnp.bfloat16))
    return tuple(out)


@functools.lru_cache(None)
def select_tables():
    i = np.arange(64)
    e = np.zeros((NB, 128, 128), np.float32)
    ex = np.zeros((NB, 128, 128), np.float32)
    jp = np.zeros((NB, 1, 128), np.float32)
    for n, (h, r) in enumerate(BLOCKS):
        b, j = np.divmod(64 * r + i, h)
        for t in range(2):
            e[n, 64 * t + i, 64 * t + b] = 1
            ex[n, b, 64 * t + i] = 1
            jp[n, 0, 64 * t + i] = j
    return e.astype(jnp.bfloat16), ex.astype(jnp.bfloat16), jp.reshape(NB, 128)


def split(x):
    hi = x.astype(BF16)
    return hi, (x - hi.astype(F32)).astype(BF16)


def dot(a, b):
    return jnp.dot(a, b, preferred_element_type=F32)


def dot3(ah, al, bh, bl):
    return dot(ah, bh) + dot(ah, bl) + dot(al, bh)


def encode(x, bound):
    size = jnp.sqrt(jnp.sqrt(jnp.abs(x) * (1.0 / bound)))
    code = jnp.minimum(size * FULL + 0.5, FULL).astype(jnp.int32)
    return jnp.where(x < 0, -code, code)


def decode(code, bound):
    x = code.astype(F32)
    return x * jnp.abs(x) * (x * x * (bound / FULL**4))


def join(high, low):
    return (high << 16) | (low & 0xFFFF)


def parted(word):
    return word >> 16, (word << 16) >> 16


def for_partners(me, act):
    far = FAR
    x = [(me // 16 + k) % 4 * 16 for k in far]
    y = [(me // 4 + k) % 4 * 4 for k in far]
    z = [(me + k) % 4 for k in far]
    plane = [b + c for b in y for c in z][:-1]

    def row(i, carry):
        first = (me // 16 + 2 + i) % 4 * 16
        for v in plane:
            act(first + v)
        return carry

    lax.fori_loop(0, 4, row, 0)
    for v in x[:-1]:
        act(v + y[-1] + z[-1])


def exchange(me, dm, src, dst, first, rows, pitch, sems):
    target = dst.at[pl.ds(pl.multiple_of(me * pitch + first, 8), rows)]

    def start(to):
        pltpu.make_async_remote_copy(
            src_ref=src.at[pl.ds(pl.multiple_of(to * pitch + first, 8), rows)],
            dst_ref=target,
            send_sem=sems[0],
            recv_sem=sems[1],
            device_id=(dm, to),
            device_id_type=pl.DeviceIdType.MESH,
        ).start()

    for_partners(me, start)
    own = pl.ds(pl.multiple_of(me * pitch + first, 8), rows)
    dst[own, :] = src[own, :]


def wait_for(ref, rows, sem):
    part = ref.at[pl.ds(0, (D - 1) * rows)]
    pltpu.make_async_copy(part, part, sem).wait()


def make_taps(vx, taps, taps8):
    lane = lax.broadcasted_iota(jnp.int32, (64, 128), 1)

    def pair(tp, carry):
        for x in range(3):
            both = []
            for z in range(2):
                rolled = []
                for t in range(2):
                    row = vx[2 * tp + t, 3 * z + x : 3 * z + x + 1, :]
                    rolled.append(
                        pltpu.roll(jnp.broadcast_to(row, (64, 128)), 64 * t, 1, stride=1, stride_axis=0)
                    )
                v = jnp.where(lane < 64, rolled[0], rolled[1])
                high = v.astype(BF16).astype(F32)
                both.append((high, (v - high) * LOW))

            def put(ref, row, kind, tr, ti):
                ref[tp, row : row + 64, 0:128] = tr.astype(kind)
                ref[tp, row : row + 64, 128:256] = ti.astype(kind)
                ref[tp, row + 64 : row + 128, 0:128] = (-ti).astype(kind)
                ref[tp, row + 64 : row + 128, 128:256] = tr.astype(kind)

            (rh, rl), (ih, il) = both
            put(taps, 128 * x, BF16, rh * LOW, ih * LOW)
            put(taps8, 128 * x, F8, rl, il)
            put(taps8, 384 + 128 * x, F8, rh, ih)
        return carry

    lax.fori_loop(0, TMPL // 2, pair, 0)


def level_of(x):
    return jnp.ceil(jnp.log2(jnp.maximum(jnp.max(jnp.abs(x), keepdims=True), 1e-30)))


def make_tap_rows(coef, offset, vx, levels):
    lane = lax.broadcasted_iota(jnp.int32, (128, 384), 1)
    m = lane % 128
    lag = lane // 128 * 64 - jnp.where(m < 64, m, m - 128)
    lag = jnp.where(m == 64, -1, lag).astype(F32)
    where = jnp.concatenate([offset[...].astype(F32), jnp.zeros((112, 128), F32)], axis=0).T
    level = level_of(coef[...])
    factor = jnp.exp2(8.0 - level)
    levels[0:8, :] = jnp.broadcast_to(level, (8, 128))
    first = coef[...].astype(BF16)
    rest = coef[...] - first.astype(F32)
    second = rest.astype(BF16)
    third = (rest - second.astype(F32)).astype(BF16)
    lhs = jnp.concatenate([first, second, third], axis=0)
    for t in range(TMPL):
        onehot = jnp.where(where[:, t : t + 1] == lag, 1.0, 0.0).astype(BF16)
        rows = dot(lhs, onehot)
        rows = (rows[0:32] + rows[32:64] + rows[64:96]) * factor
        for z in range(2):
            for x in range(3):
                vx[t, 3 * z + x : 3 * z + x + 1, :] = rows[16 * z + t : 16 * z + t + 1, 128 * x : 128 * x + 128]


def code_samples(series, out):
    v = series[...].reshape(D, 16, 128)
    word = join(encode(v[:, :8], SAMPLE_BOUND), encode(v[:, 8:], SAMPLE_BOUND))
    out[...] = word.reshape(512, 128)


def columns(xs, w1, tw, out, me, send):
    pairs = [parted(xs[pl.ds(m, D, stride=8), :]) for m in range(8)]
    x = jnp.concatenate([p[0] for p in pairs] + [p[1] for p in pairs], axis=1)
    y = dot3(*split(w1[...]), *split(decode(x, SAMPLE_BOUND)))
    for j, far in enumerate(FAR):
        plane = (me // 16 + far) % 4
        rows = pl.ds(pl.multiple_of(16 * plane, 16), 16)
        yr, yi = y[16 * j : 16 * j + 16], y[D + 16 * j : D + 16 * j + 16]
        tr, ti = tw[0, rows, :], tw[1, rows, :]
        word = join(encode(yr * tr - yi * ti, PART_BOUND), encode(yr * ti + yi * tr, PART_BOUND))
        for m in range(16):
            out[pl.ds(256 * j + (m % 2) * 8 + m // 2, 16, stride=16), :] = word[:, 128 * m : 128 * m + 128]
        send(j, plane)


def local_fft(me, arrived, b, wah, wal, tw, vbh, vbl, yacc, zn, levels):
    for j, far in enumerate(FAR):
        arrived(j)
        plane = (me // 16 + 4 - far) % 4
        v = b[pl.ds(pl.multiple_of(256 * plane, 256), 256), :].reshape(16, 2, 8, 128)
        word = jnp.concatenate([v[:, n].reshape(128, 128) for n in range(2)], axis=1)
        rhs = jnp.concatenate([decode(x, PART_BOUND) for x in parted(word)], axis=0)
        y = dot3(wah[plane], wal[plane], *split(rhs))
        if j > 0:
            y = y + yacc[...]
        if j < 3:
            yacc[...] = y
    yr, yi = y[:ALPHA], y[ALPHA:]
    t = jnp.concatenate([yr * tw[0] - yi * tw[1], yr * tw[1] + yi * tw[0]], axis=1)
    th, tl = split(t)
    z = dot3(th, tl, vbh[...], vbl[...])
    level = level_of(z)
    levels[16:24, :] = jnp.broadcast_to(level, (8, 128))
    z = jnp.clip(jnp.round(z * (jnp.exp2(-level) * FULL)), -FULL, FULL)
    zero = jnp.zeros((8, 128), F32)
    for c in range(2):
        zt = z[:, 128 * c : 128 * c + 128].T
        zn[c, 0:8, :] = zero
        zn[c, 520:528, :] = zero
        for n in range(4):
            zn[c, pl.ds(8 + n, 128, stride=4), :] = zt[:, 128 * n : 128 * n + 128]


def pack_ends(zn, levels, out):
    lane = lax.broadcasted_iota(jnp.int32, (D, 128), 1)
    ends = jnp.broadcast_to(levels[16:17, :], (D, 128)).astype(jnp.int32)
    for h in range(1, HARM + 1):
        left = [zn[c, pl.ds(7, D, stride=h), :].astype(jnp.int32) for c in range(2)]
        right = [zn[c, pl.ds(8 + h, D, stride=h), :].astype(jnp.int32) for c in range(2)]
        ends = jnp.where(lane == h - 1, join(*left)[:, 127:128], ends)
        ends = jnp.where(lane == 8 + h - 1, join(*right)[:, 0:1], ends)
    out[pl.ds(0, D, stride=ROWS), :] = ends
    for n in range(1, 4):
        out[pl.ds(n, D, stride=ROWS), :] = jnp.zeros((D, 128), jnp.int32)


def pack_harmonic(h, zn, perm, out):
    src = jnp.concatenate(
        [
            jnp.concatenate([zn[c, pl.ds(8 + n, D, stride=h), :] for n in range(h)], axis=1)
            for c in range(2)
        ],
        axis=0,
    )
    hi, lo = split(src)
    moved = dot(jnp.concatenate([hi, lo], axis=0), perm[...])
    moved = (moved[:128] + moved[128:]).astype(jnp.int32)
    word = join(moved[:64], moved[64:])
    for r in range(h):
        out[pl.ds(4 + FIRST[h] + r, D, stride=ROWS), :] = word[:, 128 * r : 128 * r + 128]


def unpack_ends(land, ends, levels):
    lane = lax.broadcasted_iota(jnp.int32, (8, 128), 1)
    word = land[pl.ds(0, D, stride=ROWS), :]
    re, im = parted(word)
    zero = jnp.zeros((D, 128), F32)
    re, im, word = [jnp.concatenate([v.astype(F32), zero], axis=0).T for v in (re, im, word)]
    level = jnp.where(lane < 64, word[16:24], -1000.0)
    top = jnp.max(level[0:1], axis=1, keepdims=True)
    levels[8:16, :] = jnp.broadcast_to(top, (8, 128))
    scale = jnp.exp2(level - top + 8.0) * (1.0 / FULL)
    scale = jnp.where(lane < 64, scale, pltpu.roll(scale, 64, 1))
    scale = jnp.broadcast_to(scale[0:1], (8, 128))
    for n in range(2):
        part = slice(8 * n, 8 * n + 8)
        ends[part, :] = jnp.where(lane < 64, re[part], pltpu.roll(im[part], 64, 1)) * scale
    ends[16:24, :] = scale


def unpack(land, ends, first, last, side, xl, xl8):
    def put(n, slot, x):
        high = x.astype(BF16)
        wide = high.astype(F32)
        parts = (high, wide.astype(F8), ((x - wide) * LOW).astype(F8))
        return put_parts(n, slot, parts)

    def put_parts(n, slot, parts):
        xl[pl.ds(128 * n, 128), pl.ds(128 * slot, 128)] = parts[0]
        xl8[pl.ds(128 * n, 128), pl.ds(128 * slot, 128)] = parts[1]
        xl8[pl.ds(128 * n, 128), pl.ds(384 + 128 * slot, 128)] = parts[2]
        return parts

    for n in range(first, last):
        h, r = BLOCKS[n]
        re, im = parted(land[pl.ds(4 + n, D, stride=ROWS), :])
        block = jnp.concatenate([re.astype(F32), im.astype(F32)], axis=0).T * ends[16:17, :]
        parts = put(n, 1, block)
        if r > 0:
            put_parts(n - 1, 2, parts)
        if r < h - 1:
            put_parts(n + 1, 0, parts)
        if r == h - 1:
            side[7:8, :] = ends[h - 1 : h, :]
            side[8:72, :] = block[64:]
            put(n - h + 1, 0, jnp.concatenate([side[7:71, :], block[:64]], axis=0))
        if r == 0:
            side[80:144, :] = block[:64]
            side[144:145, :] = ends[h + 7 : h + 8, :]
            put(n + h - 1, 2, jnp.concatenate([block[64:], side[81:145, :]], axis=0))


def make_masks(jit, ex, jp, js, msk):
    for g in range(64):
        js[8 * g : 8 * g + 8, :] = jit[:, 128 * g : 128 * g + 128].astype(F32)
    for h in range(1, HARM + 1):
        even = js[pl.ds(h - 1, 64, stride=8), :]
        lhs = jnp.concatenate([even, pltpu.roll(even, 64, 1)], axis=0).astype(BF16)
        for n in range(FIRST[h], FIRST[h] + h):
            msk[pl.ds(128 * n, 128), :] = jnp.where(dot(lhs, ex[n]) == jp[n : n + 1, :], 1.0, 0.0)


def correlate(first, last, xl, xl8, taps, taps8, msk, pm):
    groups = range(first // 4, last // 4)
    pairs = max(1, 8 // len(groups))

    def one(tp):
        for g in groups:
            rows = pl.ds(512 * g, 512)
            acc = dot(xl[rows, :], taps[tp]) + dot(xl8[rows, :], taps8[tp])
            re, im = acc[:, :128], acc[:, 128:]
            kept = jnp.where(msk[rows, :] > 0.5, re * re + im * im, 0.0).astype(BF16)
            for q in range(4):
                pm[4 * g + q, pl.ds(pl.multiple_of(128 * tp, 128), 128), :] = kept[128 * q : 128 * q + 128]

    def several(step, carry):
        for k in range(pairs):
            one(pairs * step + k)
        return carry

    lax.fori_loop(0, TMPL // 2 // pairs, several, 0)


def add_harmonics(pm, e, levels, out):
    factor = jnp.exp2(2.0 * (levels[0:1, :] + levels[8:9, :] - 25.0)) * (1.0 / HARM)
    lane = lax.broadcasted_iota(jnp.int32, (64, 128), 1)
    for tp in range(TMPL // 4):
        rows = pl.ds(256 * tp, 256)
        total = jnp.zeros((256, 128), F32)
        for n in range(0, NB, 2):
            total += dot(
                jnp.concatenate([pm[n, rows, :], pm[n + 1, rows, :]], axis=1),
                jnp.concatenate([e[n], e[n + 1]], axis=0),
            )
        total = total * factor
        for q in range(2):
            even = total[128 * q : 128 * q + 64]
            odd = total[128 * q + 64 : 128 * q + 128]
            t = 4 * tp + 2 * q
            row = t // 8 * 512 + t % 8
            out[pl.ds(row, 64, stride=8), :] = jnp.where(lane < 64, even, pltpu.roll(odd, 64, 1))
            out[pl.ds(row + 1, 64, stride=8), :] = jnp.where(lane < 64, pltpu.roll(even, 64, 1), odd)


def search_kernel(*refs):
    series, coef, offset, jit, jp, w1_all = refs[:6]
    count = len(CONSTANTS)
    held = refs[6 : 6 + count]
    out = refs[6 + count]
    rest = refs[7 + count :]
    local, rest = rest[:count], rest[count:]
    xs, w1, send1, land1, send2, land2, yacc, zn, levels, send3, land3, ends, side = rest[:13]
    xl, xl8, pm, js, msk, vx, taps, taps8, const_sem, sems = rest[13:]
    me, dm = lax.axis_index("bin"), lax.axis_index("dm")
    own = [
        pltpu.make_async_copy(series, xs, const_sem.at[count]),
        pltpu.make_async_copy(w1_all.at[me], w1, const_sem.at[count + 1]),
    ]
    copies = {
        name: pltpu.make_async_copy(held[n], local[n], const_sem.at[n])
        for n, name in enumerate(CONSTANTS)
    }
    ref = dict(zip(CONSTANTS, local))
    for copy in own:
        copy.start()

    barrier = pltpu.get_barrier_semaphore()

    def greet(to):
        pl.semaphore_signal(barrier, inc=1, device_id=(dm, to), device_id_type=pl.DeviceIdType.MESH)

    for_partners(me, greet)
    for copy in copies.values():
        copy.start()
    for copy in own:
        copy.wait()
    code_samples(xs, send1)
    pl.semaphore_wait(barrier, D - 1)

    exchange(me, dm, send1, land1, 0, 8, 8, (sems.at[0], sems.at[1]))
    copies["tw1"].wait()
    wait_for(land1, 8, sems.at[1])

    def send(j, plane):
        for y in FAR:
            for z in FAR:
                if FAR[j] or y or z:
                    within = (me // 4 + y) % 4 * 4 + (me + z) % 4
                    pltpu.make_async_remote_copy(
                        src_ref=send2.at[pl.ds(pl.multiple_of(256 * j + 16 * within, 16), 16)],
                        dst_ref=land2.at[pl.ds(pl.multiple_of(16 * me, 16), 16)],
                        send_sem=sems.at[2],
                        recv_sem=sems.at[3 + j],
                        device_id=(dm, 16 * plane + within),
                        device_id_type=pl.DeviceIdType.MESH,
                    ).start()
                else:
                    land2[pl.ds(pl.multiple_of(16 * me, 16), 16), :] = send2[
                        pl.ds(pl.multiple_of(256 * j + 16 * (me % 16), 16), 16), :
                    ]

    columns(land1, w1, ref["tw1"], send2, me, send)
    make_tap_rows(coef, offset, vx, levels)
    make_taps(vx, taps, taps8)
    copies["ex"].wait()
    make_masks(jit, ref["ex"], jp, js, msk)
    for name in ("wah", "wal", "tw2", "vbh", "vbl", "e"):
        copies[name].wait()
    for h in range(1, HARM + 1):
        copies["p%d" % h].wait()

    def arrived(j):
        part = land2.at[pl.ds(0, 16 * (16 if FAR[j] else 15))]
        pltpu.make_async_copy(part, part, sems.at[3 + j]).wait()

    local_fft(
        me, arrived, land2, ref["wah"], ref["wal"], ref["tw2"], ref["vbh"], ref["vbl"], yacc, zn, levels
    )
    pack_ends(zn, levels, send3)

    def give(n):
        row, rows, first, last = CHUNKS[n]
        for h in ORDER:
            if first <= FIRST[h] < last:
                pack_harmonic(h, zn, ref["p%d" % h], send3)
        exchange(me, dm, send3, land3, row, rows, ROWS, (sems.at[7 + 2 * n], sems.at[8 + 2 * n]))

    def take(n):
        _, rows, first, last = CHUNKS[n]
        wait_for(land3, rows, sems.at[8 + 2 * n])
        if n == 0:
            unpack_ends(land3, ends, levels)
        unpack(land3, ends, first, last, side, xl, xl8)
        correlate(first, last, xl, xl8, taps, taps8, msk, pm)

    for act, n in SCHEDULE:
        (give if act else take)(n)
    add_harmonics(pm, ref["e"], levels, out)
    wait_for(land1, 8, sems.at[0])
    wait_for(land2, 16, sems.at[2])
    for n, (_, rows, _, _) in enumerate(CHUNKS):
        wait_for(land3, rows, sems.at[7 + 2 * n])


SCHEDULE = ((1, 0), (1, 1), (1, 2), (0, 0), (1, 3), (0, 1), (0, 2), (0, 3))
CONSTANTS = ("ex", "tw1", "wah", "wal", "tw2", "vbh", "vbl") + tuple(
    "p%d" % h for h in range(1, HARM + 1)
) + ("e",)


def constants():
    w1, tw1, wah, wal, tw2, vbh, vbl = fft_tables()
    e, ex, jp = select_tables()
    return [ex, tw1, wah, wal, tw2, vbh, vbl, *perm_tables(), e], jp, w1


def search(series, coef, offset, jit):
    held, jp, w1 = constants()
    whole = pl.BlockSpec(memory_space=pltpu.VMEM)
    far = pl.BlockSpec(memory_space=pl.ANY)
    return pl.pallas_call(
        search_kernel,
        out_shape=pltpu.VMEM((TMPL * 64, 128), F32),
        in_specs=[far] + [whole] * 4 + [far] * (1 + len(held)),
        out_specs=whole,
        scratch_shapes=[pltpu.VMEM(c.shape, c.dtype) for c in held]
        + [
            pltpu.VMEM((1024, 128), F32),
            pltpu.VMEM((128, D), F32),
            pltpu.VMEM((512, 128), jnp.int32),
            pltpu.VMEM((512, 128), jnp.int32),
            pltpu.VMEM((1024, 128), jnp.int32),
            pltpu.VMEM((1024, 128), jnp.int32),
            pltpu.VMEM((2 * ALPHA, 256), F32),
            pltpu.VMEM((2, 528, 128), F32),
            pltpu.VMEM((24, 128), F32),
            pltpu.VMEM((D * ROWS, 128), jnp.int32),
            pltpu.VMEM((D * ROWS, 128), jnp.int32),
            pltpu.VMEM((24, 128), F32),
            pltpu.VMEM((152, 128), F32),
            pltpu.VMEM((NB * 128, 384), BF16),
            pltpu.VMEM((NB * 128, 768), F8),
            pltpu.VMEM((NB, 1024, 128), BF16),
            pltpu.VMEM((512, 128), F32),
            pltpu.VMEM((NB * 128, 128), F32),
            pltpu.VMEM((TMPL, 8, 128), F32),
            pltpu.VMEM((TMPL // 2, 384, 256), BF16),
            pltpu.VMEM((TMPL // 2, 768, 256), F8),
            pltpu.SemaphoreType.DMA((len(held) + 2,)),
            pltpu.SemaphoreType.DMA((7 + 2 * len(CHUNKS),)),
        ],
        compiler_params=pltpu.CompilerParams(
            collective_id=0, has_side_effects=True, vmem_limit_bytes=62 * 1024 * 1024
        ),
        cost_estimate=pl.CostEstimate(flops=3 * 10**10, bytes_accessed=3 * 10**7, transcendentals=0),
    )(series, coef, offset, jit, jp, w1, *held)


def shards(series, tap_coef, tap_offset, harm_index):
    out = search(series.reshape(1024, 128), tap_coef.reshape(32, 128), tap_offset, harm_index)
    return out.reshape(2, 64, 8, 128).transpose(0, 2, 1, 3).reshape(TMPL, 8192)


def solution(mesh):
    return jax.shard_map(
        shards,
        mesh=mesh,
        in_specs=(P(("dm", "bin")), P(), P(), P(None, "bin")),
        out_specs=P(None, ("dm", "bin")),
        check_vma=False,
    )
```

```python
import functools
import math

import jax
import jax.numpy as jnp
import numpy as np
from jax import lax
from jax.experimental import pallas as pl
from jax.experimental.pallas import tpu as pltpu
from jax.sharding import PartitionSpec as P

D = 64
TMPL = 16
TAPS = 128
HARM = 8
LENGTH = 8388608
LOCAL = LENGTH // D
ALPHA = 512
BETA = 256
ORDER = (4, 8, 7, 1, 6, 2, 5, 3)
BLOCKS = tuple((h, r) for h in ORDER for r in range(h))
NB = len(BLOCKS)
FIRST = {h: BLOCKS.index((h, 0)) for h in ORDER}
ROWS = 40
CHUNKS = ((0, 8, 0, 4), (8, 8, 4, 12), (16, 8, 12, 20), (24, 16, 20, 36))
FULL = 32767.0
FAR = (2, 1, 3, 0)
SAMPLE_BOUND = 6.0
PART_BOUND = SAMPLE_BOUND * D / math.sqrt(LENGTH)
F32 = jnp.float32
BF16 = jnp.bfloat16
F8 = jnp.float8_e4m3fn
LOW = 512.0


def np_split(x):
    x = np.asarray(x, np.float32)
    hi = x.astype(jnp.bfloat16)
    lo = (x - hi.astype(np.float32)).astype(jnp.bfloat16)
    return hi, lo


@functools.lru_cache(None)
def fft_tables():
    k1 = np.arange(D)[:, None]
    m = np.arange(LOCAL // D)[None, :]
    ang = -2 * np.pi * (k1 * m) / LENGTH
    tw1 = np.stack([np.cos(ang), np.sin(ang)]).astype(np.float32)
    k = np.arange(ALPHA)[:, None] * np.arange(ALPHA)[None, :] % ALPHA
    ang = -2 * np.pi * k / ALPHA
    c, s = np.cos(ang), np.sin(ang)
    wa = np.block([[c, -s], [s, c]])
    ang = -2 * np.pi * (np.arange(ALPHA)[:, None] * np.arange(BETA)[None, :]) / LOCAL
    tw2 = np.stack([np.cos(ang), np.sin(ang)]).astype(np.float32)
    half = BETA // 2
    ang = -2 * np.pi * (np.arange(BETA)[:, None] * np.arange(half)[None, :] % BETA) / BETA
    c, s = np.cos(ang), np.sin(ang)
    vb = np.block([[c, s], [-s, c]])
    k = k1 * (D * np.arange(D)[None, None, :] + np.arange(D)[:, None, None]) % (D * D)
    ang = -2 * np.pi * k / (D * D)
    w1 = np.stack([np.cos(ang), np.sin(ang)], axis=1) / math.sqrt(LENGTH)
    w1 = w1.reshape(D, 2, 4, 16, D)
    w1 = np.stack([w1[e][:, [(e // 16 + f) % 4 for f in FAR]] for e in range(D)]).reshape(D, 2 * D, D)
    wa = wa.reshape(2 * ALPHA, 2, 4, 128).transpose(2, 0, 1, 3).reshape(4, 2 * ALPHA, 256)
    return w1.astype(np.float32), tw1, *np_split(wa), tw2, *np_split(vb)


@functools.lru_cache(None)
def perm_tables():
    out = []
    for h in range(1, HARM + 1):
        m = np.zeros((128 * h, 128 * h), np.float32)
        a = np.arange(128)
        for r in range(h):
            m[h * a + r, 128 * r + 64 * (a % 2) + a // 2] = 1
        out.append(m.astype(jnp.bfloat16))
    return tuple(out)


@functools.lru_cache(None)
def select_tables():
    i = np.arange(64)
    e = np.zeros((NB, 128, 128), np.float32)
    ex = np.zeros((NB, 128, 128), np.float32)
    jp = np.zeros((NB, 1, 128), np.float32)
    for n, (h, r) in enumerate(BLOCKS):
        b, j = np.divmod(64 * r + i, h)
        for t in range(2):
            e[n, 64 * t + i, 64 * t + b] = 1
            ex[n, b, 64 * t + i] = 1
            jp[n, 0, 64 * t + i] = j
    return e.astype(jnp.bfloat16), ex.astype(jnp.bfloat16), jp.reshape(NB, 128)


def split(x):
    hi = x.astype(BF16)
    return hi, (x - hi.astype(F32)).astype(BF16)


def dot(a, b):
    return jnp.dot(a, b, preferred_element_type=F32)


def dot3(ah, al, bh, bl):
    return dot(ah, bh) + dot(ah, bl) + dot(al, bh)


def encode(x, bound):
    size = jnp.sqrt(jnp.sqrt(jnp.abs(x) * (1.0 / bound)))
    code = jnp.minimum(size * FULL + 0.5, FULL).astype(jnp.int32)
    return jnp.where(x < 0, -code, code)


def decode(code, bound):
    x = code.astype(F32)
    return x * jnp.abs(x) * (x * x * (bound / FULL**4))


def join(high, low):
    return (high << 16) | (low & 0xFFFF)


def parted(word):
    return word >> 16, (word << 16) >> 16


def for_partners(me, act):
    far = FAR
    x = [(me // 16 + k) % 4 * 16 for k in far]
    y = [(me // 4 + k) % 4 * 4 for k in far]
    z = [(me + k) % 4 for k in far]
    plane = [b + c for b in y for c in z][:-1]

    def row(i, carry):
        first = (me // 16 + 2 + i) % 4 * 16
        for v in plane:
            act(first + v)
        return carry

    lax.fori_loop(0, 4, row, 0)
    for v in x[:-1]:
        act(v + y[-1] + z[-1])


def exchange(me, dm, src, dst, first, rows, pitch, sems):
    target = dst.at[pl.ds(pl.multiple_of(me * pitch + first, 8), rows)]

    def start(to):
        pltpu.make_async_remote_copy(
            src_ref=src.at[pl.ds(pl.multiple_of(to * pitch + first, 8), rows)],
            dst_ref=target,
            send_sem=sems[0],
            recv_sem=sems[1],
            device_id=(dm, to),
            device_id_type=pl.DeviceIdType.MESH,
        ).start()

    for_partners(me, start)
    own = pl.ds(pl.multiple_of(me * pitch + first, 8), rows)
    dst[own, :] = src[own, :]


def wait_for(ref, rows, sem):
    part = ref.at[pl.ds(0, (D - 1) * rows)]
    pltpu.make_async_copy(part, part, sem).wait()


def make_taps(vx, taps, taps8):
    lane = lax.broadcasted_iota(jnp.int32, (64, 128), 1)

    def pair(tq, u):
        for x in range(3):
            both = []
            for z in range(2):
                rolled = []
                for t in range(2):
                    row = vx[4 * tq + 2 * u + t, 3 * z + x : 3 * z + x + 1, :]
                    rolled.append(
                        pltpu.roll(jnp.broadcast_to(row, (64, 128)), 64 * t, 1, stride=1, stride_axis=0)
                    )
                v = jnp.where(lane < 64, rolled[0], rolled[1])
                high = v.astype(BF16).astype(F32)
                both.append((high, (v - high) * LOW))

            def put(ref, row, kind, tr, ti):
                real, imag = slice(256 * u, 256 * u + 128), slice(256 * u + 128, 256 * u + 256)
                ref[tq, row : row + 64, real] = tr.astype(kind)
                ref[tq, row : row + 64, imag] = ti.astype(kind)
                ref[tq, row + 64 : row + 128, real] = (-ti).astype(kind)
                ref[tq, row + 64 : row + 128, imag] = tr.astype(kind)

            (rh, rl), (ih, il) = both
            put(taps, 128 * x, BF16, rh * LOW, ih * LOW)
            put(taps8, 128 * x, F8, rl, il)
            put(taps8, 384 + 128 * x, F8, rh, ih)

    def four(tq, carry):
        for u in range(2):
            pair(tq, u)
        return carry

    lax.fori_loop(0, TMPL // 4, four, 0)


def level_of(x):
    return jnp.ceil(jnp.log2(jnp.maximum(jnp.max(jnp.abs(x), keepdims=True), 1e-30)))


def make_tap_rows(coef, offset, vx, levels):
    lane = lax.broadcasted_iota(jnp.int32, (128, 384), 1)
    m = lane % 128
    lag = lane // 128 * 64 - jnp.where(m < 64, m, m - 128)
    lag = jnp.where(m == 64, -1, lag).astype(F32)
    where = jnp.concatenate([offset[...].astype(F32), jnp.zeros((112, 128), F32)], axis=0).T
    level = level_of(coef[...])
    factor = jnp.exp2(8.0 - level)
    levels[0:8, :] = jnp.broadcast_to(level, (8, 128))
    first = coef[...].astype(BF16)
    rest = coef[...] - first.astype(F32)
    second = rest.astype(BF16)
    third = (rest - second.astype(F32)).astype(BF16)
    lhs = jnp.concatenate([first, second, third], axis=0)
    for t in range(TMPL):
        onehot = jnp.where(where[:, t : t + 1] == lag, 1.0, 0.0).astype(BF16)
        rows = dot(lhs, onehot)
        rows = (rows[0:32] + rows[32:64] + rows[64:96]) * factor
        for z in range(2):
            for x in range(3):
                vx[t, 3 * z + x : 3 * z + x + 1, :] = rows[16 * z + t : 16 * z + t + 1, 128 * x : 128 * x + 128]


def code_samples(series, out):
    v = series[...].reshape(D, 16, 128)
    word = join(encode(v[:, :8], SAMPLE_BOUND), encode(v[:, 8:], SAMPLE_BOUND))
    out[...] = word.reshape(512, 128)


def columns(xs, w1, tw, out, me, send):
    pairs = [parted(xs[pl.ds(m, D, stride=8), :]) for m in range(8)]
    x = jnp.concatenate([p[0] for p in pairs] + [p[1] for p in pairs], axis=1)
    y = dot3(*split(w1[...]), *split(decode(x, SAMPLE_BOUND)))
    for j, far in enumerate(FAR):
        plane = (me // 16 + far) % 4
        rows = pl.ds(pl.multiple_of(16 * plane, 16), 16)
        yr, yi = y[16 * j : 16 * j + 16], y[D + 16 * j : D + 16 * j + 16]
        tr, ti = tw[0, rows, :], tw[1, rows, :]
        word = join(encode(yr * tr - yi * ti, PART_BOUND), encode(yr * ti + yi * tr, PART_BOUND))
        for m in range(16):
            out[pl.ds(256 * j + (m % 2) * 8 + m // 2, 16, stride=16), :] = word[:, 128 * m : 128 * m + 128]
        send(j, plane)


def local_fft(me, arrived, b, wah, wal, tw, vbh, vbl, yacc, zn, levels):
    for j, far in enumerate(FAR):
        arrived(j)
        plane = (me // 16 + 4 - far) % 4
        v = b[pl.ds(pl.multiple_of(256 * plane, 256), 256), :].reshape(16, 2, 8, 128)
        word = jnp.concatenate([v[:, n].reshape(128, 128) for n in range(2)], axis=1)
        rhs = jnp.concatenate([decode(x, PART_BOUND) for x in parted(word)], axis=0)
        y = dot3(wah[plane], wal[plane], *split(rhs))
        if j > 0:
            y = y + yacc[...]
        if j < 3:
            yacc[...] = y
    yr, yi = y[:ALPHA], y[ALPHA:]
    t = jnp.concatenate([yr * tw[0] - yi * tw[1], yr * tw[1] + yi * tw[0]], axis=1)
    th, tl = split(t)
    z = dot3(th, tl, vbh[...], vbl[...])
    level = level_of(z)
    levels[16:24, :] = jnp.broadcast_to(level, (8, 128))
    z = jnp.clip(jnp.round(z * (jnp.exp2(-level) * FULL)), -FULL, FULL)
    zero = jnp.zeros((8, 128), F32)
    for c in range(2):
        zt = z[:, 128 * c : 128 * c + 128].T
        zn[c, 0:8, :] = zero
        zn[c, 520:528, :] = zero
        for n in range(4):
            zn[c, pl.ds(8 + n, 128, stride=4), :] = zt[:, 128 * n : 128 * n + 128]


def pack_ends(zn, levels, out):
    lane = lax.broadcasted_iota(jnp.int32, (D, 128), 1)
    ends = jnp.broadcast_to(levels[16:17, :], (D, 128)).astype(jnp.int32)
    for h in range(1, HARM + 1):
        left = [zn[c, pl.ds(7, D, stride=h), :].astype(jnp.int32) for c in range(2)]
        right = [zn[c, pl.ds(8 + h, D, stride=h), :].astype(jnp.int32) for c in range(2)]
        ends = jnp.where(lane == h - 1, join(*left)[:, 127:128], ends)
        ends = jnp.where(lane == 8 + h - 1, join(*right)[:, 0:1], ends)
    out[pl.ds(0, D, stride=ROWS), :] = ends
    for n in range(1, 4):
        out[pl.ds(n, D, stride=ROWS), :] = jnp.zeros((D, 128), jnp.int32)


def pack_harmonic(h, zn, perm, out):
    src = jnp.concatenate(
        [
            jnp.concatenate([zn[c, pl.ds(8 + n, D, stride=h), :] for n in range(h)], axis=1)
            for c in range(2)
        ],
        axis=0,
    )
    hi, lo = split(src)
    moved = dot(jnp.concatenate([hi, lo], axis=0), perm[...])
    moved = (moved[:128] + moved[128:]).astype(jnp.int32)
    word = join(moved[:64], moved[64:])
    for r in range(h):
        out[pl.ds(4 + FIRST[h] + r, D, stride=ROWS), :] = word[:, 128 * r : 128 * r + 128]


def unpack_ends(land, ends, levels):
    lane = lax.broadcasted_iota(jnp.int32, (8, 128), 1)
    word = land[pl.ds(0, D, stride=ROWS), :]
    re, im = parted(word)
    zero = jnp.zeros((D, 128), F32)
    re, im, word = [jnp.concatenate([v.astype(F32), zero], axis=0).T for v in (re, im, word)]
    level = jnp.where(lane < 64, word[16:24], -1000.0)
    top = jnp.max(level[0:1], axis=1, keepdims=True)
    levels[8:16, :] = jnp.broadcast_to(top, (8, 128))
    scale = jnp.exp2(level - top + 8.0) * (1.0 / FULL)
    scale = jnp.where(lane < 64, scale, pltpu.roll(scale, 64, 1))
    scale = jnp.broadcast_to(scale[0:1], (8, 128))
    for n in range(2):
        part = slice(8 * n, 8 * n + 8)
        ends[part, :] = jnp.where(lane < 64, re[part], pltpu.roll(im[part], 64, 1)) * scale
    ends[16:24, :] = scale


def unpack(land, ends, first, last, side, xl, xl8):
    def put(n, slot, x):
        high = x.astype(BF16)
        wide = high.astype(F32)
        parts = (high, wide.astype(F8), ((x - wide) * LOW).astype(F8))
        return put_parts(n, slot, parts)

    def put_parts(n, slot, parts):
        xl[pl.ds(128 * n, 128), pl.ds(128 * slot, 128)] = parts[0]
        xl8[pl.ds(128 * n, 128), pl.ds(128 * slot, 128)] = parts[1]
        xl8[pl.ds(128 * n, 128), pl.ds(384 + 128 * slot, 128)] = parts[2]
        return parts

    for n in range(first, last):
        h, r = BLOCKS[n]
        re, im = parted(land[pl.ds(4 + n, D, stride=ROWS), :])
        block = jnp.concatenate([re.astype(F32), im.astype(F32)], axis=0).T * ends[16:17, :]
        parts = put(n, 1, block)
        if r > 0:
            put_parts(n - 1, 2, parts)
        if r < h - 1:
            put_parts(n + 1, 0, parts)
        if r == h - 1:
            side[7:8, :] = ends[h - 1 : h, :]
            side[8:72, :] = block[64:]
            put(n - h + 1, 0, jnp.concatenate([side[7:71, :], block[:64]], axis=0))
        if r == 0:
            side[80:144, :] = block[:64]
            side[144:145, :] = ends[h + 7 : h + 8, :]
            put(n + h - 1, 2, jnp.concatenate([block[64:], side[81:145, :]], axis=0))


def make_masks(jit, ex, jp, js, msk):
    for g in range(64):
        js[8 * g : 8 * g + 8, :] = jit[:, 128 * g : 128 * g + 128].astype(F32)
    for h in range(1, HARM + 1):
        even = js[pl.ds(h - 1, 64, stride=8), :]
        lhs = jnp.concatenate([even, pltpu.roll(even, 64, 1)], axis=0).astype(BF16)
        for n in range(FIRST[h], FIRST[h] + h):
            msk[pl.ds(128 * n, 128), :] = jnp.where(dot(lhs, ex[n]) == jp[n : n + 1, :], 1.0, 0.0)


def correlate(first, last, xl, xl8, taps, taps8, msk, pm):
    groups = range(first // 4, last // 4)
    fours = max(1, 4 // len(groups))

    def one(tq):
        for g in groups:
            rows = pl.ds(512 * g, 512)
            acc = dot(xl[rows, :], taps[tq]) + dot(xl8[rows, :], taps8[tq])
            for u in range(2):
                re, im = acc[:, 256 * u : 256 * u + 128], acc[:, 256 * u + 128 : 256 * u + 256]
                kept = jnp.where(msk[rows, :] > 0.5, re * re + im * im, 0.0).astype(BF16)
                to = pl.ds(pl.multiple_of(256 * tq + 128 * u, 128), 128)
                for q in range(4):
                    pm[4 * g + q, to, :] = kept[128 * q : 128 * q + 128]

    def several(step, carry):
        for k in range(fours):
            one(fours * step + k)
        return carry

    lax.fori_loop(0, TMPL // 4 // fours, several, 0)


def add_harmonics(pm, e, levels, out):
    factor = jnp.exp2(2.0 * (levels[0:1, :] + levels[8:9, :] - 25.0)) * (1.0 / HARM)
    lane = lax.broadcasted_iota(jnp.int32, (64, 128), 1)
    for tp in range(TMPL // 4):
        rows = pl.ds(256 * tp, 256)
        total = jnp.zeros((256, 128), F32)
        for n in range(0, NB, 2):
            total += dot(
                jnp.concatenate([pm[n, rows, :], pm[n + 1, rows, :]], axis=1),
                jnp.concatenate([e[n], e[n + 1]], axis=0),
            )
        total = total * factor
        for q in range(2):
            even = total[128 * q : 128 * q + 64]
            odd = total[128 * q + 64 : 128 * q + 128]
            t = 4 * tp + 2 * q
            row = t // 8 * 512 + t % 8
            out[pl.ds(row, 64, stride=8), :] = jnp.where(lane < 64, even, pltpu.roll(odd, 64, 1))
            out[pl.ds(row + 1, 64, stride=8), :] = jnp.where(lane < 64, pltpu.roll(even, 64, 1), odd)


def search_kernel(*refs):
    series, coef, offset, jit, jp, w1_all = refs[:6]
    count = len(CONSTANTS)
    held = refs[6 : 6 + count]
    out = refs[6 + count]
    rest = refs[7 + count :]
    local, rest = rest[:count], rest[count:]
    xs, w1, send1, land1, send2, land2, yacc, zn, levels, send3, land3, ends, side = rest[:13]
    xl, xl8, pm, js, msk, vx, taps, taps8, const_sem, sems = rest[13:]
    me, dm = lax.axis_index("bin"), lax.axis_index("dm")
    own = [
        pltpu.make_async_copy(series, xs, const_sem.at[count]),
        pltpu.make_async_copy(w1_all.at[me], w1, const_sem.at[count + 1]),
    ]
    copies = {
        name: pltpu.make_async_copy(held[n], local[n], const_sem.at[n])
        for n, name in enumerate(CONSTANTS)
    }
    ref = dict(zip(CONSTANTS, local))
    for copy in own:
        copy.start()

    barrier = pltpu.get_barrier_semaphore()

    def greet(to):
        pl.semaphore_signal(barrier, inc=1, device_id=(dm, to), device_id_type=pl.DeviceIdType.MESH)

    for_partners(me, greet)
    for copy in copies.values():
        copy.start()
    for copy in own:
        copy.wait()
    code_samples(xs, send1)
    pl.semaphore_wait(barrier, D - 1)

    exchange(me, dm, send1, land1, 0, 8, 8, (sems.at[0], sems.at[1]))
    copies["tw1"].wait()
    wait_for(land1, 8, sems.at[1])

    def send(j, plane):
        for y in FAR:
            for z in FAR:
                if FAR[j] or y or z:
                    within = (me // 4 + y) % 4 * 4 + (me + z) % 4
                    pltpu.make_async_remote_copy(
                        src_ref=send2.at[pl.ds(pl.multiple_of(256 * j + 16 * within, 16), 16)],
                        dst_ref=land2.at[pl.ds(pl.multiple_of(16 * me, 16), 16)],
                        send_sem=sems.at[2],
                        recv_sem=sems.at[3 + j],
                        device_id=(dm, 16 * plane + within),
                        device_id_type=pl.DeviceIdType.MESH,
                    ).start()
                else:
                    land2[pl.ds(pl.multiple_of(16 * me, 16), 16), :] = send2[
                        pl.ds(pl.multiple_of(256 * j + 16 * (me % 16), 16), 16), :
                    ]

    columns(land1, w1, ref["tw1"], send2, me, send)
    make_tap_rows(coef, offset, vx, levels)
    make_taps(vx, taps, taps8)
    copies["ex"].wait()
    make_masks(jit, ref["ex"], jp, js, msk)
    for name in ("wah", "wal", "tw2", "vbh", "vbl", "e"):
        copies[name].wait()
    for h in range(1, HARM + 1):
        copies["p%d" % h].wait()

    def arrived(j):
        part = land2.at[pl.ds(0, 16 * (16 if FAR[j] else 15))]
        pltpu.make_async_copy(part, part, sems.at[3 + j]).wait()

    local_fft(
        me, arrived, land2, ref["wah"], ref["wal"], ref["tw2"], ref["vbh"], ref["vbl"], yacc, zn, levels
    )
    pack_ends(zn, levels, send3)

    def give(n):
        row, rows, first, last = CHUNKS[n]
        for h in ORDER:
            if first <= FIRST[h] < last:
                pack_harmonic(h, zn, ref["p%d" % h], send3)
        exchange(me, dm, send3, land3, row, rows, ROWS, (sems.at[7 + 2 * n], sems.at[8 + 2 * n]))

    def take(n):
        _, rows, first, last = CHUNKS[n]
        wait_for(land3, rows, sems.at[8 + 2 * n])
        if n == 0:
            unpack_ends(land3, ends, levels)
        unpack(land3, ends, first, last, side, xl, xl8)
        correlate(first, last, xl, xl8, taps, taps8, msk, pm)

    for act, n in SCHEDULE:
        (give if act else take)(n)
    add_harmonics(pm, ref["e"], levels, out)
    wait_for(land1, 8, sems.at[0])
    wait_for(land2, 16, sems.at[2])
    for n, (_, rows, _, _) in enumerate(CHUNKS):
        wait_for(land3, rows, sems.at[7 + 2 * n])


SCHEDULE = ((1, 0), (1, 1), (1, 2), (0, 0), (1, 3), (0, 1), (0, 2), (0, 3))
CONSTANTS = ("ex", "tw1", "wah", "wal", "tw2", "vbh", "vbl") + tuple(
    "p%d" % h for h in range(1, HARM + 1)
) + ("e",)


def constants():
    w1, tw1, wah, wal, tw2, vbh, vbl = fft_tables()
    e, ex, jp = select_tables()
    return [ex, tw1, wah, wal, tw2, vbh, vbl, *perm_tables(), e], jp, w1


def search(series, coef, offset, jit):
    held, jp, w1 = constants()
    whole = pl.BlockSpec(memory_space=pltpu.VMEM)
    far = pl.BlockSpec(memory_space=pl.ANY)
    return pl.pallas_call(
        search_kernel,
        out_shape=pltpu.VMEM((TMPL * 64, 128), F32),
        in_specs=[far] + [whole] * 4 + [far] * (1 + len(held)),
        out_specs=whole,
        scratch_shapes=[pltpu.VMEM(c.shape, c.dtype) for c in held]
        + [
            pltpu.VMEM((1024, 128), F32),
            pltpu.VMEM((128, D), F32),
            pltpu.VMEM((512, 128), jnp.int32),
            pltpu.VMEM((512, 128), jnp.int32),
            pltpu.VMEM((1024, 128), jnp.int32),
            pltpu.VMEM((1024, 128), jnp.int32),
            pltpu.VMEM((2 * ALPHA, 256), F32),
            pltpu.VMEM((2, 528, 128), F32),
            pltpu.VMEM((24, 128), F32),
            pltpu.VMEM((D * ROWS, 128), jnp.int32),
            pltpu.VMEM((D * ROWS, 128), jnp.int32),
            pltpu.VMEM((24, 128), F32),
            pltpu.VMEM((152, 128), F32),
            pltpu.VMEM((NB * 128, 384), BF16),
            pltpu.VMEM((NB * 128, 768), F8),
            pltpu.VMEM((NB, 1024, 128), BF16),
            pltpu.VMEM((512, 128), F32),
            pltpu.VMEM((NB * 128, 128), F32),
            pltpu.VMEM((TMPL, 8, 128), F32),
            pltpu.VMEM((TMPL // 4, 384, 512), BF16),
            pltpu.VMEM((TMPL // 4, 768, 512), F8),
            pltpu.SemaphoreType.DMA((len(held) + 2,)),
            pltpu.SemaphoreType.DMA((7 + 2 * len(CHUNKS),)),
        ],
        compiler_params=pltpu.CompilerParams(
            collective_id=0, has_side_effects=True, vmem_limit_bytes=62 * 1024 * 1024
        ),
        cost_estimate=pl.CostEstimate(flops=3 * 10**10, bytes_accessed=3 * 10**7, transcendentals=0),
    )(series, coef, offset, jit, jp, w1, *held)


def shards(series, tap_coef, tap_offset, harm_index):
    out = search(series.reshape(1024, 128), tap_coef.reshape(32, 128), tap_offset, harm_index)
    return out.reshape(2, 64, 8, 128).transpose(0, 2, 1, 3).reshape(TMPL, 8192)


def solution(mesh):
    return jax.shard_map(
        shards,
        mesh=mesh,
        in_specs=(P(("dm", "bin")), P(), P(), P(None, "bin")),
        out_specs=P(None, ("dm", "bin")),
        check_vma=False,
    )
```

```python
import functools
import math

import jax
import jax.numpy as jnp
import numpy as np
from jax import lax
from jax.experimental import pallas as pl
from jax.experimental.pallas import tpu as pltpu
from jax.sharding import PartitionSpec as P

D = 64
TMPL = 16
TAPS = 128
HARM = 8
LENGTH = 8388608
LOCAL = LENGTH // D
ALPHA = 512
BETA = 256
ORDER = (4, 8, 7, 1, 6, 2, 5, 3)
BLOCKS = tuple((h, r) for h in ORDER for r in range(h))
NB = len(BLOCKS)
FIRST = {h: BLOCKS.index((h, 0)) for h in ORDER}
ROWS = 40
CHUNKS = ((0, 8, 0, 4), (8, 8, 4, 12), (16, 8, 12, 20), (24, 16, 20, 36))
FULL = 32767.0
FAR = (2, 1, 3, 0)
SAMPLE_BOUND = 6.0
PART_BOUND = SAMPLE_BOUND * D / math.sqrt(LENGTH)
F32 = jnp.float32
BF16 = jnp.bfloat16
F8 = jnp.float8_e4m3fn
LOW = 512.0


def np_split(x):
    x = np.asarray(x, np.float32)
    hi = x.astype(jnp.bfloat16)
    lo = (x - hi.astype(np.float32)).astype(jnp.bfloat16)
    return hi, lo


@functools.lru_cache(None)
def fft_tables():
    k1 = np.arange(D)[:, None]
    m = np.arange(LOCAL // D)[None, :]
    ang = -2 * np.pi * (k1 * m) / LENGTH
    tw1 = np.stack([np.cos(ang), np.sin(ang)]).astype(np.float32)
    k = np.arange(ALPHA)[:, None] * np.arange(ALPHA)[None, :] % ALPHA
    ang = -2 * np.pi * k / ALPHA
    c, s = np.cos(ang), np.sin(ang)
    wa = np.block([[c, -s], [s, c]])
    ang = -2 * np.pi * (np.arange(ALPHA)[:, None] * np.arange(BETA)[None, :]) / LOCAL
    tw2 = np.stack([np.cos(ang), np.sin(ang)]).astype(np.float32)
    half = BETA // 2
    ang = -2 * np.pi * (np.arange(BETA)[:, None] * np.arange(half)[None, :] % BETA) / BETA
    c, s = np.cos(ang), np.sin(ang)
    vb = np.block([[c, s], [-s, c]])
    k = k1 * (D * np.arange(D)[None, None, :] + np.arange(D)[:, None, None]) % (D * D)
    ang = -2 * np.pi * k / (D * D)
    w1 = np.stack([np.cos(ang), np.sin(ang)], axis=1) / math.sqrt(LENGTH)
    w1 = w1.reshape(D, 2, 4, 16, D)
    w1 = np.stack([w1[e][:, [(e // 16 + f) % 4 for f in FAR]] for e in range(D)]).reshape(D, 2 * D, D)
    wa = wa.reshape(2 * ALPHA, 2, 4, 128).transpose(2, 0, 1, 3).reshape(4, 2 * ALPHA, 256)
    return w1.astype(np.float32), tw1, *np_split(wa), tw2, *np_split(vb)


@functools.lru_cache(None)
def perm_tables():
    out = []
    for h in range(1, HARM + 1):
        m = np.zeros((128 * h, 128 * h), np.float32)
        a = np.arange(128)
        for r in range(h):
            m[h * a + r, 128 * r + 64 * (a % 2) + a // 2] = 1
        out.append(m.astype(jnp.bfloat16))
    return tuple(out)


@functools.lru_cache(None)
def select_tables():
    i = np.arange(64)
    e = np.zeros((NB, 128, 128), np.float32)
    ex = np.zeros((NB, 128, 128), np.float32)
    jp = np.zeros((NB, 1, 128), np.float32)
    for n, (h, r) in enumerate(BLOCKS):
        b, j = np.divmod(64 * r + i, h)
        for t in range(2):
            e[n, 64 * t + i, 64 * t + b] = 1
            ex[n, b, 64 * t + i] = 1
            jp[n, 0, 64 * t + i] = j
    return e.astype(jnp.bfloat16), ex.astype(jnp.bfloat16), jp.reshape(NB, 128)


def split(x):
    hi = x.astype(BF16)
    return hi, (x - hi.astype(F32)).astype(BF16)


def dot(a, b):
    return jnp.dot(a, b, preferred_element_type=F32)


def dot3(ah, al, bh, bl):
    return dot(ah, bh) + dot(ah, bl) + dot(al, bh)


def encode(x, bound):
    size = jnp.abs(x) * (1.0 / bound)
    for _ in range(2):
        size = size * lax.rsqrt(jnp.maximum(size, 1e-37))
    code = jnp.minimum(size * FULL + 0.5, FULL).astype(jnp.int32)
    return jnp.where(x < 0, -code, code)


def decode(code, bound):
    x = code.astype(F32)
    return x * jnp.abs(x) * (x * x * (bound / FULL**4))


def join(high, low):
    return (high << 16) | (low & 0xFFFF)


def parted(word):
    return word >> 16, (word << 16) >> 16


def for_partners(me, act):
    far = FAR
    x = [(me // 16 + k) % 4 * 16 for k in far]
    y = [(me // 4 + k) % 4 * 4 for k in far]
    z = [(me + k) % 4 for k in far]
    plane = [b + c for b in y for c in z][:-1]

    def row(i, carry):
        first = (me // 16 + 2 + i) % 4 * 16
        for v in plane:
            act(first + v)
        return carry

    lax.fori_loop(0, 4, row, 0)
    for v in x[:-1]:
        act(v + y[-1] + z[-1])


def exchange(me, dm, src, dst, first, rows, pitch, sems):
    target = dst.at[pl.ds(pl.multiple_of(me * pitch + first, 8), rows)]

    def start(to):
        pltpu.make_async_remote_copy(
            src_ref=src.at[pl.ds(pl.multiple_of(to * pitch + first, 8), rows)],
            dst_ref=target,
            send_sem=sems[0],
            recv_sem=sems[1],
            device_id=(dm, to),
            device_id_type=pl.DeviceIdType.MESH,
        ).start()

    for_partners(me, start)
    own = pl.ds(pl.multiple_of(me * pitch + first, 8), rows)
    dst[own, :] = src[own, :]


def wait_for(ref, rows, sem):
    part = ref.at[pl.ds(0, (D - 1) * rows)]
    pltpu.make_async_copy(part, part, sem).wait()


def make_taps(vx, taps, taps8):
    lane = lax.broadcasted_iota(jnp.int32, (64, 128), 1)

    def pair(tp, carry):
        for x in range(3):
            both = []
            for z in range(2):
                rolled = []
                for t in range(2):
                    row = vx[2 * tp + t, 3 * z + x : 3 * z + x + 1, :]
                    rolled.append(
                        pltpu.roll(jnp.broadcast_to(row, (64, 128)), 64 * t, 1, stride=1, stride_axis=0)
                    )
                v = jnp.where(lane < 64, rolled[0], rolled[1])
                high = v.astype(BF16).astype(F32)
                both.append((high, (v - high) * LOW))

            def put(ref, row, kind, tr, ti):
                ref[tp, row : row + 64, 0:128] = tr.astype(kind)
                ref[tp, row : row + 64, 128:256] = ti.astype(kind)
                ref[tp, row + 64 : row + 128, 0:128] = (-ti).astype(kind)
                ref[tp, row + 64 : row + 128, 128:256] = tr.astype(kind)

            (rh, rl), (ih, il) = both
            put(taps, 128 * x, BF16, rh * LOW, ih * LOW)
            put(taps8, 128 * x, F8, rl, il)
            put(taps8, 384 + 128 * x, F8, rh, ih)
        return carry

    lax.fori_loop(0, TMPL // 2, pair, 0)


def level_of(x):
    return jnp.ceil(jnp.log2(jnp.maximum(jnp.max(jnp.abs(x), keepdims=True), 1e-30)))


def make_tap_rows(coef, offset, vx, levels):
    lane = lax.broadcasted_iota(jnp.int32, (128, 384), 1)
    m = lane % 128
    lag = lane // 128 * 64 - jnp.where(m < 64, m, m - 128)
    lag = jnp.where(m == 64, -1, lag).astype(F32)
    where = jnp.concatenate([offset[...].astype(F32), jnp.zeros((112, 128), F32)], axis=0).T
    level = level_of(coef[...])
    factor = jnp.exp2(8.0 - level)
    levels[0:8, :] = jnp.broadcast_to(level, (8, 128))
    first = coef[...].astype(BF16)
    rest = coef[...] - first.astype(F32)
    second = rest.astype(BF16)
    third = (rest - second.astype(F32)).astype(BF16)
    lhs = jnp.concatenate([first, second, third], axis=0)
    for t in range(TMPL):
        onehot = jnp.where(where[:, t : t + 1] == lag, 1.0, 0.0).astype(BF16)
        rows = dot(lhs, onehot)
        rows = (rows[0:32] + rows[32:64] + rows[64:96]) * factor
        for z in range(2):
            for x in range(3):
                vx[t, 3 * z + x : 3 * z + x + 1, :] = rows[16 * z + t : 16 * z + t + 1, 128 * x : 128 * x + 128]


def code_samples(series, out):
    v = series[...].reshape(D, 16, 128)
    word = join(encode(v[:, :8], SAMPLE_BOUND), encode(v[:, 8:], SAMPLE_BOUND))
    out[...] = word.reshape(512, 128)


def columns(xs, w1, tw, out, me, send):
    pairs = [parted(xs[pl.ds(m, D, stride=8), :]) for m in range(8)]
    x = jnp.concatenate([p[0] for p in pairs] + [p[1] for p in pairs], axis=1)
    y = dot3(*split(w1[...]), *split(decode(x, SAMPLE_BOUND)))
    for j, far in enumerate(FAR):
        plane = (me // 16 + far) % 4
        rows = pl.ds(pl.multiple_of(16 * plane, 16), 16)
        yr, yi = y[16 * j : 16 * j + 16], y[D + 16 * j : D + 16 * j + 16]
        tr, ti = tw[0, rows, :], tw[1, rows, :]
        word = join(encode(yr * tr - yi * ti, PART_BOUND), encode(yr * ti + yi * tr, PART_BOUND))
        for m in range(16):
            out[pl.ds(256 * j + (m % 2) * 8 + m // 2, 16, stride=16), :] = word[:, 128 * m : 128 * m + 128]
        send(j, plane)


def local_fft(me, arrived, b, wah, wal, tw, vbh, vbl, yacc, zn, levels):
    for j, far in enumerate(FAR):
        arrived(j)
        plane = (me // 16 + 4 - far) % 4
        v = b[pl.ds(pl.multiple_of(256 * plane, 256), 256), :].reshape(16, 2, 8, 128)
        word = jnp.concatenate([v[:, n].reshape(128, 128) for n in range(2)], axis=1)
        rhs = jnp.concatenate([decode(x, PART_BOUND) for x in parted(word)], axis=0)
        y = dot3(wah[plane], wal[plane], *split(rhs))
        if j > 0:
            y = y + yacc[...]
        if j < 3:
            yacc[...] = y
    yr, yi = y[:ALPHA], y[ALPHA:]
    t = jnp.concatenate([yr * tw[0] - yi * tw[1], yr * tw[1] + yi * tw[0]], axis=1)
    th, tl = split(t)
    z = dot3(th, tl, vbh[...], vbl[...])
    level = level_of(z)
    levels[16:24, :] = jnp.broadcast_to(level, (8, 128))
    z = jnp.clip(jnp.round(z * (jnp.exp2(-level) * FULL)), -FULL, FULL)
    zero = jnp.zeros((8, 128), F32)
    for c in range(2):
        zt = z[:, 128 * c : 128 * c + 128].T
        zn[c, 0:8, :] = zero
        zn[c, 520:528, :] = zero
        for n in range(4):
            zn[c, pl.ds(8 + n, 128, stride=4), :] = zt[:, 128 * n : 128 * n + 128]


def pack_ends(zn, levels, out):
    lane = lax.broadcasted_iota(jnp.int32, (D, 128), 1)
    ends = jnp.broadcast_to(levels[16:17, :], (D, 128)).astype(jnp.int32)
    for h in range(1, HARM + 1):
        left = [zn[c, pl.ds(7, D, stride=h), :].astype(jnp.int32) for c in range(2)]
        right = [zn[c, pl.ds(8 + h, D, stride=h), :].astype(jnp.int32) for c in range(2)]
        ends = jnp.where(lane == h - 1, join(*left)[:, 127:128], ends)
        ends = jnp.where(lane == 8 + h - 1, join(*right)[:, 0:1], ends)
    out[pl.ds(0, D, stride=ROWS), :] = ends
    for n in range(1, 4):
        out[pl.ds(n, D, stride=ROWS), :] = jnp.zeros((D, 128), jnp.int32)


def pack_harmonic(h, zn, perm, out):
    src = jnp.concatenate(
        [
            jnp.concatenate([zn[c, pl.ds(8 + n, D, stride=h), :] for n in range(h)], axis=1)
            for c in range(2)
        ],
        axis=0,
    )
    hi, lo = split(src)
    moved = dot(jnp.concatenate([hi, lo], axis=0), perm[...])
    moved = (moved[:128] + moved[128:]).astype(jnp.int32)
    word = join(moved[:64], moved[64:])
    for r in range(h):
        out[pl.ds(4 + FIRST[h] + r, D, stride=ROWS), :] = word[:, 128 * r : 128 * r + 128]


def unpack_ends(land, ends, levels):
    lane = lax.broadcasted_iota(jnp.int32, (8, 128), 1)
    word = land[pl.ds(0, D, stride=ROWS), :]
    re, im = parted(word)
    zero = jnp.zeros((D, 128), F32)
    re, im, word = [jnp.concatenate([v.astype(F32), zero], axis=0).T for v in (re, im, word)]
    level = jnp.where(lane < 64, word[16:24], -1000.0)
    top = jnp.max(level[0:1], axis=1, keepdims=True)
    levels[8:16, :] = jnp.broadcast_to(top, (8, 128))
    scale = jnp.exp2(level - top + 8.0) * (1.0 / FULL)
    scale = jnp.where(lane < 64, scale, pltpu.roll(scale, 64, 1))
    scale = jnp.broadcast_to(scale[0:1], (8, 128))
    for n in range(2):
        part = slice(8 * n, 8 * n + 8)
        ends[part, :] = jnp.where(lane < 64, re[part], pltpu.roll(im[part], 64, 1)) * scale
    ends[16:24, :] = scale


def unpack(land, ends, first, last, side, xl, xl8):
    def put(n, slot, x):
        high = x.astype(BF16)
        wide = high.astype(F32)
        parts = (high, wide.astype(F8), ((x - wide) * LOW).astype(F8))
        return put_parts(n, slot, parts)

    def put_parts(n, slot, parts):
        xl[pl.ds(128 * n, 128), pl.ds(128 * slot, 128)] = parts[0]
        xl8[pl.ds(128 * n, 128), pl.ds(128 * slot, 128)] = parts[1]
        xl8[pl.ds(128 * n, 128), pl.ds(384 + 128 * slot, 128)] = parts[2]
        return parts

    for n in range(first, last):
        h, r = BLOCKS[n]
        re, im = parted(land[pl.ds(4 + n, D, stride=ROWS), :])
        block = jnp.concatenate([re.astype(F32), im.astype(F32)], axis=0).T * ends[16:17, :]
        parts = put(n, 1, block)
        if r > 0:
            put_parts(n - 1, 2, parts)
        if r < h - 1:
            put_parts(n + 1, 0, parts)
        if r == h - 1:
            side[7:8, :] = ends[h - 1 : h, :]
            side[8:72, :] = block[64:]
            put(n - h + 1, 0, jnp.concatenate([side[7:71, :], block[:64]], axis=0))
        if r == 0:
            side[80:144, :] = block[:64]
            side[144:145, :] = ends[h + 7 : h + 8, :]
            put(n + h - 1, 2, jnp.concatenate([block[64:], side[81:145, :]], axis=0))


def make_masks(jit, ex, jp, js, msk):
    for g in range(64):
        js[8 * g : 8 * g + 8, :] = jit[:, 128 * g : 128 * g + 128].astype(F32)
    for h in range(1, HARM + 1):
        even = js[pl.ds(h - 1, 64, stride=8), :]
        lhs = jnp.concatenate([even, pltpu.roll(even, 64, 1)], axis=0).astype(BF16)
        for n in range(FIRST[h], FIRST[h] + h):
            msk[pl.ds(128 * n, 128), :] = jnp.where(dot(lhs, ex[n]) == jp[n : n + 1, :], 1.0, 0.0)


def correlate(first, last, xl, xl8, taps, taps8, msk, pm):
    groups = range(first // 4, last // 4)
    pairs = max(1, 8 // len(groups))

    def one(tp):
        for g in groups:
            rows = pl.ds(512 * g, 512)
            acc = dot(xl[rows, :], taps[tp]) + dot(xl8[rows, :], taps8[tp])
            re, im = acc[:, :128], acc[:, 128:]
            kept = jnp.where(msk[rows, :] > 0.5, re * re + im * im, 0.0).astype(BF16)
            for q in range(4):
                pm[4 * g + q, pl.ds(pl.multiple_of(128 * tp, 128), 128), :] = kept[128 * q : 128 * q + 128]

    def several(step, carry):
        for k in range(pairs):
            one(pairs * step + k)
        return carry

    lax.fori_loop(0, TMPL // 2 // pairs, several, 0)


def add_harmonics(pm, e, levels, out):
    factor = jnp.exp2(2.0 * (levels[0:1, :] + levels[8:9, :] - 25.0)) * (1.0 / HARM)
    lane = lax.broadcasted_iota(jnp.int32, (64, 128), 1)
    for tp in range(TMPL // 4):
        rows = pl.ds(256 * tp, 256)
        total = jnp.zeros((256, 128), F32)
        for n in range(0, NB, 2):
            total += dot(
                jnp.concatenate([pm[n, rows, :], pm[n + 1, rows, :]], axis=1),
                jnp.concatenate([e[n], e[n + 1]], axis=0),
            )
        total = total * factor
        for q in range(2):
            even = total[128 * q : 128 * q + 64]
            odd = total[128 * q + 64 : 128 * q + 128]
            t = 4 * tp + 2 * q
            row = t // 8 * 512 + t % 8
            out[pl.ds(row, 64, stride=8), :] = jnp.where(lane < 64, even, pltpu.roll(odd, 64, 1))
            out[pl.ds(row + 1, 64, stride=8), :] = jnp.where(lane < 64, pltpu.roll(even, 64, 1), odd)


def search_kernel(*refs):
    series, w1_all = refs[:2]
    count = len(CONSTANTS)
    held = refs[2 : 2 + count]
    out = refs[2 + count]
    rest = refs[3 + count :]
    local, rest = rest[:count], rest[count:]
    xs, w1, send1, land1, send2, land2, yacc, zn, levels, send3, land3, ends, side = rest[:13]
    xl, xl8, pm, js, msk, vx, taps, taps8, const_sem, sems = rest[13:]
    me, dm = lax.axis_index("bin"), lax.axis_index("dm")
    own = [
        pltpu.make_async_copy(series, xs, const_sem.at[count]),
        pltpu.make_async_copy(w1_all.at[me], w1, const_sem.at[count + 1]),
    ]
    copies = {
        name: pltpu.make_async_copy(held[n], local[n], const_sem.at[n])
        for n, name in enumerate(CONSTANTS)
    }
    ref = dict(zip(CONSTANTS, local))
    for copy in own:
        copy.start()

    barrier = pltpu.get_barrier_semaphore()

    def greet(to):
        pl.semaphore_signal(barrier, inc=1, device_id=(dm, to), device_id_type=pl.DeviceIdType.MESH)

    for_partners(me, greet)
    for copy in own:
        copy.wait()
    code_samples(xs, send1)
    pl.semaphore_wait(barrier, D - 1)

    exchange(me, dm, send1, land1, 0, 8, 8, (sems.at[0], sems.at[1]))
    for copy in copies.values():
        copy.start()
    copies["tw1"].wait()
    wait_for(land1, 8, sems.at[1])

    def send(j, plane):
        for y in FAR:
            for z in FAR:
                if FAR[j] or y or z:
                    within = (me // 4 + y) % 4 * 4 + (me + z) % 4
                    pltpu.make_async_remote_copy(
                        src_ref=send2.at[pl.ds(pl.multiple_of(256 * j + 16 * within, 16), 16)],
                        dst_ref=land2.at[pl.ds(pl.multiple_of(16 * me, 16), 16)],
                        send_sem=sems.at[2],
                        recv_sem=sems.at[3 + j],
                        device_id=(dm, 16 * plane + within),
                        device_id_type=pl.DeviceIdType.MESH,
                    ).start()
                else:
                    land2[pl.ds(pl.multiple_of(16 * me, 16), 16), :] = send2[
                        pl.ds(pl.multiple_of(256 * j + 16 * (me % 16), 16), 16), :
                    ]

    columns(land1, w1, ref["tw1"], send2, me, send)
    for name in ("coef", "offset", "jit", "jp", "ex"):
        copies[name].wait()
    make_tap_rows(ref["coef"], ref["offset"], vx, levels)
    make_taps(vx, taps, taps8)
    make_masks(ref["jit"], ref["ex"], ref["jp"], js, msk)
    for name in ("wah", "wal", "tw2", "vbh", "vbl", "e"):
        copies[name].wait()
    for h in range(1, HARM + 1):
        copies["p%d" % h].wait()

    def arrived(j):
        part = land2.at[pl.ds(0, 16 * (16 if FAR[j] else 15))]
        pltpu.make_async_copy(part, part, sems.at[3 + j]).wait()

    local_fft(
        me, arrived, land2, ref["wah"], ref["wal"], ref["tw2"], ref["vbh"], ref["vbl"], yacc, zn, levels
    )
    pack_ends(zn, levels, send3)

    def give(n):
        row, rows, first, last = CHUNKS[n]
        for h in ORDER:
            if first <= FIRST[h] < last:
                pack_harmonic(h, zn, ref["p%d" % h], send3)
        exchange(me, dm, send3, land3, row, rows, ROWS, (sems.at[7 + 2 * n], sems.at[8 + 2 * n]))

    def take(n):
        _, rows, first, last = CHUNKS[n]
        wait_for(land3, rows, sems.at[8 + 2 * n])
        if n == 0:
            unpack_ends(land3, ends, levels)
        unpack(land3, ends, first, last, side, xl, xl8)
        correlate(first, last, xl, xl8, taps, taps8, msk, pm)

    for act, n in SCHEDULE:
        (give if act else take)(n)
    add_harmonics(pm, ref["e"], levels, out)
    wait_for(land1, 8, sems.at[0])
    wait_for(land2, 16, sems.at[2])
    for n, (_, rows, _, _) in enumerate(CHUNKS):
        wait_for(land3, rows, sems.at[7 + 2 * n])


SCHEDULE = ((1, 0), (1, 1), (1, 2), (0, 0), (1, 3), (0, 1), (0, 2), (0, 3))
CONSTANTS = ("tw1", "coef", "offset", "jit", "jp", "ex", "wah", "wal", "tw2", "vbh", "vbl") + tuple(
    "p%d" % h for h in range(1, HARM + 1)
) + ("e",)


def constants():
    w1, tw1, wah, wal, tw2, vbh, vbl = fft_tables()
    e, ex, jp = select_tables()
    return [tw1], [jp, ex, wah, wal, tw2, vbh, vbl, *perm_tables(), e], w1


def search(series, coef, offset, jit):
    first, later, w1 = constants()
    held = first + [coef, offset, jit] + later
    whole = pl.BlockSpec(memory_space=pltpu.VMEM)
    far = pl.BlockSpec(memory_space=pl.ANY)
    return pl.pallas_call(
        search_kernel,
        out_shape=pltpu.VMEM((TMPL * 64, 128), F32),
        in_specs=[far] * (2 + len(held)),
        out_specs=whole,
        scratch_shapes=[pltpu.VMEM(c.shape, c.dtype) for c in held]
        + [
            pltpu.VMEM((1024, 128), F32),
            pltpu.VMEM((128, D), F32),
            pltpu.VMEM((512, 128), jnp.int32),
            pltpu.VMEM((512, 128), jnp.int32),
            pltpu.VMEM((1024, 128), jnp.int32),
            pltpu.VMEM((1024, 128), jnp.int32),
            pltpu.VMEM((2 * ALPHA, 256), F32),
            pltpu.VMEM((2, 528, 128), F32),
            pltpu.VMEM((24, 128), F32),
            pltpu.VMEM((D * ROWS, 128), jnp.int32),
            pltpu.VMEM((D * ROWS, 128), jnp.int32),
            pltpu.VMEM((24, 128), F32),
            pltpu.VMEM((152, 128), F32),
            pltpu.VMEM((NB * 128, 384), BF16),
            pltpu.VMEM((NB * 128, 768), F8),
            pltpu.VMEM((NB, 1024, 128), BF16),
            pltpu.VMEM((512, 128), F32),
            pltpu.VMEM((NB * 128, 128), F32),
            pltpu.VMEM((TMPL, 8, 128), F32),
            pltpu.VMEM((TMPL // 2, 384, 256), BF16),
            pltpu.VMEM((TMPL // 2, 768, 256), F8),
            pltpu.SemaphoreType.DMA((len(held) + 2,)),
            pltpu.SemaphoreType.DMA((7 + 2 * len(CHUNKS),)),
        ],
        compiler_params=pltpu.CompilerParams(
            collective_id=0, has_side_effects=True, vmem_limit_bytes=62 * 1024 * 1024
        ),
        cost_estimate=pl.CostEstimate(flops=3 * 10**10, bytes_accessed=3 * 10**7, transcendentals=0),
    )(series, w1, *held)


def shards(series, tap_coef, tap_offset, harm_index):
    out = search(series.reshape(1024, 128), tap_coef.reshape(32, 128), tap_offset, harm_index)
    return out.reshape(2, 64, 8, 128).transpose(0, 2, 1, 3).reshape(TMPL, 8192)


def solution(mesh):
    return jax.shard_map(
        shards,
        mesh=mesh,
        in_specs=(P(("dm", "bin")), P(), P(), P(None, "bin")),
        out_specs=P(None, ("dm", "bin")),
        check_vma=False,
    )
```

```python
import functools
import math

import jax
import jax.numpy as jnp
import numpy as np
from jax import lax
from jax.experimental import pallas as pl
from jax.experimental.pallas import tpu as pltpu
from jax.sharding import PartitionSpec as P

D = 64
TMPL = 16
TAPS = 128
HARM = 8
LENGTH = 8388608
LOCAL = LENGTH // D
ALPHA = 512
BETA = 256
ORDER = (4, 8, 7, 1, 6, 2, 5, 3)
BLOCKS = tuple((h, r) for h in ORDER for r in range(h))
NB = len(BLOCKS)
FIRST = {h: BLOCKS.index((h, 0)) for h in ORDER}
ROWS = 40
CHUNKS = ((0, 8, 0, 4), (8, 8, 4, 12), (16, 8, 12, 20), (24, 16, 20, 36))
FULL = 32767.0
FAR = (2, 1, 3, 0)
SAMPLE_BOUND = 6.0
PART_BOUND = SAMPLE_BOUND * D / math.sqrt(LENGTH)
F32 = jnp.float32
BF16 = jnp.bfloat16
F8 = jnp.float8_e4m3fn
LOW = 512.0


def np_split(x):
    x = np.asarray(x, np.float32)
    hi = x.astype(jnp.bfloat16)
    lo = (x - hi.astype(np.float32)).astype(jnp.bfloat16)
    return hi, lo


@functools.lru_cache(None)
def fft_tables():
    k1 = np.arange(D)[:, None]
    m = np.arange(LOCAL // D)[None, :]
    ang = -2 * np.pi * (k1 * m) / LENGTH
    tw1 = np.stack([np.cos(ang), np.sin(ang)]).astype(np.float32)
    k = np.arange(ALPHA)[:, None] * np.arange(ALPHA)[None, :] % ALPHA
    ang = -2 * np.pi * k / ALPHA
    c, s = np.cos(ang), np.sin(ang)
    wa = np.block([[c, -s], [s, c]])
    ang = -2 * np.pi * (np.arange(ALPHA)[:, None] * np.arange(BETA)[None, :]) / LOCAL
    tw2 = np.stack([np.cos(ang), np.sin(ang)]).astype(np.float32)
    half = BETA // 2
    ang = -2 * np.pi * (np.arange(BETA)[:, None] * np.arange(half)[None, :] % BETA) / BETA
    c, s = np.cos(ang), np.sin(ang)
    vb = np.block([[c, s], [-s, c]])
    k = k1 * (D * np.arange(D)[None, None, :] + np.arange(D)[:, None, None]) % (D * D)
    ang = -2 * np.pi * k / (D * D)
    w1 = np.stack([np.cos(ang), np.sin(ang)], axis=1) / math.sqrt(LENGTH)
    w1 = w1.reshape(D, 2, 4, 16, D)
    w1 = np.stack([w1[e][:, [(e // 16 + f) % 4 for f in FAR]] for e in range(D)]).reshape(D, 2 * D, D)
    wa = wa.reshape(2 * ALPHA, 2, 4, 128).transpose(2, 0, 1, 3).reshape(4, 2 * ALPHA, 256)
    return w1.astype(np.float32), tw1, *np_split(wa), tw2, *np_split(vb.T)


@functools.lru_cache(None)
def perm_tables():
    out = []
    for h in range(1, HARM + 1):
        m = np.zeros((128 * h, 128 * h), np.float32)
        a = np.arange(128)
        for r in range(h):
            m[h * a + r, 128 * r + 64 * (a % 2) + a // 2] = 1
        out.append(m.astype(jnp.bfloat16))
    return tuple(out)


@functools.lru_cache(None)
def select_tables():
    i = np.arange(64)
    e = np.zeros((NB, 128, 128), np.float32)
    ex = np.zeros((NB, 128, 128), np.float32)
    jp = np.zeros((NB, 1, 128), np.float32)
    for n, (h, r) in enumerate(BLOCKS):
        b, j = np.divmod(64 * r + i, h)
        for t in range(2):
            e[n, 64 * t + i, 64 * t + b] = 1
            ex[n, b, 64 * t + i] = 1
            jp[n, 0, 64 * t + i] = j
    return e.astype(jnp.bfloat16), ex.astype(jnp.bfloat16), jp.reshape(NB, 128)


def split(x):
    hi = x.astype(BF16)
    return hi, (x - hi.astype(F32)).astype(BF16)


def dot(a, b):
    return jnp.dot(a, b, preferred_element_type=F32)


def dot_rows(a, b):
    return lax.dot_general(a, b, (((1,), (1,)), ((), ())), preferred_element_type=F32)


def dot3(ah, al, bh, bl):
    return dot(ah, bh) + dot(ah, bl) + dot(al, bh)


def encode(x, bound):
    size = jnp.abs(x) * (1.0 / bound)
    for _ in range(2):
        size = size * lax.rsqrt(jnp.maximum(size, 1e-37))
    code = jnp.minimum(size * FULL + 0.5, FULL).astype(jnp.int32)
    return jnp.where(x < 0, -code, code)


def decode(code, bound):
    x = code.astype(F32)
    return x * jnp.abs(x) * (x * x * (bound / FULL**4))


def join(high, low):
    return (high << 16) | (low & 0xFFFF)


def parted(word):
    return word >> 16, (word << 16) >> 16


def for_partners(me, act):
    far = FAR
    x = [(me // 16 + k) % 4 * 16 for k in far]
    y = [(me // 4 + k) % 4 * 4 for k in far]
    z = [(me + k) % 4 for k in far]
    plane = [b + c for b in y for c in z][:-1]

    def row(i, carry):
        first = (me // 16 + 2 + i) % 4 * 16
        for v in plane:
            act(first + v)
        return carry

    lax.fori_loop(0, 4, row, 0)
    for v in x[:-1]:
        act(v + y[-1] + z[-1])


def exchange(me, dm, src, dst, first, rows, pitch, sems):
    target = dst.at[pl.ds(pl.multiple_of(me * pitch + first, 8), rows)]

    def start(to):
        pltpu.make_async_remote_copy(
            src_ref=src.at[pl.ds(pl.multiple_of(to * pitch + first, 8), rows)],
            dst_ref=target,
            send_sem=sems[0],
            recv_sem=sems[1],
            device_id=(dm, to),
            device_id_type=pl.DeviceIdType.MESH,
        ).start()

    for_partners(me, start)
    own = pl.ds(pl.multiple_of(me * pitch + first, 8), rows)
    dst[own, :] = src[own, :]


def wait_for(ref, rows, sem):
    part = ref.at[pl.ds(0, (D - 1) * rows)]
    pltpu.make_async_copy(part, part, sem).wait()


def make_taps(vx, taps, taps8):
    lane = lax.broadcasted_iota(jnp.int32, (64, 128), 1)

    def pair(tp, carry):
        for x in range(3):
            both = []
            for z in range(2):
                rolled = []
                for t in range(2):
                    row = vx[2 * tp + t, 3 * z + x : 3 * z + x + 1, :]
                    rolled.append(
                        pltpu.roll(jnp.broadcast_to(row, (64, 128)), 64 * t, 1, stride=1, stride_axis=0)
                    )
                v = jnp.where(lane < 64, rolled[0], rolled[1])
                high = v.astype(BF16).astype(F32)
                both.append((high, (v - high) * LOW))

            def put(ref, row, kind, tr, ti):
                ref[tp, row : row + 64, 0:128] = tr.astype(kind)
                ref[tp, row : row + 64, 128:256] = ti.astype(kind)
                ref[tp, row + 64 : row + 128, 0:128] = (-ti).astype(kind)
                ref[tp, row + 64 : row + 128, 128:256] = tr.astype(kind)

            (rh, rl), (ih, il) = both
            put(taps, 128 * x, BF16, rh * LOW, ih * LOW)
            put(taps8, 128 * x, F8, rl, il)
            put(taps8, 384 + 128 * x, F8, rh, ih)
        return carry

    lax.fori_loop(0, TMPL // 2, pair, 0)


def level_of(x):
    return jnp.ceil(jnp.log2(jnp.maximum(jnp.max(jnp.abs(x), keepdims=True), 1e-30)))


def make_tap_rows(coef, offset, vx, levels):
    lane = lax.broadcasted_iota(jnp.int32, (128, 384), 1)
    m = lane % 128
    lag = lane // 128 * 64 - jnp.where(m < 64, m, m - 128)
    lag = jnp.where(m == 64, -1, lag).astype(F32)
    where = jnp.concatenate([offset[...].astype(F32), jnp.zeros((112, 128), F32)], axis=0).T
    level = level_of(coef[...])
    factor = jnp.exp2(8.0 - level)
    levels[0:8, :] = jnp.broadcast_to(level, (8, 128))
    first = coef[...].astype(BF16)
    rest = coef[...] - first.astype(F32)
    second = rest.astype(BF16)
    third = (rest - second.astype(F32)).astype(BF16)
    lhs = jnp.concatenate([first, second, third], axis=0)
    for t in range(TMPL):
        onehot = jnp.where(where[:, t : t + 1] == lag, 1.0, 0.0).astype(BF16)
        rows = dot(lhs, onehot)
        rows = (rows[0:32] + rows[32:64] + rows[64:96]) * factor
        for z in range(2):
            for x in range(3):
                vx[t, 3 * z + x : 3 * z + x + 1, :] = rows[16 * z + t : 16 * z + t + 1, 128 * x : 128 * x + 128]


def code_samples(series, out):
    v = series[...].reshape(D, 16, 128)
    word = join(encode(v[:, :8], SAMPLE_BOUND), encode(v[:, 8:], SAMPLE_BOUND))
    out[...] = word.reshape(512, 128)


def columns(xs, w1, tw, out, me, send):
    pairs = [parted(xs[pl.ds(m, D, stride=8), :]) for m in range(8)]
    x = jnp.concatenate([p[0] for p in pairs] + [p[1] for p in pairs], axis=1)
    y = dot3(*split(w1[...]), *split(decode(x, SAMPLE_BOUND)))
    for j, far in enumerate(FAR):
        plane = (me // 16 + far) % 4
        rows = pl.ds(pl.multiple_of(16 * plane, 16), 16)
        yr, yi = y[16 * j : 16 * j + 16], y[D + 16 * j : D + 16 * j + 16]
        tr, ti = tw[0, rows, :], tw[1, rows, :]
        word = join(encode(yr * tr - yi * ti, PART_BOUND), encode(yr * ti + yi * tr, PART_BOUND))
        for m in range(16):
            out[pl.ds(256 * j + (m % 2) * 8 + m // 2, 16, stride=16), :] = word[:, 128 * m : 128 * m + 128]
        send(j, plane)


def local_fft(me, arrived, b, wah, wal, tw, vbh, vbl, yacc, zn, levels):
    for j, far in enumerate(FAR):
        arrived(j)
        plane = (me // 16 + 4 - far) % 4
        v = b[pl.ds(pl.multiple_of(256 * plane, 256), 256), :].reshape(16, 2, 8, 128)
        word = jnp.concatenate([v[:, n].reshape(128, 128) for n in range(2)], axis=1)
        rhs = jnp.concatenate([decode(x, PART_BOUND) for x in parted(word)], axis=0)
        y = dot3(wah[plane], wal[plane], *split(rhs))
        if j > 0:
            y = y + yacc[...]
        if j < 3:
            yacc[...] = y
    yr, yi = y[:ALPHA], y[ALPHA:]
    t = jnp.concatenate([yr * tw[0] - yi * tw[1], yr * tw[1] + yi * tw[0]], axis=1)
    th, tl = split(t)
    z = dot_rows(vbh[...], th) + dot_rows(vbl[...], th) + dot_rows(vbh[...], tl)
    level = level_of(z)
    levels[16:24, :] = jnp.broadcast_to(level, (8, 128))
    z = jnp.clip(jnp.round(z * (jnp.exp2(-level) * FULL)), -FULL, FULL)
    zero = jnp.zeros((8, 128), F32)
    for c in range(2):
        zt = z[128 * c : 128 * c + 128]
        zn[c, 0:8, :] = zero
        zn[c, 520:528, :] = zero
        for n in range(4):
            zn[c, pl.ds(8 + n, 128, stride=4), :] = zt[:, 128 * n : 128 * n + 128]


def pack_ends(zn, levels, out):
    lane = lax.broadcasted_iota(jnp.int32, (D, 128), 1)
    ends = jnp.broadcast_to(levels[16:17, :], (D, 128)).astype(jnp.int32)
    for h in range(1, HARM + 1):
        left = [zn[c, pl.ds(7, D, stride=h), :].astype(jnp.int32) for c in range(2)]
        right = [zn[c, pl.ds(8 + h, D, stride=h), :].astype(jnp.int32) for c in range(2)]
        ends = jnp.where(lane == h - 1, join(*left)[:, 127:128], ends)
        ends = jnp.where(lane == 8 + h - 1, join(*right)[:, 0:1], ends)
    out[pl.ds(0, D, stride=ROWS), :] = ends
    for n in range(1, 4):
        out[pl.ds(n, D, stride=ROWS), :] = jnp.zeros((D, 128), jnp.int32)


def pack_harmonic(h, zn, perm, out):
    src = jnp.concatenate(
        [
            jnp.concatenate([zn[c, pl.ds(8 + n, D, stride=h), :] for n in range(h)], axis=1)
            for c in range(2)
        ],
        axis=0,
    )
    hi, lo = split(src)
    moved = dot(jnp.concatenate([hi, lo], axis=0), perm[...])
    moved = (moved[:128] + moved[128:]).astype(jnp.int32)
    word = join(moved[:64], moved[64:])
    for r in range(h):
        out[pl.ds(4 + FIRST[h] + r, D, stride=ROWS), :] = word[:, 128 * r : 128 * r + 128]


def unpack_ends(land, ends, levels):
    lane = lax.broadcasted_iota(jnp.int32, (8, 128), 1)
    word = land[pl.ds(0, D, stride=ROWS), :]
    re, im = parted(word)
    zero = jnp.zeros((D, 128), F32)
    re, im, word = [jnp.concatenate([v.astype(F32), zero], axis=0).T for v in (re, im, word)]
    level = jnp.where(lane < 64, word[16:24], -1000.0)
    top = jnp.max(level[0:1], axis=1, keepdims=True)
    levels[8:16, :] = jnp.broadcast_to(top, (8, 128))
    scale = jnp.exp2(level - top + 8.0) * (1.0 / FULL)
    scale = jnp.where(lane < 64, scale, pltpu.roll(scale, 64, 1))
    scale = jnp.broadcast_to(scale[0:1], (8, 128))
    for n in range(2):
        part = slice(8 * n, 8 * n + 8)
        ends[part, :] = jnp.where(lane < 64, re[part], pltpu.roll(im[part], 64, 1)) * scale
    ends[16:24, :] = scale


def unpack(land, ends, first, last, side, xl, xl8):
    def put(n, slot, x):
        high = x.astype(BF16)
        wide = high.astype(F32)
        parts = (high, wide.astype(F8), ((x - wide) * LOW).astype(F8))
        return put_parts(n, slot, parts)

    def put_parts(n, slot, parts):
        xl[pl.ds(128 * n, 128), pl.ds(128 * slot, 128)] = parts[0]
        xl8[pl.ds(128 * n, 128), pl.ds(128 * slot, 128)] = parts[1]
        xl8[pl.ds(128 * n, 128), pl.ds(384 + 128 * slot, 128)] = parts[2]
        return parts

    for n in range(first, last):
        h, r = BLOCKS[n]
        re, im = parted(land[pl.ds(4 + n, D, stride=ROWS), :])
        block = jnp.concatenate([re.astype(F32), im.astype(F32)], axis=0).T * ends[16:17, :]
        parts = put(n, 1, block)
        if r > 0:
            put_parts(n - 1, 2, parts)
        if r < h - 1:
            put_parts(n + 1, 0, parts)
        if r == h - 1:
            side[7:8, :] = ends[h - 1 : h, :]
            side[8:72, :] = block[64:]
            put(n - h + 1, 0, jnp.concatenate([side[7:71, :], block[:64]], axis=0))
        if r == 0:
            side[80:144, :] = block[:64]
            side[144:145, :] = ends[h + 7 : h + 8, :]
            put(n + h - 1, 2, jnp.concatenate([block[64:], side[81:145, :]], axis=0))


def make_masks(jit, ex, jp, js, msk):
    for g in range(64):
        js[8 * g : 8 * g + 8, :] = jit[:, 128 * g : 128 * g + 128].astype(F32)
    for h in range(1, HARM + 1):
        even = js[pl.ds(h - 1, 64, stride=8), :]
        lhs = jnp.concatenate([even, pltpu.roll(even, 64, 1)], axis=0).astype(BF16)
        for n in range(FIRST[h], FIRST[h] + h):
            msk[pl.ds(128 * n, 128), :] = jnp.where(dot(lhs, ex[n]) == jp[n : n + 1, :], 1.0, 0.0)


def correlate(first, last, xl, xl8, taps, taps8, msk, pm):
    groups = range(first // 4, last // 4)
    pairs = max(1, 8 // len(groups))

    def one(tp):
        for g in groups:
            rows = pl.ds(512 * g, 512)
            acc = dot(xl[rows, :], taps[tp]) + dot(xl8[rows, :], taps8[tp])
            re, im = acc[:, :128], acc[:, 128:]
            kept = jnp.where(msk[rows, :] > 0.5, re * re + im * im, 0.0).astype(BF16)
            for q in range(4):
                pm[4 * g + q, pl.ds(pl.multiple_of(128 * tp, 128), 128), :] = kept[128 * q : 128 * q + 128]

    def several(step, carry):
        for k in range(pairs):
            one(pairs * step + k)
        return carry

    lax.fori_loop(0, TMPL // 2 // pairs, several, 0)


def add_harmonics(pm, e, levels, out):
    factor = jnp.exp2(2.0 * (levels[0:1, :] + levels[8:9, :] - 25.0)) * (1.0 / HARM)
    lane = lax.broadcasted_iota(jnp.int32, (64, 128), 1)
    for tp in range(TMPL // 4):
        rows = pl.ds(256 * tp, 256)
        total = jnp.zeros((256, 128), F32)
        for n in range(0, NB, 2):
            total += dot(
                jnp.concatenate([pm[n, rows, :], pm[n + 1, rows, :]], axis=1),
                jnp.concatenate([e[n], e[n + 1]], axis=0),
            )
        total = total * factor
        for q in range(2):
            even = total[128 * q : 128 * q + 64]
            odd = total[128 * q + 64 : 128 * q + 128]
            t = 4 * tp + 2 * q
            row = t // 8 * 512 + t % 8
            out[pl.ds(row, 64, stride=8), :] = jnp.where(lane < 64, even, pltpu.roll(odd, 64, 1))
            out[pl.ds(row + 1, 64, stride=8), :] = jnp.where(lane < 64, pltpu.roll(even, 64, 1), odd)


def search_kernel(*refs):
    series, w1_all = refs[:2]
    count = len(CONSTANTS)
    held = refs[2 : 2 + count]
    out = refs[2 + count]
    rest = refs[3 + count :]
    local, rest = rest[:count], rest[count:]
    xs, w1, send1, land1, send2, land2, yacc, zn, levels, send3, land3, ends, side = rest[:13]
    xl, xl8, pm, js, msk, vx, taps, taps8, const_sem, sems = rest[13:]
    me, dm = lax.axis_index("bin"), lax.axis_index("dm")
    own = [
        pltpu.make_async_copy(series, xs, const_sem.at[count]),
        pltpu.make_async_copy(w1_all.at[me], w1, const_sem.at[count + 1]),
    ]
    copies = {
        name: pltpu.make_async_copy(held[n], local[n], const_sem.at[n])
        for n, name in enumerate(CONSTANTS)
    }
    ref = dict(zip(CONSTANTS, local))
    for copy in own:
        copy.start()

    barrier = pltpu.get_barrier_semaphore()

    def greet(to):
        pl.semaphore_signal(barrier, inc=1, device_id=(dm, to), device_id_type=pl.DeviceIdType.MESH)

    for_partners(me, greet)
    for copy in own:
        copy.wait()
    code_samples(xs, send1)
    pl.semaphore_wait(barrier, D - 1)

    exchange(me, dm, send1, land1, 0, 8, 8, (sems.at[0], sems.at[1]))
    for copy in copies.values():
        copy.start()
    copies["tw1"].wait()
    wait_for(land1, 8, sems.at[1])

    def send(j, plane):
        for y in FAR:
            for z in FAR:
                if FAR[j] or y or z:
                    within = (me // 4 + y) % 4 * 4 + (me + z) % 4
                    pltpu.make_async_remote_copy(
                        src_ref=send2.at[pl.ds(pl.multiple_of(256 * j + 16 * within, 16), 16)],
                        dst_ref=land2.at[pl.ds(pl.multiple_of(16 * me, 16), 16)],
                        send_sem=sems.at[2],
                        recv_sem=sems.at[3 + j],
                        device_id=(dm, 16 * plane + within),
                        device_id_type=pl.DeviceIdType.MESH,
                    ).start()
                else:
                    land2[pl.ds(pl.multiple_of(16 * me, 16), 16), :] = send2[
                        pl.ds(pl.multiple_of(256 * j + 16 * (me % 16), 16), 16), :
                    ]

    columns(land1, w1, ref["tw1"], send2, me, send)
    for name in ("coef", "offset", "jit", "jp", "ex"):
        copies[name].wait()
    make_tap_rows(ref["coef"], ref["offset"], vx, levels)
    make_taps(vx, taps, taps8)
    make_masks(ref["jit"], ref["ex"], ref["jp"], js, msk)
    for name in ("wah", "wal", "tw2", "vbh", "vbl", "e"):
        copies[name].wait()
    for h in range(1, HARM + 1):
        copies["p%d" % h].wait()

    def arrived(j):
        part = land2.at[pl.ds(0, 16 * (16 if FAR[j] else 15))]
        pltpu.make_async_copy(part, part, sems.at[3 + j]).wait()

    local_fft(
        me, arrived, land2, ref["wah"], ref["wal"], ref["tw2"], ref["vbh"], ref["vbl"], yacc, zn, levels
    )
    pack_ends(zn, levels, send3)

    def give(n):
        row, rows, first, last = CHUNKS[n]
        for h in ORDER:
            if first <= FIRST[h] < last:
                pack_harmonic(h, zn, ref["p%d" % h], send3)
        exchange(me, dm, send3, land3, row, rows, ROWS, (sems.at[7 + 2 * n], sems.at[8 + 2 * n]))

    def take(n):
        _, rows, first, last = CHUNKS[n]
        wait_for(land3, rows, sems.at[8 + 2 * n])
        if n == 0:
            unpack_ends(land3, ends, levels)
        unpack(land3, ends, first, last, side, xl, xl8)
        correlate(first, last, xl, xl8, taps, taps8, msk, pm)

    for act, n in SCHEDULE:
        (give if act else take)(n)
    add_harmonics(pm, ref["e"], levels, out)
    wait_for(land1, 8, sems.at[0])
    wait_for(land2, 16, sems.at[2])
    for n, (_, rows, _, _) in enumerate(CHUNKS):
        wait_for(land3, rows, sems.at[7 + 2 * n])


SCHEDULE = ((1, 0), (1, 1), (1, 2), (0, 0), (1, 3), (0, 1), (0, 2), (0, 3))
CONSTANTS = ("tw1", "coef", "offset", "jit", "jp", "ex", "wah", "wal", "tw2", "vbh", "vbl") + tuple(
    "p%d" % h for h in range(1, HARM + 1)
) + ("e",)


def constants():
    w1, tw1, wah, wal, tw2, vbh, vbl = fft_tables()
    e, ex, jp = select_tables()
    return [tw1], [jp, ex, wah, wal, tw2, vbh, vbl, *perm_tables(), e], w1


def search(series, coef, offset, jit):
    first, later, w1 = constants()
    held = first + [coef, offset, jit] + later
    whole = pl.BlockSpec(memory_space=pltpu.VMEM)
    far = pl.BlockSpec(memory_space=pl.ANY)
    return pl.pallas_call(
        search_kernel,
        out_shape=pltpu.VMEM((TMPL * 64, 128), F32),
        in_specs=[far] * (2 + len(held)),
        out_specs=whole,
        scratch_shapes=[pltpu.VMEM(c.shape, c.dtype) for c in held]
        + [
            pltpu.VMEM((1024, 128), F32),
            pltpu.VMEM((128, D), F32),
            pltpu.VMEM((512, 128), jnp.int32),
            pltpu.VMEM((512, 128), jnp.int32),
            pltpu.VMEM((1024, 128), jnp.int32),
            pltpu.VMEM((1024, 128), jnp.int32),
            pltpu.VMEM((2 * ALPHA, 256), F32),
            pltpu.VMEM((2, 528, 128), F32),
            pltpu.VMEM((24, 128), F32),
            pltpu.VMEM((D * ROWS, 128), jnp.int32),
            pltpu.VMEM((D * ROWS, 128), jnp.int32),
            pltpu.VMEM((24, 128), F32),
            pltpu.VMEM((152, 128), F32),
            pltpu.VMEM((NB * 128, 384), BF16),
            pltpu.VMEM((NB * 128, 768), F8),
            pltpu.VMEM((NB, 1024, 128), BF16),
            pltpu.VMEM((512, 128), F32),
            pltpu.VMEM((NB * 128, 128), F32),
            pltpu.VMEM((TMPL, 8, 128), F32),
            pltpu.VMEM((TMPL // 2, 384, 256), BF16),
            pltpu.VMEM((TMPL // 2, 768, 256), F8),
            pltpu.SemaphoreType.DMA((len(held) + 2,)),
            pltpu.SemaphoreType.DMA((7 + 2 * len(CHUNKS),)),
        ],
        compiler_params=pltpu.CompilerParams(
            collective_id=0, has_side_effects=True, vmem_limit_bytes=62 * 1024 * 1024
        ),
        cost_estimate=pl.CostEstimate(flops=3 * 10**10, bytes_accessed=3 * 10**7, transcendentals=0),
    )(series, w1, *held)


def shards(series, tap_coef, tap_offset, harm_index):
    out = search(series.reshape(1024, 128), tap_coef.reshape(32, 128), tap_offset, harm_index)
    return out.reshape(2, 64, 8, 128).transpose(0, 2, 1, 3).reshape(TMPL, 8192)


def solution(mesh):
    return jax.shard_map(
        shards,
        mesh=mesh,
        in_specs=(P(("dm", "bin")), P(), P(), P(None, "bin")),
        out_specs=P(None, ("dm", "bin")),
        check_vma=False,
    )
```
